32 devices in a mesh: dp: 16 (over z, y, x), seq: 2 (over core).
Axes of the slice: x: 2, y: 2, z: 4, core: 2. Of those that a mesh axis runs over, the one named last changes fastest.
Arguments:
- tokens: bfloat16 [64, 512, 768], P('dp', 'seq'), may hold values from -6 to 6
- cotangent: bfloat16 [64, 512, 768], P('dp', 'seq'), may hold values from -6 to 6
- seq_lengths: int32 [16, 4], P('dp'), may hold values from 1 to 512, 1536 in all within a row
- slot_order: int32 [16, 4], P('dp'), may hold values from 0 to 3, each once within a row
- attn_weights: float32 [768, 3072], P(None, ('dp', 'seq'))
- attn_moment: float32 [768, 3072], P(None, ('dp', 'seq'))
- attn_second: float32 [768, 3072], P(None, ('dp', 'seq')), as said below
- ffn_weights: float32 [768, 6144], P(None, ('dp', 'seq'))
- ffn_moment: float32 [768, 6144], P(None, ('dp', 'seq'))
- ffn_second: float32 [768, 6144], P(None, ('dp', 'seq')), as said below
- vectors: float32 [9216], P(('dp', 'seq'))
- vector_moment: float32 [9216], P(('dp', 'seq'))
- vector_second: float32 [9216], P(('dp', 'seq')), as said below
Outputs:
- layer_out: bfloat16 [64, 512, 768], P('dp', 'seq')
- input_grad: float32 [64, 512, 768], P('dp', 'seq')
- attn_moment_out: float32 [768, 3072], P(None, ('dp', 'seq'))
- attn_second_out: float32 [768, 3072], P(None, ('dp', 'seq'))
- attn_weights_out: float32 [768, 3072], P(None, ('dp', 'seq'))
- attn_copy_out: bfloat16 [768, 3072], P(None, ('dp', 'seq'))
- ffn_moment_out: float32 [768, 6144], P(None, ('dp', 'seq'))
- ffn_second_out: float32 [768, 6144], P(None, ('dp', 'seq'))
- ffn_weights_out: float32 [768, 6144], P(None, ('dp', 'seq'))
- ffn_copy_out: bfloat16 [768, 6144], P(None, ('dp', 'seq'))
- vector_moment_out: float32 [9216], P(('dp', 'seq'))
- vector_second_out: float32 [9216], P(('dp', 'seq'))
- vectors_out: float32 [9216], P(('dp', 'seq'))
- vector_copy_out: bfloat16 [9216], P(('dp', 'seq'))
The draws below stay inside these ranges and needn't reach their ends.
Inputs may be any that keep to these rules, and one draw needn't show every extreme that they name: `seq_lengths`: in each group the 4 lengths sum to 1536 and the largest is exactly 512. `slot_order`: each group's row is a permutation of 0 to 3. `attn_second`: Positive. `ffn_second`: Positive. `vector_second`: Positive.
All inputs are finite; a program needn't handle non-finite values.
Results may differ from the reference program's by a relative error of at most 0.012.
The reference program's roundings to bfloat16 on the way count: a program that leaves them out, or rounds other values in their place, can miss the bound.
Values may be sent and summed in bfloat16 or wider, within the bound.
No kernel may reach another device: no remote copies, remote signals or barrier semaphores. Data moves between devices by JAX's collectives and lax.ppermute only.
A program may use at most 192 MiB of HBM per device.

```python
import math
import jax
import jax.numpy as jnp
import numpy as np
from jax import lax

D = 768
H = 12
FF = 3072
LEN = 512
SEQS = 4
STEP = 5
DH = 64
GROUPS = 16
SEQUENCES = 64


def grad_scale():
    return math.sqrt(SEQUENCES * LEN)


def attn_kind():
    columns = jnp.arange(4 * D)
    return jnp.where(columns < 3 * D, 1.0, 0.9) * grad_scale()


def ffn_kind():
    columns = jnp.arange(2 * FF)
    return jnp.where(columns < FF, 0.3, 0.45) * grad_scale()


def vector_kind():
    entry_index = jnp.arange(8 * D + FF)
    level = 1.2 + 0.3 * (entry_index >= D) - 0.5 * (entry_index >= 2 * D) - 0.2 * (entry_index >= 3 * D)
    level = level + 0.5 * (entry_index >= 4 * D + FF) - 0.3 * (entry_index >= 6 * D + FF)
    return level * grad_scale()


def second_factor(key, shape):
    return jnp.exp(jax.random.uniform(key, shape, jnp.float32, math.log(0.5), math.log(8.0)))


def draw_attn_weights(key, part):
    key = jax.random.fold_in(key, 11)
    columns = jnp.arange(4 * D)
    column_scale = jnp.where(columns < 2 * D, math.sqrt(2.0), jnp.where(columns < 3 * D, 1.5, 1.8)) * D ** (-0.5)
    noise_draw = jax.random.normal(key, (D, 4 * D), jnp.float32)
    return (noise_draw * column_scale[None, :]).astype(jnp.float32)


def draw_attn_moment(key, part):
    key = jax.random.fold_in(key, 12)
    return (jax.random.normal(key, (D, 4 * D), jnp.float32) * attn_kind()[None, :]).astype(jnp.float32)


def draw_attn_second(key, part):
    key = jax.random.fold_in(key, 13)
    kind_sq = attn_kind() * attn_kind()
    return (second_factor(key, (D, 4 * D)) * kind_sq[None, :]).astype(jnp.float32)


def draw_ffn_weights(key, part):
    key = jax.random.fold_in(key, 21)
    columns = jnp.arange(2 * FF)
    column_scale = jnp.where(columns < FF, D ** (-0.5), 1.5 * FF ** (-0.5))
    noise_draw = jax.random.normal(key, (D, 2 * FF), jnp.float32)
    return (noise_draw * column_scale[None, :]).astype(jnp.float32)


def draw_ffn_moment(key, part):
    key = jax.random.fold_in(key, 22)
    return (jax.random.normal(key, (D, 2 * FF), jnp.float32) * ffn_kind()[None, :]).astype(jnp.float32)


def draw_ffn_second(key, part):
    key = jax.random.fold_in(key, 23)
    kind_sq = ffn_kind() * ffn_kind()
    return (second_factor(key, (D, 2 * FF)) * kind_sq[None, :]).astype(jnp.float32)


def draw_vectors(key, part):
    key = jax.random.fold_in(key, 31)
    entry_index = jnp.arange(8 * D + FF)
    first_gain = (entry_index >= 4 * D + FF) & (entry_index < 5 * D + FF)
    second_gain = (entry_index >= 6 * D + FF) & (entry_index < 7 * D + FF)
    is_gain = first_gain | second_gain
    noise_draw = jax.random.normal(key, (8 * D + FF,), jnp.float32)
    return jnp.where(is_gain, 1.0 + 0.1 * noise_draw, 0.2 * noise_draw).astype(jnp.float32)


def draw_vector_moment(key, part):
    key = jax.random.fold_in(key, 32)
    return (jax.random.normal(key, (8 * D + FF,), jnp.float32) * vector_kind()).astype(jnp.float32)


def draw_vector_second(key, part):
    key = jax.random.fold_in(key, 33)
    return (second_factor(key, (8 * D + FF,)) * vector_kind() * vector_kind()).astype(jnp.float32)


def levels(key, dims, shards, least, top_value):
    gain = 1.0
    for dim, parts in shards:
        heights = jax.random.uniform(jax.random.fold_in(jax.random.fold_in(key, 6), dim), (parts,), jnp.float32, least / len(shards), top_value / len(shards))
        gain = gain * jnp.repeat(jnp.exp(heights), dims[dim] // parts).reshape((-1,) + (1,) * (len(dims) - 1 - dim))
    return gain


def length_profile(amount, total, bound, lean):
    portions = [(1 << 20) // math.isqrt(grade ** lean) + 1 for grade in range(2, amount + 1)]
    surplus, holding = total - bound - (amount - 1), [1] * (amount - 1)
    while surplus > 0:
        candidates = [i for i in range(amount - 1) if holding[i] < bound]
        mass, remaining = sum([portions[i] for i in candidates]), surplus
        for i in candidates:
            more = min(bound - holding[i], max(1, remaining * portions[i] // mass), surplus)
            holding[i] = holding[i] + more
            surplus = surplus - more
    return np.array([bound] + holding)


def ragged(own_key, count, total, reach, lean):
    if count == 2:
        one = jax.random.randint(own_key, (), max(1, total - reach), min(reach, total - 1) + 1)
        return jnp.stack([one, total - one])
    lengths = jnp.asarray(length_profile(count, total, reach, lean), jnp.int32)
    pairs = (count - 1) // 2
    donor, taker = lengths[1:1 + 2 * pairs:2], lengths[2:2 + 2 * pairs:2]
    room = jnp.minimum(donor - 1, reach - taker)
    moved = jax.random.randint(jax.random.fold_in(own_key, 1), (pairs,), 0, 1 << 20) % (room + 1)
    lengths = lengths.at[1:1 + 2 * pairs:2].set(donor - moved).at[2:2 + 2 * pairs:2].set(taker + moved)
    return lengths[jax.random.permutation(jax.random.fold_in(own_key, 2), count)]


def centred(rng, extent, deviation, bound, split=(), kind=jnp.bfloat16):
    level = levels(rng, extent, split, -0.22, 0.18) if split else 1.0
    values = jax.random.normal(rng, extent, jnp.float32) * deviation * level
    return jnp.minimum(jnp.maximum(values, -bound), bound).astype(kind)


def setup_inputs(seed: int = 0) -> dict:
    keys = jax.random.split(jax.random.key(seed), 14)
    return {
        "tokens": centred(keys[0], (SEQUENCES, LEN, D), 1.0, 6.0, ((0, 16), (1, 2))),
        "cotangent": centred(keys[1], (SEQUENCES, LEN, D), 1.0, 6.0, ((0, 16), (1, 2))),
        "seq_lengths": jax.vmap(lambda own: ragged(own, SEQS, 3 * SEQS * LEN // 4, LEN, 1))(jax.random.split(keys[2], GROUPS)).reshape((GROUPS, SEQS)).astype(jnp.int32),
        "slot_order": jax.vmap(lambda own: jax.random.permutation(own, SEQS))(jax.random.split(keys[3], GROUPS)).reshape((GROUPS, SEQS)).astype(jnp.int32),
        "attn_weights": draw_attn_weights(jax.random.fold_in(keys[13], 71), 0),
        "attn_moment": draw_attn_moment(jax.random.fold_in(keys[13], 71), 0),
        "attn_second": draw_attn_second(jax.random.fold_in(keys[13], 71), 0),
        "ffn_weights": draw_ffn_weights(jax.random.fold_in(keys[13], 71), 0),
        "ffn_moment": draw_ffn_moment(jax.random.fold_in(keys[13], 71), 0),
        "ffn_second": draw_ffn_second(jax.random.fold_in(keys[13], 71), 0),
        "vectors": draw_vectors(jax.random.fold_in(keys[13], 71), 0),
        "vector_moment": draw_vector_moment(jax.random.fold_in(keys[13], 71), 0),
        "vector_second": draw_vector_second(jax.random.fold_in(keys[13], 71), 0),
    }


@jax.custom_vjp
def lower_precision(v):
    return lax.optimization_barrier(v.astype(jnp.bfloat16)).astype(jnp.float32)

@jax.custom_vjp
def lower_precision_backward(v):
    return v

def low_keep(v):
    return (lower_precision(v), None)

def low_pass(kept, grad):
    return (grad,)

def back_keep(v):
    return (v, None)

def back_low(kept, grad):
    return (lower_precision(grad),)
lower_precision.defvjp(low_keep, low_pass)
lower_precision_backward.defvjp(back_keep, back_low)
epsilon = 1e-06
masked_score = -1e+30
decay_rate = 0.5
adam_epsilon = 1e-08
weight_decay = 0.01
vector_rate = 0.5
highest_precision = lax.Precision.HIGHEST

def layer_norm(values, gain_vec, shift_vec):
    center = values - lax.optimization_barrier(jnp.mean(values, axis=-1, keepdims=True))
    scaled = center * lax.rsqrt(lax.optimization_barrier(jnp.mean(center * center, axis=-1, keepdims=True)) + epsilon)
    return scaled * gain_vec + shift_vec

def sequence_block(attn_w, ffn_w, vec_w, input_tokens, block_len):
    seq_count, length = (input_tokens.shape[0], input_tokens.shape[1])
    query_key_value_weight = attn_w[:, :3 * D]
    output_weight = attn_w[:, 3 * D:]
    up_weight = ffn_w[:, :FF]
    down_weight = ffn_w[:, FF:]
    bias_query = vec_w[0:D]
    bias_value = vec_w[D:2 * D]
    output_bias = vec_w[2 * D:3 * D]
    up_bias = vec_w[3 * D:3 * D + FF]
    down_bias = vec_w[3 * D + FF:4 * D + FF]
    gain_one = vec_w[4 * D + FF:5 * D + FF]
    shift_one = vec_w[5 * D + FF:6 * D + FF]
    gain_two = vec_w[6 * D + FF:7 * D + FF]
    shift_two = vec_w[7 * D + FF:8 * D + FF]
    column_scale = jnp.concatenate([jnp.full((D,), DH ** (-0.5), jnp.float32), jnp.ones((2 * D,), jnp.float32)])
    query_key_value_bias = jnp.concatenate([bias_query, jnp.zeros((D,), jnp.float32), bias_value])
    query_key_value = (jnp.einsum('aji,if->ajf', input_tokens, query_key_value_weight, precision=highest_precision) + query_key_value_bias) * column_scale
    query_key_value = lower_precision_backward(lower_precision(query_key_value))
    query_all = query_key_value[..., :D].reshape(seq_count, length, H, DH)
    key_all = query_key_value[..., D:2 * D].reshape(seq_count, length, H, DH)
    value_all = query_key_value[..., 2 * D:].reshape(seq_count, length, H, DH)
    scores = lower_precision_backward(jnp.einsum('sqhd,skhd->shqk', query_all, key_all, precision=highest_precision))
    live_mask = (jnp.arange(length)[None, :] < block_len[:, None])[:, None, None, :]
    scores = jnp.where(live_mask, scores, masked_score)
    row_max = lax.optimization_barrier(jnp.max(scores, axis=-1, keepdims=True))
    exp_terms = jnp.exp(scores - row_max)
    probs = lower_precision(exp_terms / lax.optimization_barrier(jnp.sum(exp_terms, axis=-1, keepdims=True)))
    context_rows = jnp.einsum('shqk,skhd->sqhd', probs, value_all, precision=highest_precision).reshape(seq_count, length, D)
    context_rows = lower_precision_backward(lower_precision(context_rows))
    attended_rows = lower_precision_backward(jnp.einsum('aji,if->ajf', context_rows, output_weight, precision=highest_precision) + output_bias)
    hidden_state = layer_norm(input_tokens + attended_rows, gain_one, shift_one)
    pre_activation = lower_precision_backward(jnp.einsum('kne,eh->knh', lower_precision(hidden_state), up_weight, precision=highest_precision) + up_bias)
    active_units = lower_precision(jax.nn.gelu(pre_activation, approximate=False))
    branch_output = lower_precision_backward(jnp.einsum('hyq,bq->hyb', active_units, down_weight, precision=highest_precision) + down_bias)
    return layer_norm(hidden_state + branch_output, gain_two, shift_two)

def forward(tokens_f, attn_w, ffn_w, vec_w, slot_len):
    blocks = tokens_f.reshape(GROUPS, SEQS, LEN, D)
    block_lens = slot_len.reshape(GROUPS, SEQS)

    def one_block(pair):
        return sequence_block(attn_w, ffn_w, vec_w, pair[0], pair[1])
    outputs = lax.map(jax.checkpoint(one_block), (blocks, block_lens))
    return outputs.reshape(SEQUENCES, LEN, D)

def adam_update(master, moment, second, grad, rate):
    moment_new = decay_rate * moment + (1.0 - decay_rate) * grad
    second_new = decay_rate * second + (1.0 - decay_rate) * grad * grad
    correction = 1.0 - decay_rate ** STEP
    direction = moment_new / correction / (jnp.sqrt(second_new / correction) + adam_epsilon)
    master_new = master - rate * (direction + weight_decay * master)
    return (moment_new, second_new, master_new)

def reference(tokens, cotangent, seq_lengths, slot_order, attn_weights, attn_moment, attn_second, ffn_weights, ffn_moment, ffn_second, vectors, vector_moment, vector_second):
    slot_len = jnp.take_along_axis(seq_lengths, slot_order, axis=1).reshape(-1).astype(jnp.int32)
    attn_used = attn_weights.astype(jnp.bfloat16).astype(jnp.float32)
    ffn_used = ffn_weights.astype(jnp.bfloat16).astype(jnp.float32)
    vec_used = vectors.astype(jnp.bfloat16).astype(jnp.float32)

    def closed(tokens_f, attn_w, ffn_w, vec_w):
        return forward(tokens_f, attn_w, ffn_w, vec_w, slot_len)
    result, pull_back = jax.vjp(closed, tokens.astype(jnp.float32), attn_used, ffn_used, vec_used)
    input_grad, attn_grad, ffn_grad, vector_grad = pull_back(cotangent.astype(jnp.float32))
    attn_cols = jnp.arange(4 * D)
    attn_rate = jnp.where(attn_cols < 2 * D, math.sqrt(2.0), jnp.where(attn_cols < 3 * D, 1.5, 1.8)) * D ** (-0.5)
    ffn_cols = jnp.arange(2 * FF)
    ffn_rate = jnp.where(ffn_cols < FF, D ** (-0.5), 1.5 * FF ** (-0.5))
    attn_m, attn_v, attn_new = adam_update(attn_weights, attn_moment, attn_second, attn_grad, attn_rate[None, :])
    ffn_m, ffn_v, ffn_new = adam_update(ffn_weights, ffn_moment, ffn_second, ffn_grad, ffn_rate[None, :])
    vec_m, vec_v, vec_new = adam_update(vectors, vector_moment, vector_second, vector_grad, vector_rate)
    return (result.astype(jnp.bfloat16), input_grad, attn_m, attn_v, attn_new, attn_new.astype(jnp.bfloat16), ffn_m, ffn_v, ffn_new, ffn_new.astype(jnp.bfloat16), vec_m, vec_v, vec_new, vec_new.astype(jnp.bfloat16))
```

```python
import math

import jax
import jax.numpy as jnp
from jax import lax
from jax.experimental import pallas as pl
from jax.experimental.pallas import tpu as pltpu
from jax.sharding import PartitionSpec as P

H = 12
FF = 3072
STEP = 5

epsilon = 1e-06
masked_score = -1e30
decay_rate = 0.5
adam_epsilon = 1e-08
weight_decay = 0.01
vector_rate = 0.5

AXES = ("dp", "seq")
BF = jnp.bfloat16
F32 = jnp.float32
VMEM_LIMIT = 56 * 1024 * 1024
TILE = 256
COST = 16
ANY = pl.BlockSpec(memory_space=pl.ANY)
SMEM = pl.BlockSpec(memory_space=pltpu.SMEM)
VMEM = pl.BlockSpec(memory_space=pltpu.VMEM)


def nn(a, b):
    return lax.dot_general(a, b, (((1,), (0,)), ((), ())), preferred_element_type=F32)


def nt(a, b):
    return lax.dot_general(a, b, (((1,), (1,)), ((), ())), preferred_element_type=F32)


def tn(a, b):
    return lax.dot_general(a, b, (((0,), (0,)), ((), ())), preferred_element_type=F32)


class Grid:
    def __init__(self, chips):
        power = chips.bit_length() - 1
        if 1 << power == chips:
            self.side = 1 << (power // 3)
            self.nz = chips // (self.side * self.side)
        else:
            self.side, self.nz = 1, chips
        self.devices = 2 * chips
        self.xor = 1 << power == chips

    def z_mask(self, m):
        return m * 2 * self.side * self.side

    def x_mask(self, m):
        return 2 * m

    def y_mask(self, m):
        return 2 * m * self.side

    def label(self, core, other, i3, i2, iz):
        x = jnp.where(core == 0, i2, i3)
        y = jnp.where(core == 0, i3, i2)
        return self.z_mask(iz) + self.y_mask(y) + self.x_mask(x) + other


def permute(value, grid, mask_of_core):
    pairs = [(i, i ^ mask_of_core(i & 1)) for i in range(grid.devices)]
    return lax.ppermute(value, AXES, pairs)


def along_two(grid, value, m):
    return permute(value, grid, lambda c: grid.x_mask(m) if c == 0 else grid.y_mask(m))


def along_three(grid, value, m):
    return permute(value, grid, lambda c: grid.y_mask(m) if c == 0 else grid.x_mask(m))


def gather_z(grid, block):
    return [block] + [permute(block, grid, lambda c: grid.z_mask(m)) for m in range(1, grid.nz)]


def gather_two(grid, zed):
    return [zed] + [along_two(grid, zed, m) for m in range(1, grid.side)]


def gather_three(grid, two):
    return [along_three(grid, t, m) for m in range(1, grid.side) for t in two]


def with_core(grid, own):
    return own + [permute(p, grid, lambda c: 1) for p in own]


def is_path(grid, rows):
    return grid.xor and grid.side > 1 and rows % 16 == 0


def slot_of(grid, label, core):
    other = label & 1
    x = (label // 2) & (grid.side - 1)
    y = (label // (2 * grid.side)) & (grid.side - 1)
    z = label // (2 * grid.side * grid.side)
    first = (core ^ other) == 0
    i2 = jnp.where(first, x, y)
    i3 = jnp.where(first, y, x)
    return other, (i3 * grid.side + i2) * grid.nz + z


def natural_vectors(grid, pieces, core, me, row, count):
    side, nz = grid.side, grid.nz
    table = jnp.stack([p[:, row, :count] for p in pieces]).reshape(2, side, side, nz, count)
    turned = jnp.swapaxes(table, 1, 2)
    first = jnp.stack([table[0], turned[1]])
    second = jnp.stack([turned[0], table[1]])
    value = jnp.where(core == 0, first, second)
    value = jnp.transpose(value, (3, 1, 2, 0, 4)).reshape(grid.devices, count)
    bit = 1
    while bit < grid.devices:
        pairs = value.reshape(-1, 2, bit, count)
        value = jnp.where((me & bit) == 0, pairs, pairs[:, ::-1]).reshape(grid.devices, count)
        bit *= 2
    return value.reshape(1, -1).astype(F32)


def start_natural(grid, me_ref, pieces, dest, sems, first=0, last=None):
    last = grid.devices if last is None else last
    rows = dest.shape[0] // (last - first)
    if len(pieces) == 1:
        pltpu.make_async_copy(
            pieces[0].at[pl.ds(first * rows, (last - first) * rows)], dest, sems.at[0]
        ).start()
        return
    me = me_ref[0]
    at = 0
    for other in (0, 1):
        for i3 in range(grid.side):
            for i2 in range(grid.side):
                ref = pieces[at]
                at += 1
                for iz in range(grid.nz):
                    block = me ^ grid.label((me & 1) ^ other, other, i3, i2, iz)

                    def start(block=block, ref=ref, iz=iz):
                        row = pl.multiple_of((block - first) * rows, rows)
                        pltpu.make_async_copy(
                            ref.at[iz, pl.ds(0, rows)], dest.at[pl.ds(row, rows)], sems.at[block]
                        ).start()

                    if last - first == grid.devices:
                        start()
                    else:
                        pl.when((block >= first) & (block < last))(start)


def wait_natural(grid, pieces, dest, sems, begin, end, first=0, last=None):
    last = grid.devices if last is None else last
    rows = dest.shape[0] // (last - first)
    if len(pieces) == 1:
        if begin == first:
            pltpu.make_async_copy(
                pieces[0].at[pl.ds(first * rows, (last - first) * rows)], dest, sems.at[0]
            ).wait()
        return
    for block in range(begin, end):
        pltpu.make_async_copy(
            pieces[0].at[0, pl.ds(0, rows)],
            dest.at[pl.ds((block - first) * rows, rows)],
            sems.at[block],
        ).wait()


def path_shapes(grid, blocks, per, width):
    if not is_path(grid, per):
        return [
            jax.ShapeDtypeStruct((blocks * per, width), BF),
            jax.ShapeDtypeStruct((blocks, 8, width), BF),
        ]
    return [jax.ShapeDtypeStruct((blocks // 2, per, width), BF)] * 2


class Sums:
    def __init__(self, grid, path, keep, send):
        self.grid, self.path, self.keep, self.send = grid, path, keep, send
        self.three, self.two, self.z = [], [], []
        if path:
            self.core = permute(send, grid, lambda c: 1)

    def terms(self, i3, i2, iz):
        grid = self.grid
        base = (i3 * grid.side + i2) * grid.nz
        rows = slice(base + iz.start, base + iz.stop)
        total = self.keep[rows].astype(F32) + self.core[rows].astype(F32)
        if i3 == 0:
            for at, got in self.three:
                if at == i2:
                    total = total + got[iz].astype(F32)
            if i2 == 0:
                for got in self.two:
                    total = total + got[iz].astype(F32)
        return total

    def add_core(self):
        if not self.path:
            return []
        grid = self.grid
        every = slice(0, grid.nz)
        sends = [
            (i2, m, self.terms(m, i2, every).astype(BF))
            for i2 in reversed(range(grid.side))
            for m in range(1, grid.side)
        ]
        self.three = [(i2, along_three(grid, value, m)) for i2, m, value in sends]
        return [value for _, _, value in sends]

    def add_three(self):
        if not self.path:
            return []
        grid = self.grid
        every = slice(0, grid.nz)
        sends = [self.terms(0, m, every).astype(BF) for m in range(1, grid.side)]
        self.two = [along_two(grid, sends[m - 1], m) for m in range(1, grid.side)]
        return sends

    def add_two(self):
        if not self.path:
            return []
        grid = self.grid
        sends = [self.terms(0, 0, slice(m, m + 1))[0].astype(BF) for m in range(1, grid.nz)]
        self.z = [
            permute(sends[m - 1], grid, lambda c: grid.z_mask(m)) for m in range(1, grid.nz)
        ]
        return sends

    def add_z(self):
        if not self.path:
            rows = [v.reshape(-1, v.shape[-1]).astype(F32) for v in (self.keep, self.send)]
            return jnp.concatenate(
                [lax.psum_scatter(v, AXES, scatter_dimension=0, tiled=True) for v in rows]
            )
        total = self.terms(0, 0, slice(0, 1))[0]
        for got in self.z:
            total = total + got.astype(F32)
        return total


def params(**more):
    return pltpu.CompilerParams(vmem_limit_bytes=VMEM_LIMIT, **more)


def cost(macs, bytes_accessed, trans=0):
    return pl.CostEstimate(
        flops=2 * macs // COST, bytes_accessed=bytes_accessed // COST, transcendentals=trans // COST
    )


def rows_spec(width, tile=TILE):
    return pl.BlockSpec((tile, width), lambda i: (i, 0))


def whole(shape):
    zeros = (0,) * len(shape)
    return pl.BlockSpec(shape, lambda *i: zeros)


def fixed(*shape):
    zeros = (0,) * len(shape)
    return pl.BlockSpec(shape, lambda i: zeros)


def norm_rows(values):
    center = values - jnp.mean(values, axis=-1, keepdims=True)
    inverse = lax.rsqrt(jnp.mean(center * center, axis=-1, keepdims=True) + epsilon)
    return center * inverse, inverse


def norm_back(upstream, normed, inverse, gain):
    u = upstream * gain
    centered = u - jnp.mean(u, axis=-1, keepdims=True)
    return inverse * (centered - normed * jnp.mean(u * normed, axis=-1, keepdims=True))


def gelu_pair(u):
    z = jnp.abs(u) * math.sqrt(0.5)
    e = jnp.exp(-0.5 * u * u)
    t = 1.0 / (1.0 + 0.3275911 * z)
    poly = t * (
        0.254829592
        + t * (-0.284496736 + t * (1.421413741 + t * (-1.453152027 + t * 1.061405429)))
    )
    tail = 0.5 * poly * e
    phi = jnp.where(u >= 0, 1.0 - tail, tail)
    return u * phi, phi + u * (e * (1.0 / math.sqrt(2.0 * math.pi)))


def load_sequences(core, mine, others, dest, sems):
    count = mine.shape[0] // 2
    half = mine.shape[1]
    copies = []
    for s in range(count):
        seq = core * count + s
        for i, src in enumerate((mine, others)):
            at = s * 2 * half + (core ^ i) * half
            copies.append(
                pltpu.make_async_copy(
                    src.at[seq], dest.at[pl.ds(pl.multiple_of(at, half), half)], sems.at[2 * s + i]
                )
            )
    for copy in copies:
        copy.start()
    return copies


def store_sequences(core, src, mine, others, sems):
    count, half = others.shape[0], others.shape[1]
    copies = []
    for s in range(count):
        for i, dest in enumerate((mine.at[core * count + s], others.at[s])):
            at = s * 2 * half + (core ^ i) * half
            copies.append(
                pltpu.make_async_copy(
                    src.at[pl.ds(pl.multiple_of(at, half), half)], dest, sems.at[2 * s + i]
                )
            )
    for copy in copies:
        copy.start()
    return copies


def qkv_kernel(grid, me_ref, vec_ref, mine, others, *rest):
    pieces, (out_hbm, x_hbm, w, x, out, wsem, xsem, osem) = rest[:-8], rest[-8:]
    rows, width = x.shape
    scale = (width // H) ** -0.5
    core = me_ref[0] & 1
    loads = load_sequences(core, mine, others, x, xsem)
    blocks = grid.devices // 4
    start_natural(grid, me_ref, pieces, w, wsem, 0, 3 * blocks)
    for copy in loads:
        copy.wait()
    stores = [pltpu.make_async_copy(x, x_hbm, osem.at[3])]
    stores[0].start()
    for part in range(3):
        wait_natural(
            grid, pieces, w, wsem, part * blocks, (part + 1) * blocks, 0, 3 * blocks
        )
        cols = slice(part * width, (part + 1) * width)

        @pl.loop(0, rows // TILE)
        def _(r):
            at = pl.ds(pl.multiple_of(r * TILE, TILE), TILE)
            z = nt(x[at, :], w[cols, :])
            if part == 0:
                z = (z + vec_ref[:, 0:width]) * scale
            if part == 2:
                z = z + vec_ref[:, width : 2 * width]
            out[at, cols] = z.astype(BF)

        copy = pltpu.make_async_copy(out.at[:, cols], out_hbm.at[:, cols], osem.at[part])
        copy.start()
        stores.append(copy)
    for copy in stores:
        copy.wait()


def qkv_call(grid, me, vec, mine, others, pieces):
    width = mine.shape[2]
    rows = mine.shape[0] * mine.shape[1]
    return pl.pallas_call(
        lambda *r: qkv_kernel(grid, *r),
        in_specs=[SMEM, VMEM, ANY, ANY] + [ANY] * len(pieces),
        out_specs=[ANY, ANY],
        out_shape=[
            jax.ShapeDtypeStruct((rows, 3 * width), BF),
            jax.ShapeDtypeStruct((rows, width), BF),
        ],
        scratch_shapes=[
            pltpu.VMEM((3 * width, width), BF),
            pltpu.VMEM((rows, width), BF),
            pltpu.VMEM((rows, 3 * width), BF),
            pltpu.SemaphoreType.DMA((grid.devices,)),
            pltpu.SemaphoreType.DMA((mine.shape[0],)),
            pltpu.SemaphoreType.DMA((4,)),
        ],
        compiler_params=params(),
        cost_estimate=cost(rows * width * 3 * width, 12 << 20),
        name="qkv",
    )(me, vec, mine, others, *pieces)


def vector_refs(vec_ref, width):
    tail = 3 * width + FF
    found = [vec_ref[:, 2 * width : 3 * width], vec_ref[:, 3 * width : tail]]
    return found + [vec_ref[:, tail + i * width : tail + (i + 1) * width] for i in range(5)]


def attend_kernel(grid, npieces, seq, len_ref, me_ref, q_ref, k_ref, v_ref, x_ref, vec_ref, *rest):
    pieces = rest[:npieces]
    quarter = grid.devices // 4
    ctx_ref, lse_ref, normed_ref, inv_ref, hid_ref, w, sems = rest[-7:]
    turn = pl.program_id(0)

    @pl.when(turn == 0)
    def _():
        start_natural(grid, me_ref, pieces, w, sems, 3 * quarter)

    live_len = len_ref[seq]
    length, pair = q_ref.shape
    half = pair // 2
    q, k, v = q_ref[...], k_ref[...], v_ref[...]
    lane = lax.broadcasted_iota(jnp.int32, (length, pair), 1)
    live = lax.broadcasted_iota(jnp.int32, (1, length), 1) < live_len
    outs, stats = [], []
    for h in (0, 1):
        mine = (lane >= half) if h else (lane < half)
        s = nt(jnp.where(mine, q, jnp.zeros_like(q)), k)
        s = jnp.where(live, s, masked_score)
        top = jnp.max(s, axis=-1, keepdims=True)
        p = jnp.exp(s - top)
        total = jnp.sum(p, axis=-1, keepdims=True)
        outs.append(nn(p.astype(BF), v) / total)
        stats.append(top + jnp.log(total))
    ctx = jnp.where(lane < half, outs[0], outs[1]).astype(BF)
    ctx_ref[:, pl.ds(pl.multiple_of(turn * pair, pair), pair)] = ctx
    turned = jnp.where(lane < half, stats[0], stats[1]).T
    lse_ref[0] = jnp.concatenate([turned[0:1], turned[half : half + 1]], axis=0)

    @pl.when(turn == pl.num_programs(0) - 1)
    def _():
        wait_natural(grid, pieces, w, sems, 3 * quarter, grid.devices, 3 * quarter)
        bo, _, _, g1, e1, _, _ = vector_refs(vec_ref, x_ref.shape[1])
        r = x_ref[...].astype(F32) + (nt(ctx_ref[...], w[...]) + bo)
        normed, inverse = norm_rows(r)
        normed_ref[...] = normed
        inv_ref[...] = inverse
        hid_ref[...] = (normed * g1 + e1).astype(BF)


def attend_call(grid, me, lens, qkv, x, vec, pieces, seqs, seq, before, deps):
    rows, width = x.shape
    length = rows // seqs
    pairs = H // 2
    pw = width // pairs
    at = lambda part: pl.BlockSpec((length, pw), lambda p: (seq, part * pairs + p))
    seq_rows = lambda w: pl.BlockSpec((length, w), lambda p: (seq, 0))
    first = 7 + len(pieces)
    return pl.pallas_call(
        lambda *r: attend_kernel(grid, len(pieces), seq, *r),
        grid=(pairs,),
        in_specs=[SMEM, SMEM, at(0), at(1), at(2), seq_rows(width), whole(vec.shape)]
        + [ANY] * (len(pieces) + len(before) + len(deps)),
        out_specs=[
            seq_rows(width),
            pl.BlockSpec((1, 2, length), lambda p: (seq * pairs + p, 0, 0)),
            seq_rows(width),
            seq_rows(1),
            seq_rows(width),
        ],
        out_shape=[
            jax.ShapeDtypeStruct((rows, width), BF),
            jax.ShapeDtypeStruct((seqs * pairs, 2, length), F32),
            jax.ShapeDtypeStruct((rows, width), F32),
            jax.ShapeDtypeStruct((rows, 1), F32),
            jax.ShapeDtypeStruct((rows, width), BF),
        ],
        scratch_shapes=[
            pltpu.VMEM((width, width), BF),
            pltpu.SemaphoreType.DMA((grid.devices,)),
        ],
        input_output_aliases={first + i: i for i in range(len(before))},
        compiler_params=params(),
        cost_estimate=cost(8 * H * length * length * (width // H), 9 << 20, H * length * length),
        name="attend",
    )(lens, me, qkv, qkv, qkv, x, vec, *pieces, *before, *deps)


PARTS = 4


def ffn_kernel(grid, per, me_ref, vec_ref, inv_ref, h_hbm, normed_hbm, dy_mine, dy_others, *rest):
    npieces = len(rest) - 24
    pieces = rest[:npieces]
    (out_mine, out_others, dres_hbm, datt_hbm, sums_ref, db1_ref, keep_hbm, send_hbm) = rest[
        npieces : npieces + 8
    ]
    (w, h, normed, dy, act, gp, acc, dres, dbr, out, dpre, stage, wsem, isem, osem, dsem) = rest[
        npieces + 8 :
    ]
    rows, width = h.shape
    units = w.shape[0] // 2
    size = units // PARTS
    tiles = rows // TILE
    me = me_ref[0]
    core = me & 1

    _, b1, b2, g1, e1, g2, e2 = vector_refs(vec_ref, width)
    loads = [
        pltpu.make_async_copy(src, dst, isem.at[i])
        for i, (src, dst) in enumerate(((h_hbm, h), (normed_hbm, normed)))
    ]
    loads[0].start()
    start_natural(grid, me_ref, pieces, w, wsem)
    loads[1].start()
    loads += load_sequences(core, dy_mine, dy_others, dy, dsem)
    loads[0].wait()
    half = grid.devices // 2

    def tile(r):
        return pl.ds(pl.multiple_of(r * TILE, TILE), TILE)

    for part in range(PARTS):
        for base in (0, half):
            wait_natural(
                grid, pieces, w, wsem, base + part * half // PARTS, base + (part + 1) * half // PARTS
            )
        up = slice(part * size, (part + 1) * size)
        down = slice(units + part * size, units + (part + 1) * size)

        @pl.loop(0, tiles)
        def _(r):
            at = tile(r)
            a, slope = gelu_pair(nt(h[at, :], w[up, :]) + b1[:, up])
            a = a.astype(BF)
            act[at, up] = a
            gp[at, up] = slope.astype(BF)
            more = nn(a, w[down, :])
            if part == 0:
                acc[at, :] = more
            else:
                acc[at, :] += more

    for copy in loads[1:]:
        copy.wait()
    sums_ref[...] = jnp.zeros_like(sums_ref)

    @pl.loop(0, tiles)
    def _(r):
        at = tile(r)
        hidden = normed[at, :] * g1 + e1
        value = hidden + (acc[at, :] + b2)
        n, inverse = norm_rows(value)
        out[at, :] = (n * g2 + e2).astype(BF)
        up = dy[at, :].astype(F32)
        d = norm_back(up, n, inverse, g2)
        low = d.astype(BF)
        dres[at, :] = d
        dbr[at, :] = low
        sums_ref[0:1] += jnp.sum(up * n, axis=0, keepdims=True)
        sums_ref[1:2] += jnp.sum(up, axis=0, keepdims=True)
        sums_ref[2:3] += jnp.sum(low.astype(F32), axis=0, keepdims=True)

    out_copies = store_sequences(core, out, out_mine, out_others, dsem)

    path = is_path(grid, per)
    blocks = size // per
    pending = [[], []]

    def emit(part, side, value):
        slot = part % 2
        stage[slot, side] = value
        if not path:
            copy = pltpu.make_async_copy(
                stage.at[slot, side],
                keep_hbm.at[pl.ds(side * units + part * size, size)],
                osem.at[slot, side, 0],
            )
            copy.start()
            pending[slot].append(copy)
            return
        for b in range(0, blocks, 2):
            for other, ref in ((0, keep_hbm), (1, send_hbm)):
                here = b + (core ^ other)
                block = side * half + part * blocks + here
                _, place = slot_of(grid, me ^ block, core)
                copy = pltpu.make_async_copy(
                    stage.at[slot, side, pl.ds(pl.multiple_of(here * per, per), per)],
                    ref.at[place],
                    osem.at[slot, side, b + other],
                )
                copy.start()
                pending[slot].append(copy)

    for part in range(PARTS):
        up = slice(part * size, (part + 1) * size)
        down = slice(units + part * size, units + (part + 1) * size)

        db1_ref[:, up] = jnp.zeros((1, size), F32)

        @pl.loop(0, tiles)
        def _(r):
            at = tile(r)
            d = (nt(dbr[at, :], w[down, :]) * gp[at, up].astype(F32)).astype(BF)
            dpre[at, :] = d
            db1_ref[:, up] += jnp.sum(d.astype(F32), axis=0, keepdims=True)
            more = nn(d, w[up, :])
            if part == 0:
                acc[at, :] = more
            else:
                acc[at, :] += more

        for copy in pending[part % 2]:
            copy.wait()
        pending[part % 2] = []
        emit(part, 0, tn(dpre[...], h[...]).astype(BF))
        emit(part, 1, tn(act[:, up], dbr[...]).astype(BF))

    for copy in out_copies:
        copy.wait()

    @pl.loop(0, tiles)
    def _(r):
        at = tile(r)
        dhid = dres[at, :] + acc[at, :]
        n = normed[at, :]
        d = norm_back(dhid, n, inv_ref[at, :], g1)
        low = d.astype(BF)
        dres[at, :] = d
        out[at, :] = low
        sums_ref[3:4] += jnp.sum(dhid * n, axis=0, keepdims=True)
        sums_ref[4:5] += jnp.sum(dhid, axis=0, keepdims=True)
        sums_ref[5:6] += jnp.sum(low.astype(F32), axis=0, keepdims=True)

    stores = [
        pltpu.make_async_copy(dres, dres_hbm, isem.at[1]),
        pltpu.make_async_copy(out, datt_hbm, isem.at[2]),
    ]
    for copy in stores:
        copy.start()
    for copy in stores + pending[0] + pending[1]:
        copy.wait()


def ffn_call(grid, me, vec, inv, h, normed, dy_mine, dy_others, pieces, per):
    rows, width = h.shape
    total = grid.devices * per
    units = total // 2
    size = units // PARTS
    paths = path_shapes(grid, grid.devices, per, width)
    return pl.pallas_call(
        lambda *r: ffn_kernel(grid, per, *r),
        in_specs=[SMEM, VMEM, VMEM, ANY, ANY, ANY, ANY] + [ANY] * len(pieces),
        out_specs=[ANY, ANY, ANY, ANY, VMEM, VMEM, ANY, ANY],
        out_shape=[
            jax.ShapeDtypeStruct(dy_mine.shape, BF),
            jax.ShapeDtypeStruct((dy_mine.shape[0] // 2,) + dy_mine.shape[1:], BF),
            jax.ShapeDtypeStruct((rows, width), F32),
            jax.ShapeDtypeStruct((rows, width), BF),
            jax.ShapeDtypeStruct((8, width), F32),
            jax.ShapeDtypeStruct((1, units), F32),
        ]
        + paths,
        scratch_shapes=[
            pltpu.VMEM((total, width), BF),
            pltpu.VMEM((rows, width), BF),
            pltpu.VMEM((rows, width), F32),
            pltpu.VMEM((rows, width), BF),
            pltpu.VMEM((rows, units), BF),
            pltpu.VMEM((rows, units), BF),
            pltpu.VMEM((rows, width), F32),
            pltpu.VMEM((rows, width), F32),
            pltpu.VMEM((rows, width), BF),
            pltpu.VMEM((rows, width), BF),
            pltpu.VMEM((rows, size), BF),
            pltpu.VMEM((2, 2, size, width), BF),
            pltpu.SemaphoreType.DMA((grid.devices,)),
            pltpu.SemaphoreType.DMA((3,)),
            pltpu.SemaphoreType.DMA((2, 2, max(size // per, 2))),
            pltpu.SemaphoreType.DMA((dy_mine.shape[0],)),
        ],
        compiler_params=params(),
        cost_estimate=cost(6 * rows * width * units, 40 << 20, 2 * rows * units),
        name="ffn",
    )(me, vec, inv, h, normed, dy_mine, dy_others, *pieces)


def out_back_kernel(grid, me_ref, datt_ref, ctx_ref, *rest):
    pieces, (dctx_ref, grad_ref, _, w, sems) = rest[:-6], rest[-5:]

    @pl.when(pl.program_id(0) == 0)
    def _():
        start_natural(grid, me_ref, pieces, w, sems, 3 * grid.devices // 4)
        grad_ref[...] = jnp.zeros_like(grad_ref)

    datt = datt_ref[...]
    grad_ref[...] += tn(datt, ctx_ref[...])

    @pl.when(pl.program_id(0) == 0)
    def _():
        first = 3 * grid.devices // 4
        wait_natural(grid, pieces, w, sems, first, grid.devices, first)

    dctx_ref[...] = nn(datt, w[...]).astype(BF)


def out_back_call(grid, me, datt, ctx, pieces, carry):
    rows, width = ctx.shape
    return pl.pallas_call(
        lambda *r: out_back_kernel(grid, *r),
        grid=(rows // TILE,),
        in_specs=[SMEM, rows_spec(width), rows_spec(width)] + [ANY] * (len(pieces) + 1),
        out_specs=[rows_spec(width), fixed(width, width), ANY],
        out_shape=[
            jax.ShapeDtypeStruct((rows, width), BF),
            jax.ShapeDtypeStruct((width, width), F32),
            jax.ShapeDtypeStruct(carry.shape, carry.dtype),
        ],
        input_output_aliases={3 + len(pieces): 2},
        scratch_shapes=[
            pltpu.VMEM((width, width), BF),
            pltpu.SemaphoreType.DMA((grid.devices,)),
        ],
        compiler_params=params(),
        cost_estimate=cost(2 * rows * width * width, 12 << 20),
        name="out_back",
    )(me, datt, ctx, *pieces, carry)


def attend_back_kernel(seq, len_ref, q_ref, k_ref, v_ref, d_ref, lse_ref, *rest):
    dz_ref, db_ref, _ = rest[-3:]
    live_len = len_ref[seq]
    length, pair = q_ref.shape
    half = pair // 2
    q, k, v, d = q_ref[...], k_ref[...], v_ref[...], d_ref[...]
    lane = lax.broadcasted_iota(jnp.int32, (length, pair), 1)
    live = lax.broadcasted_iota(jnp.int32, (length, 1), 0) < live_len
    zero = jnp.zeros_like(q)
    dq = dk = dv = None
    for h in (0, 1):
        mine = (lane >= half) if h else (lane < half)
        qh, kh, dh = (jnp.where(mine, t, zero) for t in (q, k, d))
        s = nt(k, qh)
        p = jnp.where(live, jnp.exp(s - lse_ref[0, h : h + 1, :]), 0.0)
        dp = nt(v, dh)
        inner = jnp.sum(p * dp, axis=0, keepdims=True)
        ds = (p * (dp - inner)).astype(BF)
        a = nn(p.astype(BF), dh)
        b = nn(ds, qh)
        c = tn(ds, kh)
        dv = a if dv is None else dv + a
        dk = b if dk is None else dk + b
        dq = c if dq is None else dq + c
    scale = half ** -0.5
    dq = (dq.astype(BF).astype(F32) * scale).astype(BF)
    dv = dv.astype(BF)
    dz_ref[0] = dq
    dz_ref[1] = dk.astype(BF)
    dz_ref[2] = dv
    db_ref[0:1] = jnp.sum(dq.astype(F32), axis=0, keepdims=True)
    db_ref[1:2] = jnp.sum(dv.astype(F32), axis=0, keepdims=True)


def attend_back_call(lens, qkv, dctx, lse, seqs, seq, dz, carry, deps):
    rows, width = dctx.shape
    length = rows // seqs
    pairs = H // 2
    pw = width // pairs
    at = lambda part: pl.BlockSpec((length, pw), lambda p: (seq, part * pairs + p))
    more = [carry] + ([] if dz is None else [dz]) + list(deps)
    return pl.pallas_call(
        lambda *r: attend_back_kernel(seq, *r),
        grid=(pairs,),
        in_specs=[
            SMEM,
            at(0),
            at(1),
            at(2),
            at(0),
            pl.BlockSpec((1, 2, length), lambda p: (seq * pairs + p, 0, 0)),
        ]
        + [ANY] * len(more),
        out_specs=[
            pl.BlockSpec((3, length, pw), lambda p: (0, seq, p)),
            pl.BlockSpec((2, pw), lambda p: (0, p)),
            ANY,
        ],
        out_shape=[
            jax.ShapeDtypeStruct((3, rows, width), BF),
            jax.ShapeDtypeStruct((2, width), F32),
            jax.ShapeDtypeStruct(carry.shape, carry.dtype),
        ],
        input_output_aliases={6: 2} if dz is None else {6: 2, 7: 0},
        compiler_params=params(),
        cost_estimate=cost(
            20 * H * length * length * (width // H), 6 << 20, H * length * length
        ),
        name="attend_back",
    )(lens, qkv, qkv, qkv, dctx, lse, *more)


def attn_grad_kernel(grid, per, me_ref, dz_ref, x_ref, gout_ref, sums, db1, db_a, db_b, *rest):
    keep_ref, send_ref, total, line, gvec = rest[-5:]
    part = pl.program_id(0)
    width = x_ref.shape[1]
    total[pl.ds(pl.multiple_of(part * width, width), width), :] = tn(dz_ref[0], x_ref[...])

    @pl.when(part == 2)
    def _():
        total[3 * width :, :] = gout_ref[...]
        db = db_a[...] + db_b[...]
        tail = 3 * width + FF
        line[:, 0:width] = db[0:1]
        line[:, width : 2 * width] = db[1:2]
        line[:, 2 * width : 3 * width] = sums[5:6]
        line[:, 3 * width : tail] = db1[...]
        for i, row in enumerate((2, 3, 4, 0, 1)):
            line[:, tail + i * width : tail + (i + 1) * width] = sums[row : row + 1]
        count = line.shape[1] // grid.devices
        gvec[...] = jnp.zeros_like(gvec)
        for d in range(grid.devices):
            gvec[d, 0:1, 0:count] = line[:, d * count : (d + 1) * count]
        if not is_path(grid, per):
            keep_ref[...] = total[...].astype(BF)
            send_ref[...] = gvec[...].astype(BF)
            return
        me = me_ref[0]
        core = me & 1
        at = 0
        for i3 in range(grid.side):
            for i2 in range(grid.side):
                for iz in range(grid.nz):
                    for other, ref in ((0, keep_ref), (1, send_ref)):
                        block = me ^ grid.label(core ^ other, other, i3, i2, iz)
                        start = pl.multiple_of(block * per, per)
                        ref[at, 0:per] = total[pl.ds(start, per), :].astype(BF)
                        ref[at, per : per + 8] = gvec[block].astype(BF)
                    at += 1


def attn_grad_call(grid, me, dz, x, gout, vectors, per, deps):
    rows, width = x.shape
    paths = path_shapes(grid, grid.devices, per, width)
    if is_path(grid, per):
        paths = [jax.ShapeDtypeStruct((p.shape[0], per + 8, width), BF) for p in paths]
    return pl.pallas_call(
        lambda *r: attn_grad_kernel(grid, per, *r),
        grid=(3,),
        in_specs=[
            SMEM,
            pl.BlockSpec((1, rows, width), lambda i: (i, 0, 0)),
            fixed(rows, width),
            fixed(width, width),
        ]
        + [fixed(*v.shape) for v in vectors]
        + [ANY] * len(deps),
        out_specs=[whole(p.shape) for p in paths],
        out_shape=paths,
        scratch_shapes=[
            pltpu.VMEM((4 * width, width), F32),
            pltpu.VMEM((1, 8 * width + FF), F32),
            pltpu.VMEM((grid.devices, 8, width), F32),
        ],
        compiler_params=params(),
        cost_estimate=cost(3 * rows * width * width, 16 << 20),
        name="attn_grad",
    )(me, dz, x, gout, *vectors, *deps)


def input_grad_kernel(grid, me_ref, dz_hbm, dres_hbm, *rest):
    pieces, (mine, others, _, dz, total, w, sems, isem, osem) = rest[:-10], rest[-9:]
    rows, width = total.shape
    blocks = grid.devices // 4
    core = me_ref[0] & 1
    loads = [
        pltpu.make_async_copy(dz_hbm.at[part], dz.at[part], isem.at[part]) for part in range(3)
    ] + [pltpu.make_async_copy(dres_hbm, total, isem.at[3])]
    loads[3].start()
    loads[0].start()
    start_natural(grid, me_ref, pieces, w, sems, 0, 3 * blocks)
    loads[1].start()
    loads[2].start()
    loads[3].wait()
    for part in range(3):
        loads[part].wait()
        wait_natural(grid, pieces, w, sems, part * blocks, (part + 1) * blocks, 0, 3 * blocks)

        @pl.loop(0, rows // TILE)
        def _(r):
            at = pl.ds(pl.multiple_of(r * TILE, TILE), TILE)
            total[at, :] += nn(dz[part, at, :], w[part * width : (part + 1) * width, :])

    for copy in store_sequences(core, total, mine, others, osem):
        copy.wait()


def input_grad_call(grid, me, dz, dres, pieces, shape, carry):
    rows, width = dres.shape
    return pl.pallas_call(
        lambda *r: input_grad_kernel(grid, *r),
        in_specs=[SMEM, ANY, ANY] + [ANY] * (len(pieces) + 1),
        out_specs=[ANY, ANY, ANY],
        out_shape=[
            jax.ShapeDtypeStruct(shape, F32),
            jax.ShapeDtypeStruct((shape[0] // 2,) + shape[1:], F32),
            jax.ShapeDtypeStruct(carry.shape, carry.dtype),
        ],
        input_output_aliases={3 + len(pieces): 2},
        scratch_shapes=[
            pltpu.VMEM((3, rows, width), BF),
            pltpu.VMEM((rows, width), F32),
            pltpu.VMEM((3 * width, width), BF),
            pltpu.SemaphoreType.DMA((grid.devices,)),
            pltpu.SemaphoreType.DMA((4,)),
            pltpu.SemaphoreType.DMA((shape[0],)),
        ],
        compiler_params=params(),
        cost_estimate=cost(3 * rows * width * width, 16 << 20),
        name="input_grad",
    )(me, dz, dres, *pieces, carry)


def gate(value, deps):
    return pl.pallas_call(
        lambda *r: None,
        in_specs=[ANY] * (1 + len(deps)),
        out_specs=ANY,
        out_shape=jax.ShapeDtypeStruct(value.shape, value.dtype),
        input_output_aliases={0: 0},
        compiler_params=params(),
        cost_estimate=cost(0, 0),
        name="gate",
    )(value, *deps)


def ordered_block_kernel(w_ref, *rest):
    rest[-1][...] = w_ref[...].T.astype(BF)


def ordered_block(weights, deps):
    width, per = weights.shape
    return pl.pallas_call(
        ordered_block_kernel,
        in_specs=[VMEM] + [ANY] * len(deps),
        out_specs=VMEM,
        out_shape=jax.ShapeDtypeStruct((per, width), BF),
        compiler_params=params(),
        name="ordered_block",
    )(weights, *deps)


def ordered_stack_kernel(count, *rest):
    for i in range(count):
        rest[-1][i] = rest[i][...]


def ordered_stack(parts, deps):
    return pl.pallas_call(
        lambda *r: ordered_stack_kernel(len(parts), *r),
        in_specs=[VMEM] * len(parts) + [ANY] * len(deps),
        out_specs=VMEM,
        out_shape=jax.ShapeDtypeStruct((len(parts),) + parts[0].shape, parts[0].dtype),
        compiler_params=params(),
        name="ordered_stack",
    )(*parts, *deps)


def adam_update(master, moment, second, grad, rate):
    moment_new = decay_rate * moment + (1.0 - decay_rate) * grad
    second_new = decay_rate * second + (1.0 - decay_rate) * grad * grad
    correction = 1.0 - decay_rate**STEP
    direction = moment_new / correction / (jnp.sqrt(second_new / correction) + adam_epsilon)
    master_new = master - rate * (direction + weight_decay * master)
    return (moment_new, second_new, master_new)


def join_sequences(mine, others, core):
    count = others.shape[0]
    return lax.dynamic_update_slice(mine, others, ((1 - core) * count, 0, 0))


def local(
    tokens,
    cotangent,
    seq_lengths,
    slot_order,
    attn_weights,
    attn_moment,
    attn_second,
    ffn_weights,
    ffn_moment,
    ffn_second,
    vectors,
    vector_moment,
    vector_second,
):
    grid = Grid(lax.axis_size("dp"))
    core = lax.axis_index("seq")
    shard_index = lax.axis_index(AXES)
    me = shard_index.astype(jnp.int32).reshape(1)
    seq_count, half_len, width = tokens.shape
    seqs = seq_count // 2
    length = 2 * half_len
    rows = seqs * length
    per, ffn_per = attn_weights.shape[1], ffn_weights.shape[1]
    vec_per = vectors.shape[0]
    path = is_path(grid, per) and is_path(grid, ffn_per)

    slot_pick = (slot_order[0][:, None] == jnp.arange(seq_count)[None, :]).astype(jnp.int32)
    slot_len = jnp.sum(slot_pick * seq_lengths[0][None, :], axis=1)
    lens = lax.dynamic_slice_in_dim(slot_len, core * seqs, seqs, 0)

    vec_rows = jnp.zeros((8, width), BF)
    vec_rows = lax.dynamic_update_slice(vec_rows, vectors.astype(BF)[None, :], (0, 0))
    attn_block = jnp.concatenate([attn_weights.astype(BF).T, vec_rows])
    ffn_block = ffn_weights.astype(BF).T

    other_core = lambda value: permute(value, grid, lambda c: 1)
    tokens_other = other_core(tokens)
    if path:
        attn_parts = gather_z(grid, attn_block)
        ffn_block = ordered_block(ffn_weights, attn_parts[1:2])
        ffn_parts = gather_z(grid, ffn_block)
        attn_z = jnp.stack(attn_parts)
        attn_two = gather_two(grid, attn_z)
        attn_three = gather_three(grid, attn_two)
        ffn_z = ordered_stack(ffn_parts, attn_three[-1:])
        ffn_two = gather_two(grid, ffn_z)
        weights = with_core(grid, attn_two + attn_three)
        vec = natural_vectors(grid, weights, core, me[0], per, vec_per)
    else:
        whole_rows = lambda block: [lax.all_gather(block, AXES, axis=0, tiled=True)]
        weights = whole_rows(attn_block[:per])
        ffn_pieces = whole_rows(ordered_block(ffn_weights, []))
        ffn_two = []
        vec = lax.all_gather(attn_block[per:], AXES)[:, 0, :vec_per].reshape(1, -1).astype(F32)
    dy_other = other_core(cotangent)

    qkv, x = qkv_call(grid, me, vec, tokens, tokens_other, weights)
    fwd = attend_call(grid, me, lens, qkv, x, vec, weights, seqs, 0, [], [])
    ffn_two = ffn_two[:1] + [gate(t, fwd[:1]) for t in ffn_two[1:]]
    fwd = attend_call(grid, me, lens, qkv, x, vec, weights, seqs, 1, fwd, ffn_two[1:])
    ctx, lse, normed, inv, hidden = fwd
    if path:
        ffn_three = gather_three(grid, ffn_two)
        ffn_three = ffn_three[:1] + [gate(t, fwd[:1]) for t in ffn_three[1:]]
        ffn_pieces = with_core(grid, ffn_two + ffn_three)
    out, out_other, dres_one, datt, sums, db1, keep_f, send_f = ffn_call(
        grid, me, vec, inv, hidden, normed, cotangent, dy_other, ffn_pieces, ffn_per
    )
    layer_out = join_sequences(out, other_core(out_other), core)

    sums_f = Sums(grid, path, keep_f, send_f)
    dctx, gout, sums_f.keep = out_back_call(grid, me, datt, ctx, weights, sums_f.keep)
    sends = sums_f.add_core()
    dz, db_a, sums_f.keep = attend_back_call(
        lens, qkv, dctx, lse, seqs, 0, None, sums_f.keep, sends
    )
    sends = sums_f.add_three()
    dz, db_b, sums_f.keep = attend_back_call(
        lens, qkv, dctx, lse, seqs, 1, dz, sums_f.keep, sends
    )
    sends = sums_f.add_two()
    keep_c, send_c = attn_grad_call(
        grid, me, dz, x, gout, [sums, db1, db_a, db_b], per, sends
    )
    sums_c = Sums(grid, path, keep_c, send_c)
    sums_c.add_core()
    dx, dx_other, sums_c.keep = input_grad_call(
        grid, me, dz, dres_one, weights, tokens.shape, sums_c.keep
    )
    sums_c.add_three()
    input_grad = join_sequences(dx, other_core(dx_other), core)
    sums_c.add_two()
    ffn_sum = sums_f.add_z()
    attn_sum = sums_c.add_z()

    vector_sum = attn_sum[per, :vec_per]
    attn_sum = attn_sum[:per].T
    ffn_sum = ffn_sum[:ffn_per].T

    attn_cols = shard_index * per + jnp.arange(per)
    attn_rate = jnp.where(
        attn_cols < 2 * width, math.sqrt(2.0), jnp.where(attn_cols < 3 * width, 1.5, 1.8)
    ) * width ** (-0.5)
    ffn_cols = shard_index * ffn_per + jnp.arange(ffn_per)
    ffn_rate = jnp.where(ffn_cols < FF, width ** (-0.5), 1.5 * FF ** (-0.5))
    attn_m, attn_v, attn_new = adam_update(
        attn_weights, attn_moment, attn_second, attn_sum, attn_rate[None, :]
    )
    ffn_m, ffn_v, ffn_new = adam_update(
        ffn_weights, ffn_moment, ffn_second, ffn_sum, ffn_rate[None, :]
    )
    vec_m, vec_v, vec_new = adam_update(
        vectors, vector_moment, vector_second, vector_sum, vector_rate
    )
    return (
        layer_out,
        input_grad,
        attn_m,
        attn_v,
        attn_new,
        attn_new.astype(BF),
        ffn_m,
        ffn_v,
        ffn_new,
        ffn_new.astype(BF),
        vec_m,
        vec_v,
        vec_new,
        vec_new.astype(BF),
    )


def solution(mesh):
    columns = P(None, AXES)
    flat = P(AXES)
    rows = P("dp", "seq", None)
    placed = (rows, rows, P("dp", None), P("dp", None)) + (columns,) * 6 + (flat,) * 3
    return jax.shard_map(
        local,
        mesh=mesh,
        in_specs=placed,
        out_specs=(rows, rows) + (columns,) * 8 + (flat,) * 4,
        check_vma=False,
    )
```

```python
import math

import jax
import jax.numpy as jnp
from jax import lax
from jax.experimental import pallas as pl
from jax.experimental.pallas import tpu as pltpu
from jax.sharding import PartitionSpec as P

H = 12
FF = 3072
STEP = 5

epsilon = 1e-06
masked_score = -1e30
decay_rate = 0.5
adam_epsilon = 1e-08
weight_decay = 0.01
vector_rate = 0.5

AXES = ("dp", "seq")
BF = jnp.bfloat16
F32 = jnp.float32
VMEM_LIMIT = 56 * 1024 * 1024
TILE = 256
COST = 16
ANY = pl.BlockSpec(memory_space=pl.ANY)
SMEM = pl.BlockSpec(memory_space=pltpu.SMEM)
VMEM = pl.BlockSpec(memory_space=pltpu.VMEM)


def nn(a, b):
    return lax.dot_general(a, b, (((1,), (0,)), ((), ())), preferred_element_type=F32)


def nt(a, b):
    return lax.dot_general(a, b, (((1,), (1,)), ((), ())), preferred_element_type=F32)


def tn(a, b):
    return lax.dot_general(a, b, (((0,), (0,)), ((), ())), preferred_element_type=F32)


class Grid:
    def __init__(self, chips):
        power = chips.bit_length() - 1
        if 1 << power == chips:
            self.side = 1 << (power // 3)
            self.nz = chips // (self.side * self.side)
        else:
            self.side, self.nz = 1, chips
        self.devices = 2 * chips
        self.xor = 1 << power == chips

    def z_mask(self, m):
        return m * 2 * self.side * self.side

    def x_mask(self, m):
        return 2 * m

    def y_mask(self, m):
        return 2 * m * self.side

    def label(self, core, other, i3, i2, iz):
        x = jnp.where(core == 0, i2, i3)
        y = jnp.where(core == 0, i3, i2)
        return self.z_mask(iz) + self.y_mask(y) + self.x_mask(x) + other


def permute(value, grid, mask_of_core):
    pairs = [(i, i ^ mask_of_core(i & 1)) for i in range(grid.devices)]
    return lax.ppermute(value, AXES, pairs)


def along_two(grid, value, m):
    return permute(value, grid, lambda c: grid.x_mask(m) if c == 0 else grid.y_mask(m))


def along_three(grid, value, m):
    return permute(value, grid, lambda c: grid.y_mask(m) if c == 0 else grid.x_mask(m))


def gather_z(grid, block):
    return [block] + [permute(block, grid, lambda c: grid.z_mask(m)) for m in range(1, grid.nz)]


def gather_two(grid, zed):
    return [zed] + [along_two(grid, zed, m) for m in range(1, grid.side)]


def gather_three(grid, two):
    return [along_three(grid, t, m) for m in range(1, grid.side) for t in two]


def with_core(grid, own, deps):
    own = [gate(own[0], deps) if deps else own[0]] + own[1:]
    return own + [permute(p, grid, lambda c: 1) for p in own]


def is_path(grid, rows):
    return grid.xor and grid.side > 1 and rows % 16 == 0


def slot_of(grid, label, core):
    other = label & 1
    x = (label // 2) & (grid.side - 1)
    y = (label // (2 * grid.side)) & (grid.side - 1)
    z = label // (2 * grid.side * grid.side)
    first = (core ^ other) == 0
    i2 = jnp.where(first, x, y)
    i3 = jnp.where(first, y, x)
    return other, (i3 * grid.side + i2) * grid.nz + z


def natural_vectors(grid, pieces, core, me, row, count):
    side, nz = grid.side, grid.nz
    table = jnp.stack([p[:, row, :count] for p in pieces]).reshape(2, side, side, nz, count)
    turned = jnp.swapaxes(table, 1, 2)
    first = jnp.stack([table[0], turned[1]])
    second = jnp.stack([turned[0], table[1]])
    value = jnp.where(core == 0, first, second)
    value = jnp.transpose(value, (3, 1, 2, 0, 4)).reshape(grid.devices, count)
    bit = 1
    while bit < grid.devices:
        pairs = value.reshape(-1, 2, bit, count)
        value = jnp.where((me & bit) == 0, pairs, pairs[:, ::-1]).reshape(grid.devices, count)
        bit *= 2
    return value.reshape(1, -1).astype(F32)


def start_natural(grid, me_ref, pieces, dest, sems, first=0, last=None, order=None):
    last = grid.devices if last is None else last
    rows = dest.shape[0] // (last - first)
    if len(pieces) == 1:
        pltpu.make_async_copy(
            pieces[0].at[pl.ds(first * rows, (last - first) * rows)], dest, sems.at[0]
        ).start()
        return
    me = me_ref[0]
    core = me & 1
    side, nz = grid.side, grid.nz
    for label in sorted(range(grid.devices), key=order or (lambda j: j // (2 * side * side))):
        other, x, y = label & 1, label // 2 % side, label // (2 * side) % side
        iz = label // (2 * side * side)
        block = me ^ label

        def start(ref, block=block, iz=iz):
            row = pl.multiple_of((block - first) * rows, rows)
            pltpu.make_async_copy(
                ref.at[iz, pl.ds(0, rows)], dest.at[pl.ds(row, rows)], sems.at[block]
            ).start()

        def either(other=other, x=x, y=y, start=start):
            one = pieces[(other * side + y) * side + x]
            two = pieces[(other * side + x) * side + y]
            if x == y:
                start(one)
            else:
                pl.when((core ^ other) == 0)(lambda: start(one))
                pl.when((core ^ other) != 0)(lambda: start(two))

        if last - first == grid.devices:
            either()
        else:
            pl.when((block >= first) & (block < last))(either)


def wait_natural(grid, pieces, dest, sems, begin, count, first=0, last=None):
    last = grid.devices if last is None else last
    rows = dest.shape[0] // (last - first)
    if len(pieces) == 1:

        @pl.when(begin == first)
        def _():
            pltpu.make_async_copy(
                pieces[0].at[pl.ds(first * rows, (last - first) * rows)], dest, sems.at[0]
            ).wait()

        return
    for i in range(count):
        block = begin + i
        pltpu.make_async_copy(
            pieces[0].at[0, pl.ds(0, rows)],
            dest.at[pl.ds(pl.multiple_of((block - first) * rows, rows), rows)],
            sems.at[block],
        ).wait()


def path_shapes(grid, blocks, per, width):
    if not is_path(grid, per):
        return [
            jax.ShapeDtypeStruct((blocks * per, width), BF),
            jax.ShapeDtypeStruct((blocks, 8, width), BF),
        ]
    return [jax.ShapeDtypeStruct((blocks // 2, per, width), BF)] * 2


class Sums:
    def __init__(self, grid, path, keep, send):
        self.grid, self.path, self.keep, self.send = grid, path, keep, send
        self.three, self.two, self.z = [], [], []
        if path:
            self.core = permute(send, grid, lambda c: 1)

    def terms(self, i3, i2, iz):
        grid = self.grid
        base = (i3 * grid.side + i2) * grid.nz
        rows = slice(base + iz.start, base + iz.stop)
        total = self.keep[rows].astype(F32) + self.core[rows].astype(F32)
        if i3 == 0:
            for at, got in self.three:
                if at == i2:
                    total = total + got[iz].astype(F32)
            if i2 == 0:
                for got in self.two:
                    total = total + got[iz].astype(F32)
        return total

    def add_core(self):
        if not self.path:
            return []
        grid = self.grid
        every = slice(0, grid.nz)
        sends = [
            (i2, m, self.terms(m, i2, every).astype(BF))
            for i2 in reversed(range(grid.side))
            for m in range(1, grid.side)
        ]
        self.three = [(i2, along_three(grid, value, m)) for i2, m, value in sends]
        return [value for _, _, value in sends]

    def add_three(self):
        if not self.path:
            return []
        grid = self.grid
        every = slice(0, grid.nz)
        sends = [self.terms(0, m, every).astype(BF) for m in range(1, grid.side)]
        self.two = [along_two(grid, sends[m - 1], m) for m in range(1, grid.side)]
        return sends

    def add_two(self):
        if not self.path:
            return []
        grid = self.grid
        sends = [self.terms(0, 0, slice(m, m + 1))[0].astype(BF) for m in range(1, grid.nz)]
        self.z = [
            permute(sends[m - 1], grid, lambda c: grid.z_mask(m)) for m in range(1, grid.nz)
        ]
        return sends

    def add_z(self):
        if not self.path:
            rows = [v.reshape(-1, v.shape[-1]).astype(F32) for v in (self.keep, self.send)]
            return jnp.concatenate(
                [lax.psum_scatter(v, AXES, scatter_dimension=0, tiled=True) for v in rows]
            )
        total = self.terms(0, 0, slice(0, 1))[0]
        for got in self.z:
            total = total + got.astype(F32)
        return total


def params(**more):
    return pltpu.CompilerParams(vmem_limit_bytes=VMEM_LIMIT, **more)


def cost(macs, bytes_accessed, trans=0):
    return pl.CostEstimate(
        flops=2 * macs // COST, bytes_accessed=bytes_accessed // COST, transcendentals=trans // COST
    )


def rows_spec(width, tile=TILE):
    return pl.BlockSpec((tile, width), lambda i: (i, 0))


def whole(shape):
    zeros = (0,) * len(shape)
    return pl.BlockSpec(shape, lambda *i: zeros)


def fixed(*shape):
    zeros = (0,) * len(shape)
    return pl.BlockSpec(shape, lambda i: zeros)


def norm_rows(values):
    center = values - jnp.mean(values, axis=-1, keepdims=True)
    inverse = lax.rsqrt(jnp.mean(center * center, axis=-1, keepdims=True) + epsilon)
    return center * inverse, inverse


def norm_back(upstream, normed, inverse, gain):
    u = upstream * gain
    centered = u - jnp.mean(u, axis=-1, keepdims=True)
    return inverse * (centered - normed * jnp.mean(u * normed, axis=-1, keepdims=True))


def gelu_pair(u):
    phi = 0.5 + 0.5 * lax.erf(u * math.sqrt(0.5))
    density = jnp.exp(-0.5 * (u * u))
    return u * phi, phi + (u * (1.0 / math.sqrt(2.0 * math.pi))) * density


def load_sequences(core, mine, others, dest, sems):
    count = mine.shape[0] // 2
    half = mine.shape[1]
    copies = []
    for s in range(count):
        seq = core * count + s
        for i, src in enumerate((mine, others)):
            at = s * 2 * half + (core ^ i) * half
            copies.append(
                pltpu.make_async_copy(
                    src.at[seq], dest.at[pl.ds(pl.multiple_of(at, half), half)], sems.at[2 * s + i]
                )
            )
    for copy in copies:
        copy.start()
    return copies


def store_sequences(core, src, mine, others, sems):
    count, half = others.shape[0], others.shape[1]
    copies = []
    for s in range(count):
        for i, dest in enumerate((mine.at[core * count + s], others.at[s])):
            at = s * 2 * half + (core ^ i) * half
            copies.append(
                pltpu.make_async_copy(
                    src.at[pl.ds(pl.multiple_of(at, half), half)], dest, sems.at[2 * s + i]
                )
            )
    for copy in copies:
        copy.start()
    return copies


def quarter_order(grid, me_ref, pieces, i):
    if len(pieces) == 1:
        return i
    lines = grid.nz // 4
    return (i * lines ^ me_ref[0] // (2 * grid.side * grid.side)) // lines


def qkv_kernel(grid, me_ref, vec_ref, mine, others, *rest):
    pieces, (out_hbm, x_hbm, w, x, out, wsem, xsem, osem) = rest[:-8], rest[-8:]
    rows, width = x.shape
    core = me_ref[0] & 1
    loads = load_sequences(core, mine, others, x, xsem)
    blocks = grid.devices // 4
    start_natural(grid, me_ref, pieces, w, wsem, 0, 3 * blocks)
    for copy in loads:
        copy.wait()
    copy_x = pltpu.make_async_copy(x, x_hbm, osem.at[3])
    copy_x.start()

    def store(part):
        cols = pl.ds(pl.multiple_of(part * width, width), width)
        return pltpu.make_async_copy(out.at[:, cols], out_hbm.at[:, cols], osem.at[part])

    @pl.loop(0, 4)
    def _(i):
        part = quarter_order(grid, me_ref, pieces, i)

        @pl.when(part < 3)
        def _():
            wait_natural(grid, pieces, w, wsem, part * blocks, blocks, 0, 3 * blocks)
            cols = pl.ds(pl.multiple_of(part * width, width), width)
            bias = vec_ref[:, pl.ds(pl.multiple_of(part // 2 * width, width), width)]
            bias = jnp.where(part == 1, 0.0, bias)
            scale = jnp.where(part == 0, (width // H) ** -0.5, 1.0)
            out[:, cols] = ((nt(x[...], w[cols, :]) + bias) * scale).astype(BF)
            store(part).start()

    for part in range(3):
        store(part).wait()
    copy_x.wait()


def qkv_call(grid, me, vec, mine, others, pieces):
    width = mine.shape[2]
    rows = mine.shape[0] * mine.shape[1]
    return pl.pallas_call(
        lambda *r: qkv_kernel(grid, *r),
        in_specs=[SMEM, VMEM, ANY, ANY] + [ANY] * len(pieces),
        out_specs=[ANY, ANY],
        out_shape=[
            jax.ShapeDtypeStruct((rows, 3 * width), BF),
            jax.ShapeDtypeStruct((rows, width), BF),
        ],
        scratch_shapes=[
            pltpu.VMEM((3 * width, width), BF),
            pltpu.VMEM((rows, width), BF),
            pltpu.VMEM((rows, 3 * width), BF),
            pltpu.SemaphoreType.DMA((grid.devices,)),
            pltpu.SemaphoreType.DMA((mine.shape[0],)),
            pltpu.SemaphoreType.DMA((4,)),
        ],
        compiler_params=params(),
        cost_estimate=cost(rows * width * 3 * width, 12 << 20),
        name="qkv",
    )(me, vec, mine, others, *pieces)


def vector_refs(vec_ref, width):
    tail = 3 * width + FF
    found = [vec_ref[:, 2 * width : 3 * width], vec_ref[:, 3 * width : tail]]
    return found + [vec_ref[:, tail + i * width : tail + (i + 1) * width] for i in range(5)]


def attend_kernel(grid, npieces, seq, len_ref, me_ref, q_ref, k_ref, v_ref, x_ref, vec_ref, *rest):
    pieces = rest[:npieces]
    quarter = grid.devices // 4
    ctx_ref, lse_ref, normed_ref, inv_ref, hid_ref, w, sems = rest[-7:]
    turn = pl.program_id(0)

    @pl.when(turn == 0)
    def _():
        start_natural(grid, me_ref, pieces, w, sems, 3 * quarter)

    live_len = len_ref[seq]
    length, pair = q_ref.shape
    half = pair // 2
    q, k, v = q_ref[...], k_ref[...], v_ref[...]
    lane = lax.broadcasted_iota(jnp.int32, (length, pair), 1)
    live = lax.broadcasted_iota(jnp.int32, (1, length), 1) < live_len
    outs, stats = [], []
    for h in (0, 1):
        mine = (lane >= half) if h else (lane < half)
        s = nt(jnp.where(mine, q, jnp.zeros_like(q)), k)
        s = jnp.where(live, s, masked_score)
        top = jnp.max(s, axis=-1, keepdims=True)
        p = jnp.exp(s - top)
        total = jnp.sum(p, axis=-1, keepdims=True)
        outs.append(nn(p.astype(BF), v) / total)
        stats.append(top + jnp.log(total))
    ctx = jnp.where(lane < half, outs[0], outs[1]).astype(BF)
    ctx_ref[:, pl.ds(pl.multiple_of(turn * pair, pair), pair)] = ctx
    turned = jnp.where(lane < half, stats[0], stats[1]).T
    lse_ref[0] = jnp.concatenate([turned[0:1], turned[half : half + 1]], axis=0)

    @pl.when(turn == pl.num_programs(0) - 1)
    def _():
        wait_natural(grid, pieces, w, sems, 3 * quarter, quarter, 3 * quarter)
        bo, _, _, g1, e1, _, _ = vector_refs(vec_ref, x_ref.shape[1])
        r = x_ref[...].astype(F32) + (nt(ctx_ref[...], w[...]) + bo)
        normed, inverse = norm_rows(r)
        normed_ref[...] = normed
        inv_ref[...] = inverse
        hid_ref[...] = (normed * g1 + e1).astype(BF)


def attend_call(grid, me, lens, qkv, x, vec, pieces, seqs, seq, before, deps):
    rows, width = x.shape
    length = rows // seqs
    pairs = H // 2
    pw = width // pairs
    at = lambda part: pl.BlockSpec((length, pw), lambda p: (seq, part * pairs + p))
    seq_rows = lambda w: pl.BlockSpec((length, w), lambda p: (seq, 0))
    first = 7 + len(pieces)
    return pl.pallas_call(
        lambda *r: attend_kernel(grid, len(pieces), seq, *r),
        grid=(pairs,),
        in_specs=[SMEM, SMEM, at(0), at(1), at(2), seq_rows(width), whole(vec.shape)]
        + [ANY] * (len(pieces) + len(before) + len(deps)),
        out_specs=[
            seq_rows(width),
            pl.BlockSpec((1, 2, length), lambda p: (seq * pairs + p, 0, 0)),
            seq_rows(width),
            seq_rows(1),
            seq_rows(width),
        ],
        out_shape=[
            jax.ShapeDtypeStruct((rows, width), BF),
            jax.ShapeDtypeStruct((seqs * pairs, 2, length), F32),
            jax.ShapeDtypeStruct((rows, width), F32),
            jax.ShapeDtypeStruct((rows, 1), F32),
            jax.ShapeDtypeStruct((rows, width), BF),
        ],
        scratch_shapes=[
            pltpu.VMEM((width, width), BF),
            pltpu.SemaphoreType.DMA((grid.devices,)),
        ],
        input_output_aliases={first + i: i for i in range(len(before))},
        compiler_params=params(),
        cost_estimate=cost(8 * H * length * length * (width // H), 9 << 20, H * length * length),
        name="attend",
    )(lens, me, qkv, qkv, qkv, x, vec, *pieces, *before, *deps)


PARTS = 4


def ffn_kernel(grid, per, me_ref, vec_ref, inv_ref, h_hbm, normed_hbm, dy_mine, dy_others, *rest):
    npieces = len(rest) - 24
    pieces = rest[:npieces]
    (out_mine, out_others, dres_hbm, datt_hbm, sums_ref, db1_ref, keep_hbm, send_hbm) = rest[
        npieces : npieces + 8
    ]
    (w, h, normed, dy, act, gp, acc, dres, dbr, out, dpre, stage, wsem, isem, osem, dsem) = rest[
        npieces + 8 :
    ]
    rows, width = h.shape
    units = w.shape[0] // 2
    size = units // PARTS
    tiles = rows // TILE
    me = me_ref[0]
    core = me & 1

    _, _, b2, g1, e1, g2, e2 = vector_refs(vec_ref, width)
    loads = [
        pltpu.make_async_copy(src, dst, isem.at[i])
        for i, (src, dst) in enumerate(((h_hbm, h), (normed_hbm, normed)))
    ]
    loads[0].start()
    half = grid.devices // 2
    start_natural(grid, me_ref, pieces, w, wsem, order=lambda j: (j % half // (half // PARTS), j))
    loads[1].start()
    loads += load_sequences(core, dy_mine, dy_others, dy, dsem)
    loads[0].wait()

    def tile(r):
        return pl.ds(pl.multiple_of(r * TILE, TILE), TILE)

    def natural_part(part):
        if len(pieces) == 1:
            return part
        return part ^ (me % half // (half // PARTS))

    def span(start, count):
        return pl.ds(pl.multiple_of(start, count), count)

    for part in range(PARTS):
        there = natural_part(part)
        for base in (0, half):
            wait_natural(
                grid, pieces, w, wsem, base + there * (half // PARTS), half // PARTS
            )
        here = slice(part * size, (part + 1) * size)
        up, down = span(there * size, size), span(units + there * size, size)
        a, slope = gelu_pair(nt(h[...], w[up, :]) + vec_ref[:, span(3 * width + there * size, size)])
        a = a.astype(BF)
        act[:, here] = a
        gp[:, here] = slope.astype(BF)
        more = nn(a, w[down, :])
        if part == 0:
            acc[...] = more
        else:
            acc[...] += more

    for copy in loads[1:]:
        copy.wait()
    sums_ref[...] = jnp.zeros_like(sums_ref)

    @pl.loop(0, tiles)
    def _(r):
        at = tile(r)
        hidden = normed[at, :] * g1 + e1
        value = hidden + (acc[at, :] + b2)
        n, inverse = norm_rows(value)
        out[at, :] = (n * g2 + e2).astype(BF)
        up = dy[at, :].astype(F32)
        d = norm_back(up, n, inverse, g2)
        low = d.astype(BF)
        dres[at, :] = d
        dbr[at, :] = low
        sums_ref[0:1] += jnp.sum(up * n, axis=0, keepdims=True)
        sums_ref[1:2] += jnp.sum(up, axis=0, keepdims=True)
        sums_ref[2:3] += jnp.sum(low.astype(F32), axis=0, keepdims=True)

    out_copies = store_sequences(core, out, out_mine, out_others, dsem)

    path = is_path(grid, per)
    blocks = size // per
    pending = [[], []]

    def emit(part, side, value):
        slot, there = part % 2, natural_part(part)
        stage[slot, side] = value
        if not path:
            copy = pltpu.make_async_copy(
                stage.at[slot, side],
                keep_hbm.at[span(side * units + there * size, size)],
                osem.at[slot, side, 0],
            )
            copy.start()
            pending[slot].append(copy)
            return
        for b in range(0, blocks, 2):
            for other, ref in ((0, keep_hbm), (1, send_hbm)):
                here = b + (core ^ other)
                block = side * half + there * blocks + here
                _, place = slot_of(grid, me ^ block, core)
                copy = pltpu.make_async_copy(
                    stage.at[slot, side, pl.ds(pl.multiple_of(here * per, per), per)],
                    ref.at[place],
                    osem.at[slot, side, b + other],
                )
                copy.start()
                pending[slot].append(copy)

    for part in range(PARTS):
        there = natural_part(part)
        here = slice(part * size, (part + 1) * size)
        up, down = span(there * size, size), span(units + there * size, size)
        d = (nt(dbr[...], w[down, :]) * gp[:, here].astype(F32)).astype(BF)
        dpre[...] = d
        db1_ref[:, span(there * size, size)] = jnp.sum(d.astype(F32), axis=0, keepdims=True)
        more = nn(d, w[up, :])
        if part == 0:
            acc[...] = more
        else:
            acc[...] += more
        for copy in pending[part % 2]:
            copy.wait()
        pending[part % 2] = []
        emit(part, 0, tn(dpre[...], h[...]).astype(BF))
        emit(part, 1, tn(act[:, here], dbr[...]).astype(BF))

    def stores(r):
        return [
            pltpu.make_async_copy(dres.at[tile(r)], dres_hbm.at[tile(r)], isem.at[1]),
            pltpu.make_async_copy(out.at[tile(r)], datt_hbm.at[tile(r)], isem.at[2]),
        ]

    for copy in out_copies:
        copy.wait()

    @pl.loop(0, tiles)
    def _(r):
        at = tile(r)
        dhid = dres[at, :] + acc[at, :]
        n = normed[at, :]
        d = norm_back(dhid, n, inv_ref[at, :], g1)
        low = d.astype(BF)
        dres[at, :] = d
        out[at, :] = low
        sums_ref[3:4] += jnp.sum(dhid * n, axis=0, keepdims=True)
        sums_ref[4:5] += jnp.sum(dhid, axis=0, keepdims=True)
        sums_ref[5:6] += jnp.sum(low.astype(F32), axis=0, keepdims=True)
        for copy in stores(r):
            copy.start()

    @pl.loop(0, tiles)
    def _(r):
        for copy in stores(r):
            copy.wait()

    for copy in pending[0] + pending[1]:
        copy.wait()


def ffn_call(grid, me, vec, inv, h, normed, dy_mine, dy_others, pieces, per):
    rows, width = h.shape
    total = grid.devices * per
    units = total // 2
    size = units // PARTS
    paths = path_shapes(grid, grid.devices, per, width)
    return pl.pallas_call(
        lambda *r: ffn_kernel(grid, per, *r),
        in_specs=[SMEM, VMEM, VMEM, ANY, ANY, ANY, ANY] + [ANY] * len(pieces),
        out_specs=[ANY, ANY, ANY, ANY, VMEM, VMEM, ANY, ANY],
        out_shape=[
            jax.ShapeDtypeStruct(dy_mine.shape, BF),
            jax.ShapeDtypeStruct((dy_mine.shape[0] // 2,) + dy_mine.shape[1:], BF),
            jax.ShapeDtypeStruct((rows, width), F32),
            jax.ShapeDtypeStruct((rows, width), BF),
            jax.ShapeDtypeStruct((8, width), F32),
            jax.ShapeDtypeStruct((1, units), F32),
        ]
        + paths,
        scratch_shapes=[
            pltpu.VMEM((total, width), BF),
            pltpu.VMEM((rows, width), BF),
            pltpu.VMEM((rows, width), F32),
            pltpu.VMEM((rows, width), BF),
            pltpu.VMEM((rows, units), BF),
            pltpu.VMEM((rows, units), BF),
            pltpu.VMEM((rows, width), F32),
            pltpu.VMEM((rows, width), F32),
            pltpu.VMEM((rows, width), BF),
            pltpu.VMEM((rows, width), BF),
            pltpu.VMEM((rows, size), BF),
            pltpu.VMEM((2, 2, size, width), BF),
            pltpu.SemaphoreType.DMA((grid.devices,)),
            pltpu.SemaphoreType.DMA((3,)),
            pltpu.SemaphoreType.DMA((2, 2, max(size // per, 2))),
            pltpu.SemaphoreType.DMA((dy_mine.shape[0],)),
        ],
        compiler_params=params(),
        cost_estimate=cost(6 * rows * width * units, 40 << 20, 2 * rows * units),
        name="ffn",
    )(me, vec, inv, h, normed, dy_mine, dy_others, *pieces)


def out_back_kernel(grid, me_ref, datt_hbm, ctx_hbm, *rest):
    pieces = rest[:-12]
    dctx_hbm, grad_hbm, _, w, datt, ctx, dctx, grad, sems, isem, osem = rest[-11:]
    first = 3 * grid.devices // 4
    loads = [
        pltpu.make_async_copy(datt_hbm, datt, isem.at[0]),
        pltpu.make_async_copy(ctx_hbm, ctx, isem.at[1]),
    ]
    loads[0].start()
    start_natural(grid, me_ref, pieces, w, sems, first)
    loads[1].start()
    loads[0].wait()
    wait_natural(grid, pieces, w, sems, first, grid.devices - first, first)
    dctx[...] = nn(datt[...], w[...]).astype(BF)
    stores = [
        pltpu.make_async_copy(dctx, dctx_hbm, osem.at[0]),
        pltpu.make_async_copy(grad, grad_hbm, osem.at[1]),
    ]
    stores[0].start()
    loads[1].wait()
    grad[...] = tn(datt[...], ctx[...]).astype(BF)
    stores[1].start()
    for copy in stores:
        copy.wait()


def out_back_call(grid, me, datt, ctx, pieces, carry):
    rows, width = ctx.shape
    return pl.pallas_call(
        lambda *r: out_back_kernel(grid, *r),
        in_specs=[SMEM, ANY, ANY] + [ANY] * (len(pieces) + 1),
        out_specs=[ANY, ANY, ANY],
        out_shape=[
            jax.ShapeDtypeStruct((rows, width), BF),
            jax.ShapeDtypeStruct((width, width), BF),
            jax.ShapeDtypeStruct(carry.shape, carry.dtype),
        ],
        input_output_aliases={3 + len(pieces): 2},
        scratch_shapes=[
            pltpu.VMEM((width, width), BF),
            pltpu.VMEM((rows, width), BF),
            pltpu.VMEM((rows, width), BF),
            pltpu.VMEM((rows, width), BF),
            pltpu.VMEM((width, width), BF),
            pltpu.SemaphoreType.DMA((grid.devices,)),
            pltpu.SemaphoreType.DMA((2,)),
            pltpu.SemaphoreType.DMA((2,)),
        ],
        compiler_params=params(),
        cost_estimate=cost(2 * rows * width * width, 12 << 20),
        name="out_back",
    )(me, datt, ctx, *pieces, carry)


def attend_back_kernel(seq, len_ref, q_ref, k_ref, v_ref, d_ref, lse_ref, *rest):
    dz_ref, db_ref, _ = rest[-3:]
    live_len = len_ref[seq]
    length, pair = q_ref.shape
    half = pair // 2
    q, k, v, d = q_ref[...], k_ref[...], v_ref[...], d_ref[...]
    lane = lax.broadcasted_iota(jnp.int32, (length, pair), 1)
    live = lax.broadcasted_iota(jnp.int32, (length, 1), 0) < live_len
    zero = jnp.zeros_like(q)
    dq = dk = dv = None
    for h in (0, 1):
        mine = (lane >= half) if h else (lane < half)
        qh, kh, dh = (jnp.where(mine, t, zero) for t in (q, k, d))
        s = nt(k, qh)
        p = jnp.where(live, jnp.exp(s - lse_ref[0, h : h + 1, :]), 0.0)
        dp = nt(v, dh)
        inner = jnp.sum(p * dp, axis=0, keepdims=True)
        ds = (p * (dp - inner)).astype(BF)
        a = nn(p.astype(BF), dh)
        b = nn(ds, qh)
        c = tn(ds, kh)
        dv = a if dv is None else dv + a
        dk = b if dk is None else dk + b
        dq = c if dq is None else dq + c
    scale = half ** -0.5
    dq = (dq.astype(BF).astype(F32) * scale).astype(BF)
    dv = dv.astype(BF)
    dz_ref[0] = dq
    dz_ref[1] = dk.astype(BF)
    dz_ref[2] = dv
    db_ref[0:1] = jnp.sum(dq.astype(F32), axis=0, keepdims=True)
    db_ref[1:2] = jnp.sum(dv.astype(F32), axis=0, keepdims=True)


def attend_back_call(lens, qkv, dctx, lse, seqs, seq, dz, carry, deps):
    rows, width = dctx.shape
    length = rows // seqs
    pairs = H // 2
    pw = width // pairs
    at = lambda part: pl.BlockSpec((length, pw), lambda p: (seq, part * pairs + p))
    more = [carry] + ([] if dz is None else [dz]) + list(deps)
    return pl.pallas_call(
        lambda *r: attend_back_kernel(seq, *r),
        grid=(pairs,),
        in_specs=[
            SMEM,
            at(0),
            at(1),
            at(2),
            at(0),
            pl.BlockSpec((1, 2, length), lambda p: (seq * pairs + p, 0, 0)),
        ]
        + [ANY] * len(more),
        out_specs=[
            pl.BlockSpec((3, length, pw), lambda p: (0, seq, p)),
            pl.BlockSpec((2, pw), lambda p: (0, p)),
            ANY,
        ],
        out_shape=[
            jax.ShapeDtypeStruct((3, rows, width), BF),
            jax.ShapeDtypeStruct((2, width), F32),
            jax.ShapeDtypeStruct(carry.shape, carry.dtype),
        ],
        input_output_aliases={6: 2} if dz is None else {6: 2, 7: 0},
        compiler_params=params(),
        cost_estimate=cost(
            20 * H * length * length * (width // H), 6 << 20, H * length * length
        ),
        name="attend_back",
    )(lens, qkv, qkv, qkv, dctx, lse, *more)


def attn_grad_kernel(
    grid, per, npieces, me_ref, sums, db1, db_a, db_b, dz_hbm, x_hbm, gout_hbm, dres_hbm, *rest
):
    pieces = rest[:npieces]
    (keep_hbm, send_hbm, mine, others, stage, dz, x, gout, line, total, w) = rest[-15:-4]
    isem, osem, wsem, dsem = rest[-4:]
    rows, width = x.shape
    me = me_ref[0]
    core = me & 1
    blocks = grid.devices // 4
    path = is_path(grid, per)
    loads = [pltpu.make_async_copy(gout_hbm, gout, isem.at[4])]
    loads += [pltpu.make_async_copy(x_hbm, x, isem.at[3])]
    loads += [pltpu.make_async_copy(dz_hbm.at[p], dz.at[p], isem.at[p]) for p in range(3)]
    for copy in loads:
        copy.start()
    load_total = pltpu.make_async_copy(dres_hbm, total, isem.at[5])
    load_total.start()
    start_natural(grid, me_ref, pieces, w, wsem, 0, 3 * blocks)

    db = db_a[...] + db_b[...]
    tail = 3 * width + FF
    line[:, 0:width] = db[0:1]
    line[:, width : 2 * width] = db[1:2]
    line[:, 2 * width : 3 * width] = sums[5:6]
    line[:, 3 * width : tail] = db1[...]
    for i, row in enumerate((2, 3, 4, 0, 1)):
        line[:, tail + i * width : tail + (i + 1) * width] = sums[row : row + 1]
    count = line.shape[1] // grid.devices
    blank = jnp.zeros((8, width), F32)
    first_row = lax.broadcasted_iota(jnp.int32, (8, count), 0) == 0
    for d in range(grid.devices):
        values = jnp.where(first_row, line[:, d * count : (d + 1) * count], 0.0)
        values = jnp.concatenate([values, blank[:, count:]], axis=1).astype(BF)
        if path:
            stage[d, per : per + 8] = values
        else:
            send_hbm[d] = values

    copies = []

    def emit(part, value):
        value = value.astype(BF)
        if not path:
            keep_hbm[part * width : (part + 1) * width, :] = value
            return
        stage[part * blocks : (part + 1) * blocks, 0:per] = value.reshape(blocks, per, width)
        for b in range(0, blocks, 2):
            for other, ref in ((0, keep_hbm), (1, send_hbm)):
                block = part * blocks + b + (core ^ other)
                _, place = slot_of(grid, me ^ block, core)
                copy = pltpu.make_async_copy(stage.at[block], ref.at[place], osem.at[block])
                copy.start()
                copies.append(copy)

    loads[0].wait()
    emit(3, gout[...])
    loads[1].wait()
    for part in range(3):
        loads[2 + part].wait()
        emit(part, tn(dz[part], x[...]))
    load_total.wait()
    for part in range(3):
        wait_natural(grid, pieces, w, wsem, part * blocks, blocks, 0, 3 * blocks)
        total[...] += nn(dz[part], w[part * width : (part + 1) * width, :])
    for copy in store_sequences(core, total, mine, others, dsem) + copies:
        copy.wait()


def attn_grad_call(grid, me, dz, x, gout, dres, vectors, pieces, per, shape, deps):
    rows, width = x.shape
    paths = path_shapes(grid, grid.devices, per, width)
    path = is_path(grid, per)
    if path:
        paths = [jax.ShapeDtypeStruct((p.shape[0], per + 8, width), BF) for p in paths]
    return pl.pallas_call(
        lambda *r: attn_grad_kernel(grid, per, len(pieces), *r),
        in_specs=[SMEM] + [VMEM] * len(vectors) + [ANY] * (4 + len(pieces) + len(deps)),
        out_specs=[ANY if path else VMEM] * 2 + [ANY, ANY],
        out_shape=paths
        + [
            jax.ShapeDtypeStruct(shape, F32),
            jax.ShapeDtypeStruct((shape[0] // 2,) + shape[1:], F32),
        ],
        scratch_shapes=[
            pltpu.VMEM((grid.devices, per + 8, width), BF),
            pltpu.VMEM((3, rows, width), BF),
            pltpu.VMEM((rows, width), BF),
            pltpu.VMEM((width, width), BF),
            pltpu.VMEM((1, 8 * width + FF), F32),
            pltpu.VMEM((rows, width), F32),
            pltpu.VMEM((3 * width, width), BF),
            pltpu.SemaphoreType.DMA((6,)),
            pltpu.SemaphoreType.DMA((grid.devices,)),
            pltpu.SemaphoreType.DMA((grid.devices,)),
            pltpu.SemaphoreType.DMA((shape[0],)),
        ],
        compiler_params=params(),
        cost_estimate=cost(6 * rows * width * width, 28 << 20),
        name="attn_grad",
    )(me, *vectors, dz, x, gout, dres, *pieces, *deps)


def gate(value, deps):
    return pl.pallas_call(
        lambda *r: None,
        in_specs=[ANY] * (1 + len(deps)),
        out_specs=ANY,
        out_shape=jax.ShapeDtypeStruct(value.shape, value.dtype),
        input_output_aliases={0: 0},
        compiler_params=params(),
        cost_estimate=cost(0, 0),
        name="gate",
    )(value, *deps)


def ordered_stack_kernel(count, *rest):
    for i in range(count):
        rest[-1][i] = rest[i][...]


def ordered_stack(parts, deps):
    return pl.pallas_call(
        lambda *r: ordered_stack_kernel(len(parts), *r),
        in_specs=[VMEM] * len(parts) + [ANY] * len(deps),
        out_specs=VMEM,
        out_shape=jax.ShapeDtypeStruct((len(parts),) + parts[0].shape, parts[0].dtype),
        compiler_params=params(),
        name="ordered_stack",
    )(*parts, *deps)


def adam_update(master, moment, second, grad, rate):
    moment_new = decay_rate * moment + (1.0 - decay_rate) * grad
    second_new = decay_rate * second + (1.0 - decay_rate) * grad * grad
    correction = 1.0 - decay_rate**STEP
    direction = moment_new / correction / (jnp.sqrt(second_new / correction) + adam_epsilon)
    master_new = master - rate * (direction + weight_decay * master)
    return (moment_new, second_new, master_new)


def join_sequences(mine, others, core):
    count = others.shape[0]
    return lax.dynamic_update_slice(mine, others, ((1 - core) * count, 0, 0))


def local(
    tokens,
    cotangent,
    seq_lengths,
    slot_order,
    attn_weights,
    attn_moment,
    attn_second,
    ffn_weights,
    ffn_moment,
    ffn_second,
    vectors,
    vector_moment,
    vector_second,
):
    grid = Grid(lax.axis_size("dp"))
    core = lax.axis_index("seq")
    shard_index = lax.axis_index(AXES)
    me = shard_index.astype(jnp.int32).reshape(1)
    seq_count, half_len, width = tokens.shape
    seqs = seq_count // 2
    length = 2 * half_len
    rows = seqs * length
    per, ffn_per = attn_weights.shape[1], ffn_weights.shape[1]
    vec_per = vectors.shape[0]
    path = is_path(grid, per) and is_path(grid, ffn_per)

    slot_pick = (slot_order[0][:, None] == jnp.arange(seq_count)[None, :]).astype(jnp.int32)
    slot_len = jnp.sum(slot_pick * seq_lengths[0][None, :], axis=1)
    lens = lax.dynamic_slice_in_dim(slot_len, core * seqs, seqs, 0)

    vec_rows = jnp.zeros((8, width), BF)
    vec_rows = lax.dynamic_update_slice(vec_rows, vectors.astype(BF)[None, :], (0, 0))
    attn_block = jnp.concatenate([attn_weights.astype(BF).T, vec_rows])

    other_core = lambda value: permute(value, grid, lambda c: 1)
    tokens_other = other_core(tokens)
    if path:
        attn_parts = gather_z(grid, attn_block)
        ffn_block = ffn_weights.astype(BF).T
        ffn_parts = gather_z(grid, ffn_block)
        attn_z = ordered_stack(attn_parts, [ffn_block])
        attn_two = gather_two(grid, attn_z)
        attn_two = attn_two[:1] + [gate(t, ffn_parts[1:2]) for t in attn_two[1:]]
        attn_three = gather_three(grid, attn_two)
        ffn_z = ordered_stack(ffn_parts, attn_two[1:])
        ffn_two = gather_two(grid, ffn_z)
        weights = with_core(grid, attn_two + attn_three, [ffn_z])
        vec = natural_vectors(grid, weights, core, me[0], per, vec_per)
    else:
        whole_rows = lambda block: [lax.all_gather(block, AXES, axis=0, tiled=True)]
        weights = whole_rows(attn_block[:per])
        ffn_pieces = whole_rows(ffn_weights.astype(BF).T)
        ffn_two = []
        vec = lax.all_gather(attn_block[per:], AXES)[:, 0, :vec_per].reshape(1, -1).astype(F32)
    dy_other = other_core(cotangent)

    qkv, x = qkv_call(grid, me, vec, tokens, tokens_other, weights)
    fwd = attend_call(grid, me, lens, qkv, x, vec, weights, seqs, 0, [], [])
    ffn_two = ffn_two[:1] + [gate(t, fwd[:1]) for t in ffn_two[1:]]
    fwd = attend_call(grid, me, lens, qkv, x, vec, weights, seqs, 1, fwd, ffn_two[1:])
    ctx, lse, normed, inv, hidden = fwd
    if path:
        ffn_three = gather_three(grid, ffn_two)
        ffn_three = ffn_three[:1] + [gate(t, fwd[:1]) for t in ffn_three[1:]]
        ffn_pieces = with_core(grid, ffn_two + ffn_three, [])
    out, out_other, dres_one, datt, sums, db1, keep_f, send_f = ffn_call(
        grid, me, vec, inv, hidden, normed, cotangent, dy_other, ffn_pieces, ffn_per
    )
    layer_out = join_sequences(out, other_core(out_other), core)

    sums_f = Sums(grid, path, keep_f, send_f)
    dctx, gout, sums_f.keep = out_back_call(grid, me, datt, ctx, weights, sums_f.keep)
    sends = sums_f.add_core()
    dz, db_a, sums_f.keep = attend_back_call(
        lens, qkv, dctx, lse, seqs, 0, None, sums_f.keep, sends
    )
    sends = sums_f.add_three()
    dz, db_b, sums_f.keep = attend_back_call(
        lens, qkv, dctx, lse, seqs, 1, dz, sums_f.keep, sends
    )
    sends = sums_f.add_two()
    keep_c, send_c, dx, dx_other = attn_grad_call(
        grid, me, dz, x, gout, dres_one, [sums, db1, db_a, db_b], weights, per, tokens.shape, sends
    )
    if path:
        send_c = gate(send_c, sums_f.z[1:2])
    sums_c = Sums(grid, path, keep_c, send_c)
    sums_c.add_core()
    ffn_sum = sums_f.add_z()
    sums_c.add_three()
    sums_c.keep = gate(sums_c.keep, [ffn_sum])
    input_grad = join_sequences(dx, other_core(dx_other), core)
    sums_c.add_two()
    attn_sum = sums_c.add_z()

    vector_sum = attn_sum[per, :vec_per]
    attn_sum = attn_sum[:per].T
    ffn_sum = ffn_sum[:ffn_per].T

    attn_cols = shard_index * per + jnp.arange(per)
    attn_rate = jnp.where(
        attn_cols < 2 * width, math.sqrt(2.0), jnp.where(attn_cols < 3 * width, 1.5, 1.8)
    ) * width ** (-0.5)
    ffn_cols = shard_index * ffn_per + jnp.arange(ffn_per)
    ffn_rate = jnp.where(ffn_cols < FF, width ** (-0.5), 1.5 * FF ** (-0.5))
    attn_m, attn_v, attn_new = adam_update(
        attn_weights, attn_moment, attn_second, attn_sum, attn_rate[None, :]
    )
    ffn_m, ffn_v, ffn_new = adam_update(
        ffn_weights, ffn_moment, ffn_second, ffn_sum, ffn_rate[None, :]
    )
    vec_m, vec_v, vec_new = adam_update(
        vectors, vector_moment, vector_second, vector_sum, vector_rate
    )
    return (
        layer_out,
        input_grad,
        attn_m,
        attn_v,
        attn_new,
        attn_new.astype(BF),
        ffn_m,
        ffn_v,
        ffn_new,
        ffn_new.astype(BF),
        vec_m,
        vec_v,
        vec_new,
        vec_new.astype(BF),
    )


def solution(mesh):
    columns = P(None, AXES)
    flat = P(AXES)
    rows = P("dp", "seq", None)
    placed = (rows, rows, P("dp", None), P("dp", None)) + (columns,) * 6 + (flat,) * 3
    return jax.shard_map(
        local,
        mesh=mesh,
        in_specs=placed,
        out_specs=(rows, rows) + (columns,) * 8 + (flat,) * 4,
        check_vma=False,
    )
```

```python
import math

import jax
import jax.numpy as jnp
from jax import lax
from jax.experimental import pallas as pl
from jax.experimental.pallas import tpu as pltpu
from jax.sharding import PartitionSpec as P

H = 12
FF = 3072
STEP = 5

epsilon = 1e-06
masked_score = -1e30
decay_rate = 0.5
adam_epsilon = 1e-08
weight_decay = 0.01
vector_rate = 0.5

AXES = ("dp", "seq")
BF = jnp.bfloat16
F32 = jnp.float32
VMEM_LIMIT = 56 * 1024 * 1024
TILE = 256
COST = 16
ANY = pl.BlockSpec(memory_space=pl.ANY)
SMEM = pl.BlockSpec(memory_space=pltpu.SMEM)
VMEM = pl.BlockSpec(memory_space=pltpu.VMEM)


def nn(a, b):
    return lax.dot_general(a, b, (((1,), (0,)), ((), ())), preferred_element_type=F32)


def nt(a, b):
    return lax.dot_general(a, b, (((1,), (1,)), ((), ())), preferred_element_type=F32)


def tn(a, b):
    return lax.dot_general(a, b, (((0,), (0,)), ((), ())), preferred_element_type=F32)


class Grid:
    def __init__(self, chips):
        power = chips.bit_length() - 1
        if 1 << power == chips:
            self.side = 1 << (power // 3)
            self.nz = chips // (self.side * self.side)
        else:
            self.side, self.nz = 1, chips
        self.devices = 2 * chips
        self.xor = 1 << power == chips

    def z_mask(self, m):
        return m * 2 * self.side * self.side

    def x_mask(self, m):
        return 2 * m

    def y_mask(self, m):
        return 2 * m * self.side

    def label(self, core, other, i3, i2, iz):
        x = jnp.where(core == 0, i2, i3)
        y = jnp.where(core == 0, i3, i2)
        return self.z_mask(iz) + self.y_mask(y) + self.x_mask(x) + other


def permute(value, grid, mask_of_core):
    pairs = [(i, i ^ mask_of_core(i & 1)) for i in range(grid.devices)]
    return lax.ppermute(value, AXES, pairs)


def along_two(grid, value, m):
    return permute(value, grid, lambda c: grid.x_mask(m) if c == 0 else grid.y_mask(m))


def along_three(grid, value, m):
    return permute(value, grid, lambda c: grid.y_mask(m) if c == 0 else grid.x_mask(m))


def gather_z(grid, block):
    return [block] + [permute(block, grid, lambda c: grid.z_mask(m)) for m in range(1, grid.nz)]


def gather_two(grid, zed):
    return [zed] + [along_two(grid, zed, m) for m in range(1, grid.side)]


def gather_three(grid, two):
    return [along_three(grid, t, m) for m in range(1, grid.side) for t in two]


def with_core(grid, own, deps):
    own = [gate(own[0], deps) if deps else own[0]] + own[1:]
    return own + [permute(p, grid, lambda c: 1) for p in own]


def is_path(grid, rows):
    return grid.side == 2 and grid.nz == 4 and rows % 16 == 0


def slot_of(grid, label, core):
    other = label & 1
    x = (label // 2) & (grid.side - 1)
    y = (label // (2 * grid.side)) & (grid.side - 1)
    z = label // (2 * grid.side * grid.side)
    first = (core ^ other) == 0
    i2 = jnp.where(first, x, y)
    i3 = jnp.where(first, y, x)
    return other, (i3 * grid.side + i2) * grid.nz + z


def natural_vectors(grid, pieces, core, me, row, count):
    side, nz = grid.side, grid.nz
    table = jnp.stack([p[:, row, :count] for p in pieces]).reshape(2, side, side, nz, count)
    turned = jnp.swapaxes(table, 1, 2)
    first = jnp.stack([table[0], turned[1]])
    second = jnp.stack([turned[0], table[1]])
    value = jnp.where(core == 0, first, second)
    value = jnp.transpose(value, (3, 1, 2, 0, 4)).reshape(grid.devices, count)
    bit = 1
    while bit < grid.devices:
        pairs = value.reshape(-1, 2, bit, count)
        value = jnp.where((me & bit) == 0, pairs, pairs[:, ::-1]).reshape(grid.devices, count)
        bit *= 2
    return value.reshape(1, -1).astype(F32)


def start_natural(grid, me_ref, pieces, dest, sems, first=0, last=None, order=None):
    last = grid.devices if last is None else last
    rows = dest.shape[0] // (last - first)
    if len(pieces) == 1:
        pltpu.make_async_copy(
            pieces[0].at[pl.ds(first * rows, (last - first) * rows)], dest, sems.at[0]
        ).start()
        return
    me = me_ref[0]
    core = me & 1
    side, nz = grid.side, grid.nz
    for label in sorted(range(grid.devices), key=order or (lambda j: j // (2 * side * side))):
        other, x, y = label & 1, label // 2 % side, label // (2 * side) % side
        iz = label // (2 * side * side)
        block = me ^ label

        def start(ref, block=block, iz=iz):
            row = pl.multiple_of((block - first) * rows, rows)
            pltpu.make_async_copy(
                ref.at[iz, pl.ds(0, rows)], dest.at[pl.ds(row, rows)], sems.at[block]
            ).start()

        def either(other=other, x=x, y=y, start=start):
            one = pieces[(other * side + y) * side + x]
            two = pieces[(other * side + x) * side + y]
            if x == y:
                start(one)
            else:
                pl.when((core ^ other) == 0)(lambda: start(one))
                pl.when((core ^ other) != 0)(lambda: start(two))

        if last - first == grid.devices:
            either()
        else:
            pl.when((block >= first) & (block < last))(either)


def wait_natural(grid, pieces, dest, sems, begin, count, first=0, last=None):
    last = grid.devices if last is None else last
    rows = dest.shape[0] // (last - first)
    if len(pieces) == 1:

        @pl.when(begin == first)
        def _():
            pltpu.make_async_copy(
                pieces[0].at[pl.ds(first * rows, (last - first) * rows)], dest, sems.at[0]
            ).wait()

        return
    for i in range(count):
        block = begin + i
        pltpu.make_async_copy(
            pieces[0].at[0, pl.ds(0, rows)],
            dest.at[pl.ds(pl.multiple_of((block - first) * rows, rows), rows)],
            sems.at[block],
        ).wait()


def path_shapes(grid, blocks, per, width):
    if not is_path(grid, per):
        return [
            jax.ShapeDtypeStruct((blocks * per, width), BF),
            jax.ShapeDtypeStruct((blocks, 8, width), BF),
        ]
    return [jax.ShapeDtypeStruct((grid.nz, per, width), BF)] * 8


def start_store(core, src, dests, x, y, other, iz, sem):
    one, two = (dests[4 * other + k].at[iz] for k in (2 * y + x, 2 * x + y))
    copy = pltpu.make_async_copy(src, one, sem)
    if x == y:
        copy.start()
    else:
        pl.when((core ^ other) == 0)(lambda: copy.start())
        pl.when((core ^ other) != 0)(lambda: pltpu.make_async_copy(src, two, sem).start())
    return copy


class Sums:
    def __init__(self, grid, path, blocks):
        self.grid, self.path = grid, path
        self.three, self.two, self.z = [], [], []
        if path:
            self.keep = list(blocks[:4])
            got = {k: permute(blocks[4 + k], grid, lambda c: 1) for k in (3, 2, 1, 0)}
            self.core = [got[k] for k in range(4)]
        else:
            self.keep = list(blocks)

    def terms(self, i3, i2, iz):
        grid = self.grid
        at = i3 * grid.side + i2
        total = self.keep[at][iz].astype(F32) + self.core[at][iz].astype(F32)
        if i3 == 0:
            for there, got in self.three:
                if there == i2:
                    total = total + got[iz].astype(F32)
            if i2 == 0:
                for got in self.two:
                    total = total + got[iz].astype(F32)
        return total

    def add_core(self):
        if not self.path:
            return []
        grid = self.grid
        every = slice(0, grid.nz)
        sends = [
            (i2, m, self.terms(m, i2, every).astype(BF))
            for i2 in reversed(range(grid.side))
            for m in range(1, grid.side)
        ]
        self.three = [(i2, along_three(grid, value, m)) for i2, m, value in sends]
        return [value for _, _, value in sends]

    def add_three(self):
        if not self.path:
            return []
        grid = self.grid
        every = slice(0, grid.nz)
        sends = [self.terms(0, m, every).astype(BF) for m in range(1, grid.side)]
        self.two = [along_two(grid, sends[m - 1], m) for m in range(1, grid.side)]
        return sends

    def add_two(self):
        if not self.path:
            return []
        grid = self.grid
        sends = [self.terms(0, 0, slice(m, m + 1))[0].astype(BF) for m in range(1, grid.nz)]
        self.z = [
            permute(sends[m - 1], grid, lambda c: grid.z_mask(m)) for m in range(1, grid.nz)
        ]
        return sends

    def add_z(self):
        if not self.path:
            rows = [v.reshape(-1, v.shape[-1]).astype(F32) for v in self.keep]
            return jnp.concatenate(
                [lax.psum_scatter(v, AXES, scatter_dimension=0, tiled=True) for v in rows]
            )
        total = self.terms(0, 0, slice(0, 1))[0]
        for got in self.z:
            total = total + got.astype(F32)
        return total


def params(**more):
    return pltpu.CompilerParams(vmem_limit_bytes=VMEM_LIMIT, **more)


def cost(macs, bytes_accessed, trans=0):
    return pl.CostEstimate(
        flops=2 * macs // COST, bytes_accessed=bytes_accessed // COST, transcendentals=trans // COST
    )


def rows_spec(width, tile=TILE):
    return pl.BlockSpec((tile, width), lambda i: (i, 0))


def whole(shape):
    zeros = (0,) * len(shape)
    return pl.BlockSpec(shape, lambda *i: zeros)


def fixed(*shape):
    zeros = (0,) * len(shape)
    return pl.BlockSpec(shape, lambda i: zeros)


def norm_rows(values):
    center = values - jnp.mean(values, axis=-1, keepdims=True)
    inverse = lax.rsqrt(jnp.mean(center * center, axis=-1, keepdims=True) + epsilon)
    return center * inverse, inverse


def norm_back(upstream, normed, inverse, gain):
    u = upstream * gain
    centered = u - jnp.mean(u, axis=-1, keepdims=True)
    return inverse * (centered - normed * jnp.mean(u * normed, axis=-1, keepdims=True))


def gelu_pair(u):
    phi = 0.5 + 0.5 * lax.erf(u * math.sqrt(0.5))
    density = jnp.exp(-0.5 * (u * u))
    return u * phi, phi + (u * (1.0 / math.sqrt(2.0 * math.pi))) * density


def load_sequences(core, mine, others, dest, sems):
    count = mine.shape[0] // 2
    half = mine.shape[1]
    copies = []
    for s in range(count):
        seq = core * count + s
        for i, src in enumerate((mine, others)):
            at = s * 2 * half + (core ^ i) * half
            copies.append(
                pltpu.make_async_copy(
                    src.at[seq], dest.at[pl.ds(pl.multiple_of(at, half), half)], sems.at[2 * s + i]
                )
            )
    for copy in copies:
        copy.start()
    return copies


def store_sequences(core, src, mine, others, sems):
    count, half = others.shape[0], others.shape[1]
    copies = []
    for s in range(count):
        for i, dest in enumerate((mine.at[core * count + s], others.at[s])):
            at = s * 2 * half + (core ^ i) * half
            copies.append(
                pltpu.make_async_copy(
                    src.at[pl.ds(pl.multiple_of(at, half), half)], dest, sems.at[2 * s + i]
                )
            )
    for copy in copies:
        copy.start()
    return copies


def quarter_order(grid, me_ref, pieces, i):
    if len(pieces) == 1:
        return i
    lines = grid.nz // 4
    return (i * lines ^ me_ref[0] // (2 * grid.side * grid.side)) // lines


def qkv_kernel(grid, me_ref, vec_ref, mine, others, *rest):
    pieces, (out_hbm, x_hbm, w, x, out, wsem, xsem, osem) = rest[:-8], rest[-8:]
    rows, width = x.shape
    core = me_ref[0] & 1
    loads = load_sequences(core, mine, others, x, xsem)
    blocks = grid.devices // 4
    start_natural(grid, me_ref, pieces, w, wsem, 0, 3 * blocks)
    for copy in loads:
        copy.wait()
    copy_x = pltpu.make_async_copy(x, x_hbm, osem.at[3])
    copy_x.start()

    def store(part):
        cols = pl.ds(pl.multiple_of(part * width, width), width)
        return pltpu.make_async_copy(out.at[:, cols], out_hbm.at[:, cols], osem.at[part])

    @pl.loop(0, 4)
    def _(i):
        part = quarter_order(grid, me_ref, pieces, i)

        @pl.when(part < 3)
        def _():
            wait_natural(grid, pieces, w, wsem, part * blocks, blocks, 0, 3 * blocks)
            cols = pl.ds(pl.multiple_of(part * width, width), width)
            bias = vec_ref[:, pl.ds(pl.multiple_of(part // 2 * width, width), width)]
            bias = jnp.where(part == 1, 0.0, bias)
            scale = jnp.where(part == 0, (width // H) ** -0.5, 1.0)
            out[:, cols] = ((nt(x[...], w[cols, :]) + bias) * scale).astype(BF)
            store(part).start()

    for part in range(3):
        store(part).wait()
    copy_x.wait()


def qkv_call(grid, me, vec, mine, others, pieces):
    width = mine.shape[2]
    rows = mine.shape[0] * mine.shape[1]
    return pl.pallas_call(
        lambda *r: qkv_kernel(grid, *r),
        in_specs=[SMEM, VMEM, ANY, ANY] + [ANY] * len(pieces),
        out_specs=[ANY, ANY],
        out_shape=[
            jax.ShapeDtypeStruct((rows, 3 * width), BF),
            jax.ShapeDtypeStruct((rows, width), BF),
        ],
        scratch_shapes=[
            pltpu.VMEM((3 * width, width), BF),
            pltpu.VMEM((rows, width), BF),
            pltpu.VMEM((rows, 3 * width), BF),
            pltpu.SemaphoreType.DMA((grid.devices,)),
            pltpu.SemaphoreType.DMA((mine.shape[0],)),
            pltpu.SemaphoreType.DMA((4,)),
        ],
        compiler_params=params(),
        cost_estimate=cost(rows * width * 3 * width, 12 << 20),
        name="qkv",
    )(me, vec, mine, others, *pieces)


def vector_refs(vec_ref, width):
    tail = 3 * width + FF
    found = [vec_ref[:, 2 * width : 3 * width], vec_ref[:, 3 * width : tail]]
    return found + [vec_ref[:, tail + i * width : tail + (i + 1) * width] for i in range(5)]


def attend_kernel(grid, npieces, seq, len_ref, me_ref, q_ref, k_ref, v_ref, x_ref, vec_ref, *rest):
    pieces = rest[:npieces]
    quarter = grid.devices // 4
    ctx_ref, lse_ref, normed_ref, inv_ref, hid_ref, w, sems = rest[-7:]
    turn = pl.program_id(0)

    @pl.when(turn == 0)
    def _():
        start_natural(grid, me_ref, pieces, w, sems, 3 * quarter)

    live_len = len_ref[seq]
    length, pair = q_ref.shape
    half = pair // 2
    q, k, v = q_ref[...], k_ref[...], v_ref[...]
    lane = lax.broadcasted_iota(jnp.int32, (length, pair), 1)
    live = lax.broadcasted_iota(jnp.int32, (1, length), 1) < live_len
    outs, stats = [], []
    for h in (0, 1):
        mine = (lane >= half) if h else (lane < half)
        s = nt(jnp.where(mine, q, jnp.zeros_like(q)), k)
        s = jnp.where(live, s, masked_score)
        top = jnp.max(s, axis=-1, keepdims=True)
        p = jnp.exp(s - top)
        total = jnp.sum(p, axis=-1, keepdims=True)
        outs.append(nn(p.astype(BF), v) / total)
        stats.append(top + jnp.log(total))
    ctx = jnp.where(lane < half, outs[0], outs[1]).astype(BF)
    ctx_ref[:, pl.ds(pl.multiple_of(turn * pair, pair), pair)] = ctx
    turned = jnp.where(lane < half, stats[0], stats[1]).T
    lse_ref[0] = jnp.concatenate([turned[0:1], turned[half : half + 1]], axis=0)

    @pl.when(turn == pl.num_programs(0) - 1)
    def _():
        wait_natural(grid, pieces, w, sems, 3 * quarter, quarter, 3 * quarter)
        bo, _, _, g1, e1, _, _ = vector_refs(vec_ref, x_ref.shape[1])
        r = x_ref[...].astype(F32) + (nt(ctx_ref[...], w[...]) + bo)
        normed, inverse = norm_rows(r)
        normed_ref[...] = normed
        inv_ref[...] = inverse
        hid_ref[...] = (normed * g1 + e1).astype(BF)


def attend_call(grid, me, lens, qkv, x, vec, pieces, seqs, seq, before, deps):
    rows, width = x.shape
    length = rows // seqs
    pairs = H // 2
    pw = width // pairs
    at = lambda part: pl.BlockSpec((length, pw), lambda p: (seq, part * pairs + p))
    seq_rows = lambda w: pl.BlockSpec((length, w), lambda p: (seq, 0))
    first = 7 + len(pieces)
    return pl.pallas_call(
        lambda *r: attend_kernel(grid, len(pieces), seq, *r),
        grid=(pairs,),
        in_specs=[SMEM, SMEM, at(0), at(1), at(2), seq_rows(width), whole(vec.shape)]
        + [ANY] * (len(pieces) + len(before) + len(deps)),
        out_specs=[
            seq_rows(width),
            pl.BlockSpec((1, 2, length), lambda p: (seq * pairs + p, 0, 0)),
            seq_rows(width),
            seq_rows(1),
            seq_rows(width),
        ],
        out_shape=[
            jax.ShapeDtypeStruct((rows, width), BF),
            jax.ShapeDtypeStruct((seqs * pairs, 2, length), F32),
            jax.ShapeDtypeStruct((rows, width), F32),
            jax.ShapeDtypeStruct((rows, 1), F32),
            jax.ShapeDtypeStruct((rows, width), BF),
        ],
        scratch_shapes=[
            pltpu.VMEM((width, width), BF),
            pltpu.SemaphoreType.DMA((grid.devices,)),
        ],
        input_output_aliases={first + i: i for i in range(len(before))},
        compiler_params=params(),
        cost_estimate=cost(8 * H * length * length * (width // H), 9 << 20, H * length * length),
        name="attend",
    )(lens, me, qkv, qkv, qkv, x, vec, *pieces, *before, *deps)


PARTS = 4


def ffn_kernel(grid, per, me_ref, vec_ref, inv_ref, h_hbm, normed_hbm, dy_mine, dy_others, *rest):
    npieces = len(rest) - 22 - (8 if is_path(grid, per) else 2)
    pieces = rest[:npieces]
    out_mine, out_others, dres_hbm, datt_hbm, sums_ref, db1_ref = rest[npieces : npieces + 6]
    grads = rest[npieces + 6 : -16]
    (w, h, normed, dy, act, gp, acc, dres, dbr, out, dpre, stage, wsem, isem, osem, dsem) = rest[-16:]
    rows, width = h.shape
    units = w.shape[0] // 2
    size = units // PARTS
    tiles = rows // TILE
    me = me_ref[0]
    core = me & 1

    _, _, b2, g1, e1, g2, e2 = vector_refs(vec_ref, width)
    loads = [
        pltpu.make_async_copy(src, dst, isem.at[i])
        for i, (src, dst) in enumerate(((h_hbm, h), (normed_hbm, normed)))
    ]
    loads[0].start()
    half = grid.devices // 2
    start_natural(grid, me_ref, pieces, w, wsem, order=lambda j: (j % half // (half // PARTS), j))
    loads[1].start()
    loads += load_sequences(core, dy_mine, dy_others, dy, dsem)
    loads[0].wait()

    def tile(r):
        return pl.ds(pl.multiple_of(r * TILE, TILE), TILE)

    def natural_part(part):
        if len(pieces) == 1:
            return part
        return part ^ (me % half // (half // PARTS))

    def span(start, count):
        return pl.ds(pl.multiple_of(start, count), count)

    for part in range(PARTS):
        there = natural_part(part)
        for base in (0, half):
            wait_natural(
                grid, pieces, w, wsem, base + there * (half // PARTS), half // PARTS
            )
        here = slice(part * size, (part + 1) * size)
        up, down = span(there * size, size), span(units + there * size, size)
        a, slope = gelu_pair(nt(h[...], w[up, :]) + vec_ref[:, span(3 * width + there * size, size)])
        a = a.astype(BF)
        act[:, here] = a
        gp[:, here] = slope.astype(BF)
        more = nn(a, w[down, :])
        if part == 0:
            acc[...] = more
        else:
            acc[...] += more

    for copy in loads[1:]:
        copy.wait()
    sums_ref[...] = jnp.zeros_like(sums_ref)

    @pl.loop(0, tiles)
    def _(r):
        at = tile(r)
        hidden = normed[at, :] * g1 + e1
        value = hidden + (acc[at, :] + b2)
        n, inverse = norm_rows(value)
        out[at, :] = (n * g2 + e2).astype(BF)
        up = dy[at, :].astype(F32)
        d = norm_back(up, n, inverse, g2)
        low = d.astype(BF)
        dres[at, :] = d
        dbr[at, :] = low
        sums_ref[0:1] += jnp.sum(up * n, axis=0, keepdims=True)
        sums_ref[1:2] += jnp.sum(up, axis=0, keepdims=True)
        sums_ref[2:3] += jnp.sum(low.astype(F32), axis=0, keepdims=True)

    out_copies = store_sequences(core, out, out_mine, out_others, dsem)

    path = is_path(grid, per)
    blocks = size // per
    pending = [[], []]

    def emit(part, side, value):
        slot, there = part % 2, natural_part(part)
        stage[slot, side] = value
        if not path:
            copy = pltpu.make_async_copy(
                stage.at[slot, side],
                grads[0].at[span(side * units + there * size, size)],
                osem.at[slot, side, 0],
            )
            copy.start()
            pending[slot].append(copy)
            return
        spread = 2 * grid.side * grid.side
        iz = (side * half ^ me & half) // spread + part // 2
        for x in (0, 1):
            for other in (0, 1):
                label = 2 * x + other
                here = label ^ (me & 3)
                src = stage.at[slot, side, pl.ds(pl.multiple_of(here * per, per), per)]
                pending[slot].append(
                    start_store(core, src, grads, x, part % 2, other, iz, osem.at[slot, side, label])
                )

    for part in range(PARTS):
        there = natural_part(part)
        here = slice(part * size, (part + 1) * size)
        up, down = span(there * size, size), span(units + there * size, size)
        d = (nt(dbr[...], w[down, :]) * gp[:, here].astype(F32)).astype(BF)
        dpre[...] = d
        db1_ref[:, span(there * size, size)] = jnp.sum(d.astype(F32), axis=0, keepdims=True)
        more = nn(d, w[up, :])
        if part == 0:
            acc[...] = more
        else:
            acc[...] += more
        for copy in pending[part % 2]:
            copy.wait()
        pending[part % 2] = []
        emit(part, 0, tn(dpre[...], h[...]).astype(BF))
        emit(part, 1, tn(act[:, here], dbr[...]).astype(BF))

    def stores(r):
        return [
            pltpu.make_async_copy(dres.at[tile(r)], dres_hbm.at[tile(r)], isem.at[1]),
            pltpu.make_async_copy(out.at[tile(r)], datt_hbm.at[tile(r)], isem.at[2]),
        ]

    for copy in out_copies:
        copy.wait()

    @pl.loop(0, tiles)
    def _(r):
        at = tile(r)
        dhid = dres[at, :] + acc[at, :]
        n = normed[at, :]
        d = norm_back(dhid, n, inv_ref[at, :], g1)
        low = d.astype(BF)
        dres[at, :] = d
        out[at, :] = low
        sums_ref[3:4] += jnp.sum(dhid * n, axis=0, keepdims=True)
        sums_ref[4:5] += jnp.sum(dhid, axis=0, keepdims=True)
        sums_ref[5:6] += jnp.sum(low.astype(F32), axis=0, keepdims=True)
        for copy in stores(r):
            copy.start()

    @pl.loop(0, tiles)
    def _(r):
        for copy in stores(r):
            copy.wait()

    for copy in pending[0] + pending[1]:
        copy.wait()


def ffn_call(grid, me, vec, inv, h, normed, dy_mine, dy_others, pieces, per):
    rows, width = h.shape
    total = grid.devices * per
    units = total // 2
    size = units // PARTS
    paths = path_shapes(grid, grid.devices, per, width)
    return pl.pallas_call(
        lambda *r: ffn_kernel(grid, per, *r),
        in_specs=[SMEM, VMEM, VMEM, ANY, ANY, ANY, ANY] + [ANY] * len(pieces),
        out_specs=[ANY, ANY, ANY, ANY, VMEM, VMEM] + [ANY] * len(paths),
        out_shape=[
            jax.ShapeDtypeStruct(dy_mine.shape, BF),
            jax.ShapeDtypeStruct((dy_mine.shape[0] // 2,) + dy_mine.shape[1:], BF),
            jax.ShapeDtypeStruct((rows, width), F32),
            jax.ShapeDtypeStruct((rows, width), BF),
            jax.ShapeDtypeStruct((8, width), F32),
            jax.ShapeDtypeStruct((1, units), F32),
        ]
        + paths,
        scratch_shapes=[
            pltpu.VMEM((total, width), BF),
            pltpu.VMEM((rows, width), BF),
            pltpu.VMEM((rows, width), F32),
            pltpu.VMEM((rows, width), BF),
            pltpu.VMEM((rows, units), BF),
            pltpu.VMEM((rows, units), BF),
            pltpu.VMEM((rows, width), F32),
            pltpu.VMEM((rows, width), F32),
            pltpu.VMEM((rows, width), BF),
            pltpu.VMEM((rows, width), BF),
            pltpu.VMEM((rows, size), BF),
            pltpu.VMEM((2, 2, size, width), BF),
            pltpu.SemaphoreType.DMA((grid.devices,)),
            pltpu.SemaphoreType.DMA((3,)),
            pltpu.SemaphoreType.DMA((2, 2, max(size // per, 2))),
            pltpu.SemaphoreType.DMA((dy_mine.shape[0],)),
        ],
        compiler_params=params(),
        cost_estimate=cost(6 * rows * width * units, 40 << 20, 2 * rows * units),
        name="ffn",
    )(me, vec, inv, h, normed, dy_mine, dy_others, *pieces)


def out_back_kernel(grid, npieces, me_ref, datt_hbm, ctx_hbm, *rest):
    pieces = rest[:npieces]
    dctx_hbm, grad_hbm, w, datt, ctx, dctx, grad, sems, isem, osem = rest[-10:]
    first = 3 * grid.devices // 4
    loads = [
        pltpu.make_async_copy(datt_hbm, datt, isem.at[0]),
        pltpu.make_async_copy(ctx_hbm, ctx, isem.at[1]),
    ]
    loads[0].start()
    start_natural(grid, me_ref, pieces, w, sems, first)
    loads[1].start()
    loads[0].wait()
    wait_natural(grid, pieces, w, sems, first, grid.devices - first, first)
    dctx[...] = nn(datt[...], w[...]).astype(BF)
    stores = [
        pltpu.make_async_copy(dctx, dctx_hbm, osem.at[0]),
        pltpu.make_async_copy(grad, grad_hbm, osem.at[1]),
    ]
    stores[0].start()
    loads[1].wait()
    grad[...] = tn(datt[...], ctx[...]).astype(BF)
    stores[1].start()
    for copy in stores:
        copy.wait()


def out_back_call(grid, me, datt, ctx, pieces, deps):
    rows, width = ctx.shape
    return pl.pallas_call(
        lambda *r: out_back_kernel(grid, len(pieces), *r),
        in_specs=[SMEM, ANY, ANY] + [ANY] * (len(pieces) + len(deps)),
        out_specs=[ANY, ANY],
        out_shape=[
            jax.ShapeDtypeStruct((rows, width), BF),
            jax.ShapeDtypeStruct((width, width), BF),
        ],
        scratch_shapes=[
            pltpu.VMEM((width, width), BF),
            pltpu.VMEM((rows, width), BF),
            pltpu.VMEM((rows, width), BF),
            pltpu.VMEM((rows, width), BF),
            pltpu.VMEM((width, width), BF),
            pltpu.SemaphoreType.DMA((grid.devices,)),
            pltpu.SemaphoreType.DMA((2,)),
            pltpu.SemaphoreType.DMA((2,)),
        ],
        compiler_params=params(),
        cost_estimate=cost(2 * rows * width * width, 12 << 20),
        name="out_back",
    )(me, datt, ctx, *pieces, *deps)


def attend_back_kernel(seq, len_ref, q_ref, k_ref, v_ref, d_ref, lse_ref, *rest):
    dz_ref, db_ref, _ = rest[-3:]
    live_len = len_ref[seq]
    length, pair = q_ref.shape
    half = pair // 2
    q, k, v, d = q_ref[...], k_ref[...], v_ref[...], d_ref[...]
    lane = lax.broadcasted_iota(jnp.int32, (length, pair), 1)
    live = lax.broadcasted_iota(jnp.int32, (length, 1), 0) < live_len
    zero = jnp.zeros_like(q)
    first = lane < half
    q2, d2 = (
        jnp.concatenate([jnp.where(first, t, zero), jnp.where(first, zero, t)]) for t in (q, d)
    )
    log_total = jnp.concatenate([lse_ref[0, 0:1, :], lse_ref[0, 1:2, :]], axis=1)
    p = jnp.where(live, jnp.exp(nt(k, q2) - log_total), 0.0)
    dp = nt(v, d2)
    inner = jnp.sum(p * dp, axis=0, keepdims=True)
    ds = (p * (dp - inner)).astype(BF)
    dv = nn(p.astype(BF), d2)
    dk = nn(ds, q2)
    turned = nn(k.T, ds)
    dq = jnp.concatenate([turned[:half, :length], turned[half:, length:]]).T
    scale = half ** -0.5
    dq = (dq.astype(BF).astype(F32) * scale).astype(BF)
    dv = dv.astype(BF)
    dz_ref[0] = dq
    dz_ref[1] = dk.astype(BF)
    dz_ref[2] = dv
    db_ref[0:1] = jnp.sum(dq.astype(F32), axis=0, keepdims=True)
    db_ref[1:2] = jnp.sum(dv.astype(F32), axis=0, keepdims=True)


def attend_back_call(lens, qkv, dctx, lse, seqs, seq, dz, carry, deps):
    rows, width = dctx.shape
    length = rows // seqs
    pairs = H // 2
    pw = width // pairs
    at = lambda part: pl.BlockSpec((length, pw), lambda p: (seq, part * pairs + p))
    more = [carry] + ([] if dz is None else [dz]) + list(deps)
    return pl.pallas_call(
        lambda *r: attend_back_kernel(seq, *r),
        grid=(pairs,),
        in_specs=[
            SMEM,
            at(0),
            at(1),
            at(2),
            at(0),
            pl.BlockSpec((1, 2, length), lambda p: (seq * pairs + p, 0, 0)),
        ]
        + [ANY] * len(more),
        out_specs=[
            pl.BlockSpec((3, length, pw), lambda p: (0, seq, p)),
            pl.BlockSpec((2, pw), lambda p: (0, p)),
            ANY,
        ],
        out_shape=[
            jax.ShapeDtypeStruct((3, rows, width), BF),
            jax.ShapeDtypeStruct((2, width), F32),
            jax.ShapeDtypeStruct(carry.shape, carry.dtype),
        ],
        input_output_aliases={6: 2} if dz is None else {6: 2, 7: 0},
        compiler_params=params(),
        cost_estimate=cost(
            20 * H * length * length * (width // H), 6 << 20, H * length * length
        ),
        name="attend_back",
    )(lens, qkv, qkv, qkv, dctx, lse, *more)


def attn_grad_kernel(
    grid, per, npieces, me_ref, sums, db1, db_a, db_b, dz_hbm, x_hbm, gout_hbm, dres_hbm, *rest
):
    pieces = rest[:npieces]
    count = 8 if is_path(grid, per) else 2
    grads, (mine, others) = rest[-13 - count : -13], rest[-13:-11]
    stage, dz, x, gout, line, total, w = rest[-11:-4]
    isem, osem, wsem, dsem = rest[-4:]
    rows, width = x.shape
    me = me_ref[0]
    core = me & 1
    blocks = grid.devices // 4
    path = is_path(grid, per)
    loads = [pltpu.make_async_copy(gout_hbm, gout, isem.at[4])]
    loads += [pltpu.make_async_copy(x_hbm, x, isem.at[3])]
    loads += [pltpu.make_async_copy(dz_hbm.at[p], dz.at[p], isem.at[p]) for p in range(3)]
    for copy in loads:
        copy.start()
    load_total = pltpu.make_async_copy(dres_hbm, total, isem.at[5])
    load_total.start()
    start_natural(grid, me_ref, pieces, w, wsem, 0, 3 * blocks)

    db = db_a[...] + db_b[...]
    tail = 3 * width + FF
    line[:, 0:width] = db[0:1]
    line[:, width : 2 * width] = db[1:2]
    line[:, 2 * width : 3 * width] = sums[5:6]
    line[:, 3 * width : tail] = db1[...]
    for i, row in enumerate((2, 3, 4, 0, 1)):
        line[:, tail + i * width : tail + (i + 1) * width] = sums[row : row + 1]
    count = line.shape[1] // grid.devices
    blank = jnp.zeros((8, width), F32)
    first_row = lax.broadcasted_iota(jnp.int32, (8, count), 0) == 0
    for d in range(grid.devices):
        values = jnp.where(first_row, line[:, d * count : (d + 1) * count], 0.0)
        values = jnp.concatenate([values, blank[:, count:]], axis=1).astype(BF)
        if path:
            stage[d, per : per + 8] = values
        else:
            grads[1][d] = values

    copies = []

    def emit(part, value):
        value = value.astype(BF)
        if not path:
            grads[0][part * width : (part + 1) * width, :] = value
            return
        stage[part * blocks : (part + 1) * blocks, 0:per] = value.reshape(blocks, per, width)
        iz = part ^ me // blocks
        for label in range(blocks):
            other, side_x, side_y = label & 1, label // 2 % 2, label // 4
            block = part * blocks + (label ^ (me & (blocks - 1)))
            copies.append(
                start_store(
                    core, stage.at[block], grads, side_x, side_y, other, iz, osem.at[part * blocks + label]
                )
            )

    loads[0].wait()
    emit(3, gout[...])
    loads[1].wait()
    for part in range(3):
        loads[2 + part].wait()
        emit(part, tn(dz[part], x[...]))
    load_total.wait()
    for part in range(3):
        wait_natural(grid, pieces, w, wsem, part * blocks, blocks, 0, 3 * blocks)
        total[...] += nn(dz[part], w[part * width : (part + 1) * width, :])
    for copy in store_sequences(core, total, mine, others, dsem) + copies:
        copy.wait()


def attn_grad_call(grid, me, dz, x, gout, dres, vectors, pieces, per, shape, deps):
    rows, width = x.shape
    paths = path_shapes(grid, grid.devices, per, width)
    path = is_path(grid, per)
    if path:
        paths = [jax.ShapeDtypeStruct((p.shape[0], per + 8, width), BF) for p in paths]
    return pl.pallas_call(
        lambda *r: attn_grad_kernel(grid, per, len(pieces), *r),
        in_specs=[SMEM] + [VMEM] * len(vectors) + [ANY] * (4 + len(pieces) + len(deps)),
        out_specs=[ANY if path else VMEM] * len(paths) + [ANY, ANY],
        out_shape=paths
        + [
            jax.ShapeDtypeStruct(shape, F32),
            jax.ShapeDtypeStruct((shape[0] // 2,) + shape[1:], F32),
        ],
        scratch_shapes=[
            pltpu.VMEM((grid.devices, per + 8, width), BF),
            pltpu.VMEM((3, rows, width), BF),
            pltpu.VMEM((rows, width), BF),
            pltpu.VMEM((width, width), BF),
            pltpu.VMEM((1, 8 * width + FF), F32),
            pltpu.VMEM((rows, width), F32),
            pltpu.VMEM((3 * width, width), BF),
            pltpu.SemaphoreType.DMA((6,)),
            pltpu.SemaphoreType.DMA((grid.devices,)),
            pltpu.SemaphoreType.DMA((grid.devices,)),
            pltpu.SemaphoreType.DMA((shape[0],)),
        ],
        compiler_params=params(),
        cost_estimate=cost(6 * rows * width * width, 28 << 20),
        name="attn_grad",
    )(me, *vectors, dz, x, gout, dres, *pieces, *deps)


def gate(value, deps):
    return pl.pallas_call(
        lambda *r: None,
        in_specs=[ANY] * (1 + len(deps)),
        out_specs=ANY,
        out_shape=jax.ShapeDtypeStruct(value.shape, value.dtype),
        input_output_aliases={0: 0},
        compiler_params=params(),
        cost_estimate=cost(0, 0),
        name="gate",
    )(value, *deps)


def ordered_stack_kernel(count, *rest):
    for i in range(count):
        rest[-1][i] = rest[i][...]


def ordered_stack(parts, deps):
    return pl.pallas_call(
        lambda *r: ordered_stack_kernel(len(parts), *r),
        in_specs=[VMEM] * len(parts) + [ANY] * len(deps),
        out_specs=VMEM,
        out_shape=jax.ShapeDtypeStruct((len(parts),) + parts[0].shape, parts[0].dtype),
        compiler_params=params(),
        name="ordered_stack",
    )(*parts, *deps)


def adam_update(master, moment, second, grad, rate):
    moment_new = decay_rate * moment + (1.0 - decay_rate) * grad
    second_new = decay_rate * second + (1.0 - decay_rate) * grad * grad
    correction = 1.0 - decay_rate**STEP
    direction = moment_new / correction / (jnp.sqrt(second_new / correction) + adam_epsilon)
    master_new = master - rate * (direction + weight_decay * master)
    return (moment_new, second_new, master_new)


def join_sequences(mine, others, core):
    count = others.shape[0]
    return lax.dynamic_update_slice(mine, others, ((1 - core) * count, 0, 0))


def local(
    tokens,
    cotangent,
    seq_lengths,
    slot_order,
    attn_weights,
    attn_moment,
    attn_second,
    ffn_weights,
    ffn_moment,
    ffn_second,
    vectors,
    vector_moment,
    vector_second,
):
    grid = Grid(lax.axis_size("dp"))
    core = lax.axis_index("seq")
    shard_index = lax.axis_index(AXES)
    me = shard_index.astype(jnp.int32).reshape(1)
    seq_count, half_len, width = tokens.shape
    seqs = seq_count // 2
    length = 2 * half_len
    rows = seqs * length
    per, ffn_per = attn_weights.shape[1], ffn_weights.shape[1]
    vec_per = vectors.shape[0]
    path = is_path(grid, per) and is_path(grid, ffn_per)

    slot_pick = (slot_order[0][:, None] == jnp.arange(seq_count)[None, :]).astype(jnp.int32)
    slot_len = jnp.sum(slot_pick * seq_lengths[0][None, :], axis=1)
    lens = lax.dynamic_slice_in_dim(slot_len, core * seqs, seqs, 0)

    vec_rows = jnp.zeros((8, width), BF)
    vec_rows = lax.dynamic_update_slice(vec_rows, vectors.astype(BF)[None, :], (0, 0))
    attn_block = jnp.concatenate([attn_weights.astype(BF).T, vec_rows])

    other_core = lambda value: permute(value, grid, lambda c: 1)
    tokens_other = other_core(tokens)
    if path:
        attn_parts = gather_z(grid, attn_block)
        ffn_block = ffn_weights.astype(BF).T
        ffn_parts = gather_z(grid, ffn_block)
        attn_z = ordered_stack(attn_parts, [ffn_block])
        attn_two = gather_two(grid, attn_z)
        attn_two = attn_two[:1] + [gate(t, ffn_parts[1:2]) for t in attn_two[1:]]
        attn_three = gather_three(grid, attn_two)
        ffn_z = ordered_stack(ffn_parts, attn_two[1:])
        ffn_two = gather_two(grid, ffn_z)
        weights = with_core(grid, attn_two + attn_three, [ffn_z])
        vec = natural_vectors(grid, weights, core, me[0], per, vec_per)
    else:
        whole_rows = lambda block: [lax.all_gather(block, AXES, axis=0, tiled=True)]
        weights = whole_rows(attn_block[:per])
        ffn_pieces = whole_rows(ffn_weights.astype(BF).T)
        ffn_two = []
        vec = lax.all_gather(attn_block[per:], AXES)[:, 0, :vec_per].reshape(1, -1).astype(F32)
    dy_other = other_core(cotangent)

    qkv, x = qkv_call(grid, me, vec, tokens, tokens_other, weights)
    fwd = attend_call(grid, me, lens, qkv, x, vec, weights, seqs, 0, [], [])
    ffn_two = ffn_two[:1] + [gate(t, fwd[:1]) for t in ffn_two[1:]]
    fwd = attend_call(grid, me, lens, qkv, x, vec, weights, seqs, 1, fwd, ffn_two[1:])
    ctx, lse, normed, inv, hidden = fwd
    if path:
        ffn_three = gather_three(grid, ffn_two)
        ffn_three = ffn_three[:1] + [gate(t, fwd[:1]) for t in ffn_three[1:]]
        ffn_pieces = with_core(grid, ffn_two + ffn_three, [])
    out, out_other, dres_one, datt, sums, db1, *grads_f = ffn_call(
        grid, me, vec, inv, hidden, normed, cotangent, dy_other, ffn_pieces, ffn_per
    )
    layer_out = join_sequences(out, other_core(out_other), core)

    sums_f = Sums(grid, path, grads_f)
    sends = sums_f.add_core()
    dctx, gout = out_back_call(grid, me, datt, ctx, weights, sends)
    dz, db_a, sums_f.keep[1] = attend_back_call(
        lens, qkv, dctx, lse, seqs, 0, None, sums_f.keep[1], sends
    )
    sends = sums_f.add_three()
    dz, db_b, sums_f.keep[0] = attend_back_call(
        lens, qkv, dctx, lse, seqs, 1, dz, sums_f.keep[0], sends
    )
    sends = sums_f.add_two()
    *grads_c, dx, dx_other = attn_grad_call(
        grid, me, dz, x, gout, dres_one, [sums, db1, db_a, db_b], weights, per, tokens.shape, sends
    )
    if path:
        grads_c[7] = gate(grads_c[7], sums_f.z[1:2])
    sums_c = Sums(grid, path, grads_c)
    sums_c.add_core()
    ffn_sum = sums_f.add_z()
    sums_c.add_three()
    sums_c.keep[0] = gate(sums_c.keep[0], [ffn_sum])
    input_grad = join_sequences(dx, other_core(dx_other), core)
    sums_c.add_two()
    attn_sum = sums_c.add_z()

    vector_sum = attn_sum[per, :vec_per]
    attn_sum = attn_sum[:per].T
    ffn_sum = ffn_sum[:ffn_per].T

    attn_cols = shard_index * per + jnp.arange(per)
    attn_rate = jnp.where(
        attn_cols < 2 * width, math.sqrt(2.0), jnp.where(attn_cols < 3 * width, 1.5, 1.8)
    ) * width ** (-0.5)
    ffn_cols = shard_index * ffn_per + jnp.arange(ffn_per)
    ffn_rate = jnp.where(ffn_cols < FF, width ** (-0.5), 1.5 * FF ** (-0.5))
    attn_m, attn_v, attn_new = adam_update(
        attn_weights, attn_moment, attn_second, attn_sum, attn_rate[None, :]
    )
    ffn_m, ffn_v, ffn_new = adam_update(
        ffn_weights, ffn_moment, ffn_second, ffn_sum, ffn_rate[None, :]
    )
    vec_m, vec_v, vec_new = adam_update(
        vectors, vector_moment, vector_second, vector_sum, vector_rate
    )
    return (
        layer_out,
        input_grad,
        attn_m,
        attn_v,
        attn_new,
        attn_new.astype(BF),
        ffn_m,
        ffn_v,
        ffn_new,
        ffn_new.astype(BF),
        vec_m,
        vec_v,
        vec_new,
        vec_new.astype(BF),
    )


def solution(mesh):
    columns = P(None, AXES)
    flat = P(AXES)
    rows = P("dp", "seq", None)
    placed = (rows, rows, P("dp", None), P("dp", None)) + (columns,) * 6 + (flat,) * 3
    return jax.shard_map(
        local,
        mesh=mesh,
        in_specs=placed,
        out_specs=(rows, rows) + (columns,) * 8 + (flat,) * 4,
        check_vma=False,
    )
```

```python
import math

import jax
import jax.numpy as jnp
from jax import lax
from jax.experimental import pallas as pl
from jax.experimental.pallas import tpu as pltpu
from jax.sharding import PartitionSpec as P

H = 12
FF = 3072
STEP = 5

epsilon = 1e-06
masked_score = -1e30
decay_rate = 0.5
adam_epsilon = 1e-08
weight_decay = 0.01
vector_rate = 0.5

AXES = ("dp", "seq")
BF = jnp.bfloat16
F32 = jnp.float32
VMEM_LIMIT = 56 * 1024 * 1024
TILE = 256
COST = 16
ANY = pl.BlockSpec(memory_space=pl.ANY)
SMEM = pl.BlockSpec(memory_space=pltpu.SMEM)
VMEM = pl.BlockSpec(memory_space=pltpu.VMEM)


def nn(a, b):
    return lax.dot_general(a, b, (((1,), (0,)), ((), ())), preferred_element_type=F32)


def nt(a, b):
    return lax.dot_general(a, b, (((1,), (1,)), ((), ())), preferred_element_type=F32)


def tn(a, b):
    return lax.dot_general(a, b, (((0,), (0,)), ((), ())), preferred_element_type=F32)


class Grid:
    def __init__(self, chips):
        power = chips.bit_length() - 1
        if 1 << power == chips:
            self.side = 1 << (power // 3)
            self.nz = chips // (self.side * self.side)
        else:
            self.side, self.nz = 1, chips
        self.devices = 2 * chips
        self.xor = 1 << power == chips

    def z_mask(self, m):
        return m * 2 * self.side * self.side

    def x_mask(self, m):
        return 2 * m

    def y_mask(self, m):
        return 2 * m * self.side

    def label(self, core, other, i3, i2, iz):
        x = jnp.where(core == 0, i2, i3)
        y = jnp.where(core == 0, i3, i2)
        return self.z_mask(iz) + self.y_mask(y) + self.x_mask(x) + other


def permute(value, grid, mask_of_core):
    pairs = [(i, i ^ mask_of_core(i & 1)) for i in range(grid.devices)]
    return lax.ppermute(value, AXES, pairs)


def along_two(grid, value, m):
    return permute(value, grid, lambda c: grid.x_mask(m) if c == 0 else grid.y_mask(m))


def along_three(grid, value, m):
    return permute(value, grid, lambda c: grid.y_mask(m) if c == 0 else grid.x_mask(m))


def gather_z(grid, block):
    return [block] + [permute(block, grid, lambda c: grid.z_mask(m)) for m in range(1, grid.nz)]


def gather_two(grid, zed):
    return [zed] + [along_two(grid, zed, m) for m in range(1, grid.side)]


def gather_three(grid, two):
    return [along_three(grid, t, m) for m in range(1, grid.side) for t in two]


def with_core(grid, own, deps):
    own = [gate(own[0], deps) if deps else own[0]] + own[1:]
    return own + [permute(p, grid, lambda c: 1) for p in own]


def is_path(grid, rows):
    return grid.side == 2 and grid.nz == 4 and rows % 16 == 0


def slot_of(grid, label, core):
    other = label & 1
    x = (label // 2) & (grid.side - 1)
    y = (label // (2 * grid.side)) & (grid.side - 1)
    z = label // (2 * grid.side * grid.side)
    first = (core ^ other) == 0
    i2 = jnp.where(first, x, y)
    i3 = jnp.where(first, y, x)
    return other, (i3 * grid.side + i2) * grid.nz + z


def natural_vectors(grid, pieces, core, me, row, count):
    side, nz = grid.side, grid.nz
    table = jnp.stack([p[:, row, :count] for p in pieces]).reshape(2, side, side, nz, count)
    turned = jnp.swapaxes(table, 1, 2)
    first = jnp.stack([table[0], turned[1]])
    second = jnp.stack([turned[0], table[1]])
    value = jnp.where(core == 0, first, second)
    value = jnp.transpose(value, (3, 1, 2, 0, 4)).reshape(grid.devices, count)
    bit = 1
    while bit < grid.devices:
        pairs = value.reshape(-1, 2, bit, count)
        value = jnp.where((me & bit) == 0, pairs, pairs[:, ::-1]).reshape(grid.devices, count)
        bit *= 2
    return value.reshape(1, -1).astype(F32)


def start_natural(grid, me_ref, pieces, dest, sems, first=0, last=None, order=None):
    last = grid.devices if last is None else last
    rows = dest.shape[0] // (last - first)
    if len(pieces) == 1:
        pltpu.make_async_copy(
            pieces[0].at[pl.ds(first * rows, (last - first) * rows)], dest, sems.at[0]
        ).start()
        return
    me = me_ref[0]
    core = me & 1
    side, nz = grid.side, grid.nz
    for label in sorted(range(grid.devices), key=order or (lambda j: j // (2 * side * side))):
        other, x, y = label & 1, label // 2 % side, label // (2 * side) % side
        iz = label // (2 * side * side)
        block = me ^ label

        def start(ref, block=block, iz=iz):
            row = pl.multiple_of((block - first) * rows, rows)
            pltpu.make_async_copy(
                ref.at[iz, pl.ds(0, rows)], dest.at[pl.ds(row, rows)], sems.at[block]
            ).start()

        def either(other=other, x=x, y=y, start=start):
            one = pieces[(other * side + y) * side + x]
            two = pieces[(other * side + x) * side + y]
            if x == y:
                start(one)
            else:
                pl.when((core ^ other) == 0)(lambda: start(one))
                pl.when((core ^ other) != 0)(lambda: start(two))

        if last - first == grid.devices:
            either()
        else:
            pl.when((block >= first) & (block < last))(either)


def wait_natural(grid, pieces, dest, sems, begin, count, first=0, last=None):
    last = grid.devices if last is None else last
    rows = dest.shape[0] // (last - first)
    if len(pieces) == 1:

        @pl.when(begin == first)
        def _():
            pltpu.make_async_copy(
                pieces[0].at[pl.ds(first * rows, (last - first) * rows)], dest, sems.at[0]
            ).wait()

        return
    for i in range(count):
        block = begin + i
        pltpu.make_async_copy(
            pieces[0].at[0, pl.ds(0, rows)],
            dest.at[pl.ds(pl.multiple_of((block - first) * rows, rows), rows)],
            sems.at[block],
        ).wait()


def path_shapes(grid, blocks, per, width):
    if not is_path(grid, per):
        return [
            jax.ShapeDtypeStruct((blocks * per, width), BF),
            jax.ShapeDtypeStruct((blocks, 8, width), BF),
        ]
    return [jax.ShapeDtypeStruct((grid.nz, per, width), BF)] * 8


def start_store(core, src, dests, x, y, other, iz, sem):
    one, two = (dests[4 * other + k].at[iz] for k in (2 * y + x, 2 * x + y))
    copy = pltpu.make_async_copy(src, one, sem)
    if x == y:
        copy.start()
    else:
        pl.when((core ^ other) == 0)(lambda: copy.start())
        pl.when((core ^ other) != 0)(lambda: pltpu.make_async_copy(src, two, sem).start())
    return copy


class Sums:
    def __init__(self, grid, path, blocks):
        self.grid, self.path = grid, path
        self.three, self.two, self.z = [], [], []
        if path:
            self.keep = list(blocks[:4])
            got = {k: permute(blocks[4 + k], grid, lambda c: 1) for k in (3, 2, 1, 0)}
            self.core = [got[k] for k in range(4)]
        else:
            self.keep = list(blocks)

    def terms(self, i3, i2, iz):
        grid = self.grid
        at = i3 * grid.side + i2
        total = self.keep[at][iz].astype(F32) + self.core[at][iz].astype(F32)
        if i3 == 0:
            for there, got in self.three:
                if there == i2:
                    total = total + got[iz].astype(F32)
            if i2 == 0:
                for got in self.two:
                    total = total + got[iz].astype(F32)
        return total

    def add_core(self):
        if not self.path:
            return []
        grid = self.grid
        every = slice(0, grid.nz)
        sends = [
            (i2, m, self.terms(m, i2, every).astype(BF))
            for i2 in reversed(range(grid.side))
            for m in range(1, grid.side)
        ]
        self.three = [(i2, along_three(grid, value, m)) for i2, m, value in sends]
        return [value for _, _, value in sends]

    def add_three(self):
        if not self.path:
            return []
        grid = self.grid
        every = slice(0, grid.nz)
        sends = [self.terms(0, m, every).astype(BF) for m in range(1, grid.side)]
        self.two = [along_two(grid, sends[m - 1], m) for m in range(1, grid.side)]
        return sends

    def add_two(self):
        if not self.path:
            return []
        grid = self.grid
        sends = [self.terms(0, 0, slice(m, m + 1))[0].astype(BF) for m in range(1, grid.nz)]
        self.z = [
            permute(sends[m - 1], grid, lambda c: grid.z_mask(m)) for m in range(1, grid.nz)
        ]
        return sends

    def add_z(self):
        if not self.path:
            rows = [v.reshape(-1, v.shape[-1]).astype(F32) for v in self.keep]
            return jnp.concatenate(
                [lax.psum_scatter(v, AXES, scatter_dimension=0, tiled=True) for v in rows]
            )
        total = self.terms(0, 0, slice(0, 1))[0]
        for got in self.z:
            total = total + got.astype(F32)
        return total


def params(**more):
    return pltpu.CompilerParams(vmem_limit_bytes=VMEM_LIMIT, **more)


def cost(macs, bytes_accessed, trans=0):
    return pl.CostEstimate(
        flops=2 * macs // COST, bytes_accessed=bytes_accessed // COST, transcendentals=trans // COST
    )


def rows_spec(width, tile=TILE):
    return pl.BlockSpec((tile, width), lambda i: (i, 0))


def whole(shape):
    zeros = (0,) * len(shape)
    return pl.BlockSpec(shape, lambda *i: zeros)


def fixed(*shape):
    zeros = (0,) * len(shape)
    return pl.BlockSpec(shape, lambda i: zeros)


def norm_rows(values):
    center = values - jnp.mean(values, axis=-1, keepdims=True)
    inverse = lax.rsqrt(jnp.mean(center * center, axis=-1, keepdims=True) + epsilon)
    return center * inverse, inverse


def norm_back(upstream, normed, inverse, gain):
    u = upstream * gain
    centered = u - jnp.mean(u, axis=-1, keepdims=True)
    return inverse * (centered - normed * jnp.mean(u * normed, axis=-1, keepdims=True))


def gelu_pair(u):
    phi = 0.5 + 0.5 * lax.erf(u * math.sqrt(0.5))
    density = jnp.exp(-0.5 * (u * u))
    return u * phi, phi + (u * (1.0 / math.sqrt(2.0 * math.pi))) * density


def load_sequences(me_ref, mine, others, dest, sems):
    count = mine.shape[0] // 2
    half = mine.shape[1]
    core = me_ref[0] & 1
    copies = []
    for s in range(count):
        seq = me_ref[1 + s]
        for i, src in enumerate((mine, others)):
            at = s * 2 * half + (core ^ i) * half
            copies.append(
                pltpu.make_async_copy(
                    src.at[seq], dest.at[pl.ds(pl.multiple_of(at, half), half)], sems.at[2 * s + i]
                )
            )
    for copy in copies:
        copy.start()
    return copies


def store_sequences(me_ref, src, mine, others, sems):
    count, half = others.shape[0], others.shape[1]
    core = me_ref[0] & 1
    copies = []
    for s in range(count):
        for i, dest in enumerate((mine.at[me_ref[1 + s]], others.at[s])):
            at = s * 2 * half + (core ^ i) * half
            copies.append(
                pltpu.make_async_copy(
                    src.at[pl.ds(pl.multiple_of(at, half), half)], dest, sems.at[2 * s + i]
                )
            )
    for copy in copies:
        copy.start()
    return copies


def quarter_order(grid, me_ref, pieces, i):
    if len(pieces) == 1:
        return i
    lines = grid.nz // 4
    return (i * lines ^ me_ref[0] // (2 * grid.side * grid.side)) // lines


def qkv_kernel(grid, me_ref, vec_ref, mine, others, *rest):
    pieces, (out_hbm, x_hbm, w, x, out, wsem, xsem, osem) = rest[:-8], rest[-8:]
    rows, width = x.shape
    loads = load_sequences(me_ref, mine, others, x, xsem)
    blocks = grid.devices // 4
    start_natural(grid, me_ref, pieces, w, wsem, 0, 3 * blocks)
    for copy in loads:
        copy.wait()
    copy_x = pltpu.make_async_copy(x, x_hbm, osem.at[3])
    copy_x.start()

    def store(part):
        cols = pl.ds(pl.multiple_of(part * width, width), width)
        return pltpu.make_async_copy(out.at[:, cols], out_hbm.at[:, cols], osem.at[part])

    @pl.loop(0, 4)
    def _(i):
        part = quarter_order(grid, me_ref, pieces, i)

        @pl.when(part < 3)
        def _():
            wait_natural(grid, pieces, w, wsem, part * blocks, blocks, 0, 3 * blocks)
            cols = pl.ds(pl.multiple_of(part * width, width), width)
            bias = vec_ref[:, pl.ds(pl.multiple_of(part // 2 * width, width), width)]
            bias = jnp.where(part == 1, 0.0, bias)
            scale = jnp.where(part == 0, (width // H) ** -0.5, 1.0)
            out[:, cols] = ((nt(x[...], w[cols, :]) + bias) * scale).astype(BF)
            store(part).start()

    for part in range(3):
        store(part).wait()
    copy_x.wait()


def qkv_call(grid, me, vec, mine, others, pieces):
    width = mine.shape[2]
    rows = mine.shape[0] * mine.shape[1]
    return pl.pallas_call(
        lambda *r: qkv_kernel(grid, *r),
        in_specs=[SMEM, VMEM, ANY, ANY] + [ANY] * len(pieces),
        out_specs=[ANY, ANY],
        out_shape=[
            jax.ShapeDtypeStruct((rows, 3 * width), BF),
            jax.ShapeDtypeStruct((rows, width), BF),
        ],
        scratch_shapes=[
            pltpu.VMEM((3 * width, width), BF),
            pltpu.VMEM((rows, width), BF),
            pltpu.VMEM((rows, 3 * width), BF),
            pltpu.SemaphoreType.DMA((grid.devices,)),
            pltpu.SemaphoreType.DMA((mine.shape[0],)),
            pltpu.SemaphoreType.DMA((4,)),
        ],
        compiler_params=params(),
        cost_estimate=cost(rows * width * 3 * width, 12 << 20),
        name="qkv",
    )(me, vec, mine, others, *pieces)


def vector_refs(vec_ref, width):
    tail = 3 * width + FF
    found = [vec_ref[:, 2 * width : 3 * width], vec_ref[:, 3 * width : tail]]
    return found + [vec_ref[:, tail + i * width : tail + (i + 1) * width] for i in range(5)]


def live_blocks(live_len, length, body):
    size = min(128, length)
    count = (live_len + (size - 1)) // size
    for n in range(1, length // size + 1):
        pl.when(count == n)(lambda n=n: body(n * size))


def attend_kernel(grid, npieces, seq, len_ref, me_ref, q_ref, k_ref, v_ref, x_ref, vec_ref, *rest):
    pieces = rest[:npieces]
    quarter = grid.devices // 4
    ctx_ref, lse_ref, normed_ref, inv_ref, hid_ref, w, sems = rest[-7:]
    turn = pl.program_id(0)

    @pl.when(turn == 0)
    def _():
        start_natural(grid, me_ref, pieces, w, sems, 3 * quarter)

    live_len = len_ref[seq]
    length, pair = q_ref.shape
    half = pair // 2

    def attend(keys):
        q, k, v = q_ref[...], k_ref[0:keys, :], v_ref[0:keys, :]
        lane = lax.broadcasted_iota(jnp.int32, (length, pair), 1)
        live = lax.broadcasted_iota(jnp.int32, (1, keys), 1) < live_len
        outs, stats = [], []
        for h in (0, 1):
            mine = (lane >= half) if h else (lane < half)
            s = nt(jnp.where(mine, q, jnp.zeros_like(q)), k)
            s = jnp.where(live, s, masked_score)
            top = jnp.max(s, axis=-1, keepdims=True)
            p = jnp.exp(s - top)
            total = jnp.sum(p, axis=-1, keepdims=True)
            outs.append(nn(p.astype(BF), v) / total)
            stats.append(top + jnp.log(total))
        ctx = jnp.where(lane < half, outs[0], outs[1]).astype(BF)
        ctx_ref[:, pl.ds(pl.multiple_of(turn * pair, pair), pair)] = ctx
        turned = jnp.where(lane < half, stats[0], stats[1]).T
        lse_ref[0] = jnp.concatenate([turned[0:1], turned[half : half + 1]], axis=0)

    live_blocks(live_len, length, attend)

    @pl.when(turn == pl.num_programs(0) - 1)
    def _():
        wait_natural(grid, pieces, w, sems, 3 * quarter, quarter, 3 * quarter)
        bo, _, _, g1, e1, _, _ = vector_refs(vec_ref, x_ref.shape[1])
        r = x_ref[...].astype(F32) + (nt(ctx_ref[...], w[...]) + bo)
        normed, inverse = norm_rows(r)
        normed_ref[...] = normed
        inv_ref[...] = inverse
        hid_ref[...] = (normed * g1 + e1).astype(BF)


def attend_call(grid, me, lens, qkv, x, vec, pieces, seqs, seq, before, deps):
    rows, width = x.shape
    length = rows // seqs
    pairs = H // 2
    pw = width // pairs
    at = lambda part: pl.BlockSpec((length, pw), lambda p: (seq, part * pairs + p))
    seq_rows = lambda w: pl.BlockSpec((length, w), lambda p: (seq, 0))
    first = 7 + len(pieces)
    return pl.pallas_call(
        lambda *r: attend_kernel(grid, len(pieces), seq, *r),
        grid=(pairs,),
        in_specs=[SMEM, SMEM, at(0), at(1), at(2), seq_rows(width), whole(vec.shape)]
        + [ANY] * (len(pieces) + len(before) + len(deps)),
        out_specs=[
            seq_rows(width),
            pl.BlockSpec((1, 2, length), lambda p: (seq * pairs + p, 0, 0)),
            seq_rows(width),
            seq_rows(1),
            seq_rows(width),
        ],
        out_shape=[
            jax.ShapeDtypeStruct((rows, width), BF),
            jax.ShapeDtypeStruct((seqs * pairs, 2, length), F32),
            jax.ShapeDtypeStruct((rows, width), F32),
            jax.ShapeDtypeStruct((rows, 1), F32),
            jax.ShapeDtypeStruct((rows, width), BF),
        ],
        scratch_shapes=[
            pltpu.VMEM((width, width), BF),
            pltpu.SemaphoreType.DMA((grid.devices,)),
        ],
        input_output_aliases={first + i: i for i in range(len(before))},
        compiler_params=params(),
        cost_estimate=cost(8 * H * length * length * (width // H), 9 << 20, H * length * length),
        name="attend",
    )(lens, me, qkv, qkv, qkv, x, vec, *pieces, *before, *deps)


PARTS = 4


def ffn_kernel(grid, per, me_ref, vec_ref, inv_ref, h_hbm, normed_hbm, dy_mine, dy_others, *rest):
    npieces = len(rest) - 22 - (8 if is_path(grid, per) else 2)
    pieces = rest[:npieces]
    out_mine, out_others, dres_hbm, datt_hbm, sums_ref, db1_ref = rest[npieces : npieces + 6]
    grads = rest[npieces + 6 : -16]
    (w, h, normed, dy, act, gp, acc, dres, dbr, out, dpre, stage, wsem, isem, osem, dsem) = rest[-16:]
    rows, width = h.shape
    units = w.shape[0] // 2
    size = units // PARTS
    tiles = rows // TILE
    me = me_ref[0]
    core = me & 1

    _, _, b2, g1, e1, g2, e2 = vector_refs(vec_ref, width)
    loads = [
        pltpu.make_async_copy(src, dst, isem.at[i])
        for i, (src, dst) in enumerate(((h_hbm, h), (normed_hbm, normed)))
    ]
    loads[0].start()
    half = grid.devices // 2
    start_natural(grid, me_ref, pieces, w, wsem, order=lambda j: (j % half // (half // PARTS), j))
    loads[1].start()
    loads += load_sequences(me_ref, dy_mine, dy_others, dy, dsem)
    loads[0].wait()

    def tile(r):
        return pl.ds(pl.multiple_of(r * TILE, TILE), TILE)

    def natural_part(part):
        if len(pieces) == 1:
            return part
        return part ^ (me % half // (half // PARTS))

    def span(start, count):
        return pl.ds(pl.multiple_of(start, count), count)

    for part in range(PARTS):
        there = natural_part(part)
        for base in (0, half):
            wait_natural(
                grid, pieces, w, wsem, base + there * (half // PARTS), half // PARTS
            )
        here = slice(part * size, (part + 1) * size)
        up, down = span(there * size, size), span(units + there * size, size)
        a, slope = gelu_pair(nt(h[...], w[up, :]) + vec_ref[:, span(3 * width + there * size, size)])
        a = a.astype(BF)
        act[:, here] = a
        gp[:, here] = slope.astype(BF)
        more = nn(a, w[down, :])
        if part == 0:
            acc[...] = more
        else:
            acc[...] += more

    for copy in loads[1:]:
        copy.wait()
    sums_ref[...] = jnp.zeros_like(sums_ref)

    @pl.loop(0, tiles)
    def _(r):
        at = tile(r)
        hidden = normed[at, :] * g1 + e1
        value = hidden + (acc[at, :] + b2)
        n, inverse = norm_rows(value)
        out[at, :] = (n * g2 + e2).astype(BF)
        up = dy[at, :].astype(F32)
        d = norm_back(up, n, inverse, g2)
        low = d.astype(BF)
        dres[at, :] = d
        dbr[at, :] = low
        sums_ref[0:1] += jnp.sum(up * n, axis=0, keepdims=True)
        sums_ref[1:2] += jnp.sum(up, axis=0, keepdims=True)
        sums_ref[2:3] += jnp.sum(low.astype(F32), axis=0, keepdims=True)

    out_copies = store_sequences(me_ref, out, out_mine, out_others, dsem)

    path = is_path(grid, per)
    blocks = size // per
    pending = [[], []]

    def emit(part, side, value):
        slot, there = part % 2, natural_part(part)
        stage[slot, side] = value
        if not path:
            copy = pltpu.make_async_copy(
                stage.at[slot, side],
                grads[0].at[span(side * units + there * size, size)],
                osem.at[slot, side, 0],
            )
            copy.start()
            pending[slot].append(copy)
            return
        spread = 2 * grid.side * grid.side
        iz = (side * half ^ me & half) // spread + part // 2
        for x in (0, 1):
            for other in (0, 1):
                label = 2 * x + other
                here = label ^ (me & 3)
                src = stage.at[slot, side, pl.ds(pl.multiple_of(here * per, per), per)]
                pending[slot].append(
                    start_store(core, src, grads, x, part % 2, other, iz, osem.at[slot, side, label])
                )

    for part in range(PARTS):
        there = natural_part(part)
        here = slice(part * size, (part + 1) * size)
        up, down = span(there * size, size), span(units + there * size, size)
        d = (nt(dbr[...], w[down, :]) * gp[:, here].astype(F32)).astype(BF)
        dpre[...] = d
        db1_ref[:, span(there * size, size)] = jnp.sum(d.astype(F32), axis=0, keepdims=True)
        more = nn(d, w[up, :])
        if part == 0:
            acc[...] = more
        else:
            acc[...] += more
        for copy in pending[part % 2]:
            copy.wait()
        pending[part % 2] = []
        emit(part, 0, tn(dpre[...], h[...]).astype(BF))
        emit(part, 1, tn(act[:, here], dbr[...]).astype(BF))

    def stores(r):
        return [
            pltpu.make_async_copy(dres.at[tile(r)], dres_hbm.at[tile(r)], isem.at[1]),
            pltpu.make_async_copy(out.at[tile(r)], datt_hbm.at[tile(r)], isem.at[2]),
        ]

    for copy in out_copies:
        copy.wait()

    @pl.loop(0, tiles)
    def _(r):
        at = tile(r)
        dhid = dres[at, :] + acc[at, :]
        n = normed[at, :]
        d = norm_back(dhid, n, inv_ref[at, :], g1)
        low = d.astype(BF)
        dres[at, :] = d
        out[at, :] = low
        sums_ref[3:4] += jnp.sum(dhid * n, axis=0, keepdims=True)
        sums_ref[4:5] += jnp.sum(dhid, axis=0, keepdims=True)
        sums_ref[5:6] += jnp.sum(low.astype(F32), axis=0, keepdims=True)
        for copy in stores(r):
            copy.start()

    @pl.loop(0, tiles)
    def _(r):
        for copy in stores(r):
            copy.wait()

    for copy in pending[0] + pending[1]:
        copy.wait()


def ffn_call(grid, me, vec, inv, h, normed, dy_mine, dy_others, pieces, per):
    rows, width = h.shape
    total = grid.devices * per
    units = total // 2
    size = units // PARTS
    paths = path_shapes(grid, grid.devices, per, width)
    return pl.pallas_call(
        lambda *r: ffn_kernel(grid, per, *r),
        in_specs=[SMEM, VMEM, VMEM, ANY, ANY, ANY, ANY] + [ANY] * len(pieces),
        out_specs=[ANY, ANY, ANY, ANY, VMEM, VMEM] + [ANY] * len(paths),
        out_shape=[
            jax.ShapeDtypeStruct(dy_mine.shape, BF),
            jax.ShapeDtypeStruct((dy_mine.shape[0] // 2,) + dy_mine.shape[1:], BF),
            jax.ShapeDtypeStruct((rows, width), F32),
            jax.ShapeDtypeStruct((rows, width), BF),
            jax.ShapeDtypeStruct((8, width), F32),
            jax.ShapeDtypeStruct((1, units), F32),
        ]
        + paths,
        scratch_shapes=[
            pltpu.VMEM((total, width), BF),
            pltpu.VMEM((rows, width), BF),
            pltpu.VMEM((rows, width), F32),
            pltpu.VMEM((rows, width), BF),
            pltpu.VMEM((rows, units), BF),
            pltpu.VMEM((rows, units), BF),
            pltpu.VMEM((rows, width), F32),
            pltpu.VMEM((rows, width), F32),
            pltpu.VMEM((rows, width), BF),
            pltpu.VMEM((rows, width), BF),
            pltpu.VMEM((rows, size), BF),
            pltpu.VMEM((2, 2, size, width), BF),
            pltpu.SemaphoreType.DMA((grid.devices,)),
            pltpu.SemaphoreType.DMA((3,)),
            pltpu.SemaphoreType.DMA((2, 2, max(size // per, 2))),
            pltpu.SemaphoreType.DMA((dy_mine.shape[0],)),
        ],
        compiler_params=params(),
        cost_estimate=cost(6 * rows * width * units, 40 << 20, 2 * rows * units),
        name="ffn",
    )(me, vec, inv, h, normed, dy_mine, dy_others, *pieces)


def out_back_kernel(grid, npieces, me_ref, datt_hbm, ctx_hbm, *rest):
    pieces = rest[:npieces]
    dctx_hbm, grad_hbm, w, datt, ctx, dctx, grad, sems, isem, osem = rest[-10:]
    first = 3 * grid.devices // 4
    loads = [
        pltpu.make_async_copy(datt_hbm, datt, isem.at[0]),
        pltpu.make_async_copy(ctx_hbm, ctx, isem.at[1]),
    ]
    loads[0].start()
    start_natural(grid, me_ref, pieces, w, sems, first)
    loads[1].start()
    loads[0].wait()
    wait_natural(grid, pieces, w, sems, first, grid.devices - first, first)
    dctx[...] = nn(datt[...], w[...]).astype(BF)
    stores = [
        pltpu.make_async_copy(dctx, dctx_hbm, osem.at[0]),
        pltpu.make_async_copy(grad, grad_hbm, osem.at[1]),
    ]
    stores[0].start()
    loads[1].wait()
    grad[...] = tn(datt[...], ctx[...]).astype(BF)
    stores[1].start()
    for copy in stores:
        copy.wait()


def out_back_call(grid, me, datt, ctx, pieces, deps):
    rows, width = ctx.shape
    return pl.pallas_call(
        lambda *r: out_back_kernel(grid, len(pieces), *r),
        in_specs=[SMEM, ANY, ANY] + [ANY] * (len(pieces) + len(deps)),
        out_specs=[ANY, ANY],
        out_shape=[
            jax.ShapeDtypeStruct((rows, width), BF),
            jax.ShapeDtypeStruct((width, width), BF),
        ],
        scratch_shapes=[
            pltpu.VMEM((width, width), BF),
            pltpu.VMEM((rows, width), BF),
            pltpu.VMEM((rows, width), BF),
            pltpu.VMEM((rows, width), BF),
            pltpu.VMEM((width, width), BF),
            pltpu.SemaphoreType.DMA((grid.devices,)),
            pltpu.SemaphoreType.DMA((2,)),
            pltpu.SemaphoreType.DMA((2,)),
        ],
        compiler_params=params(),
        cost_estimate=cost(2 * rows * width * width, 12 << 20),
        name="out_back",
    )(me, datt, ctx, *pieces, *deps)


def attend_back_kernel(seq, len_ref, q_ref, k_ref, v_ref, d_ref, lse_ref, *rest):
    dz_ref, db_ref, _ = rest[-3:]
    live_len = len_ref[seq]
    length, pair = q_ref.shape
    half = pair // 2

    def back(keys):
        q, k, v, d = q_ref[...], k_ref[0:keys, :], v_ref[0:keys, :], d_ref[...]
        first = lax.broadcasted_iota(jnp.int32, (length, pair), 1) < half
        live = lax.broadcasted_iota(jnp.int32, (keys, 1), 0) < live_len
        zero = jnp.zeros_like(q)
        q2, d2 = (
            jnp.concatenate([jnp.where(first, t, zero), jnp.where(first, zero, t)]) for t in (q, d)
        )
        log_total = jnp.concatenate([lse_ref[0, 0:1, :], lse_ref[0, 1:2, :]], axis=1)
        p = jnp.where(live, jnp.exp(nt(k, q2) - log_total), 0.0)
        dp = nt(v, d2)
        inner = jnp.sum(p * dp, axis=0, keepdims=True)
        ds = (p * (dp - inner)).astype(BF)
        dv = nn(p.astype(BF), d2).astype(BF)
        dk = nn(ds, q2).astype(BF)
        turned = nn(k.T, ds)
        dq = jnp.concatenate([turned[:half, :length], turned[half:, length:]]).T
        dq = (dq.astype(BF).astype(F32) * half**-0.5).astype(BF)
        dz_ref[0] = dq
        dz_ref[1, 0:keys] = dk
        dz_ref[2, 0:keys] = dv
        if keys < length:
            dead = jnp.zeros((length - keys, pair), BF)
            dz_ref[1, keys:length] = dead
            dz_ref[2, keys:length] = dead
        db_ref[0:1] = jnp.sum(dq.astype(F32), axis=0, keepdims=True)
        db_ref[1:2] = jnp.sum(dv.astype(F32), axis=0, keepdims=True)

    live_blocks(live_len, length, back)


def attend_back_call(lens, qkv, dctx, lse, seqs, seq, dz, carry, deps):
    rows, width = dctx.shape
    length = rows // seqs
    pairs = H // 2
    pw = width // pairs
    at = lambda part: pl.BlockSpec((length, pw), lambda p: (seq, part * pairs + p))
    more = [carry] + ([] if dz is None else [dz]) + list(deps)
    return pl.pallas_call(
        lambda *r: attend_back_kernel(seq, *r),
        grid=(pairs,),
        in_specs=[
            SMEM,
            at(0),
            at(1),
            at(2),
            at(0),
            pl.BlockSpec((1, 2, length), lambda p: (seq * pairs + p, 0, 0)),
        ]
        + [ANY] * len(more),
        out_specs=[
            pl.BlockSpec((3, length, pw), lambda p: (0, seq, p)),
            pl.BlockSpec((2, pw), lambda p: (0, p)),
            ANY,
        ],
        out_shape=[
            jax.ShapeDtypeStruct((3, rows, width), BF),
            jax.ShapeDtypeStruct((2, width), F32),
            jax.ShapeDtypeStruct(carry.shape, carry.dtype),
        ],
        input_output_aliases={6: 2} if dz is None else {6: 2, 7: 0},
        compiler_params=params(),
        cost_estimate=cost(
            20 * H * length * length * (width // H), 6 << 20, H * length * length
        ),
        name="attend_back",
    )(lens, qkv, qkv, qkv, dctx, lse, *more)


def attn_grad_kernel(
    grid, per, npieces, me_ref, sums, db1, db_a, db_b, dz_hbm, x_hbm, gout_hbm, dres_hbm, *rest
):
    pieces = rest[:npieces]
    count = 8 if is_path(grid, per) else 2
    grads, (mine, others) = rest[-13 - count : -13], rest[-13:-11]
    stage, dz, x, gout, line, total, w = rest[-11:-4]
    isem, osem, wsem, dsem = rest[-4:]
    rows, width = x.shape
    me = me_ref[0]
    core = me & 1
    blocks = grid.devices // 4
    path = is_path(grid, per)
    loads = [pltpu.make_async_copy(gout_hbm, gout, isem.at[4])]
    loads += [pltpu.make_async_copy(x_hbm, x, isem.at[3])]
    loads += [pltpu.make_async_copy(dz_hbm.at[p], dz.at[p], isem.at[p]) for p in range(3)]
    for copy in loads:
        copy.start()
    load_total = pltpu.make_async_copy(dres_hbm, total, isem.at[5])
    load_total.start()
    start_natural(grid, me_ref, pieces, w, wsem, 0, 3 * blocks)

    db = db_a[...] + db_b[...]
    tail = 3 * width + FF
    line[:, 0:width] = db[0:1]
    line[:, width : 2 * width] = db[1:2]
    line[:, 2 * width : 3 * width] = sums[5:6]
    line[:, 3 * width : tail] = db1[...]
    for i, row in enumerate((2, 3, 4, 0, 1)):
        line[:, tail + i * width : tail + (i + 1) * width] = sums[row : row + 1]
    count = line.shape[1] // grid.devices
    blank = jnp.zeros((8, width), F32)
    first_row = lax.broadcasted_iota(jnp.int32, (8, count), 0) == 0
    for d in range(grid.devices):
        values = jnp.where(first_row, line[:, d * count : (d + 1) * count], 0.0)
        values = jnp.concatenate([values, blank[:, count:]], axis=1).astype(BF)
        if path:
            stage[d, per : per + 8] = values
        else:
            grads[1][d] = values

    copies = []

    def emit(part, value):
        value = value.astype(BF)
        if not path:
            grads[0][part * width : (part + 1) * width, :] = value
            return
        stage[part * blocks : (part + 1) * blocks, 0:per] = value.reshape(blocks, per, width)
        iz = part ^ me // blocks
        for label in range(blocks):
            other, side_x, side_y = label & 1, label // 2 % 2, label // 4
            block = part * blocks + (label ^ (me & (blocks - 1)))
            copies.append(
                start_store(
                    core, stage.at[block], grads, side_x, side_y, other, iz, osem.at[part * blocks + label]
                )
            )

    loads[0].wait()
    emit(3, gout[...])
    loads[1].wait()
    for part in range(3):
        loads[2 + part].wait()
        emit(part, tn(dz[part], x[...]))
    load_total.wait()
    for part in range(3):
        wait_natural(grid, pieces, w, wsem, part * blocks, blocks, 0, 3 * blocks)
        total[...] += nn(dz[part], w[part * width : (part + 1) * width, :])
    for copy in store_sequences(me_ref, total, mine, others, dsem) + copies:
        copy.wait()


def attn_grad_call(grid, me, dz, x, gout, dres, vectors, pieces, per, shape, deps):
    rows, width = x.shape
    paths = path_shapes(grid, grid.devices, per, width)
    path = is_path(grid, per)
    if path:
        paths = [jax.ShapeDtypeStruct((p.shape[0], per + 8, width), BF) for p in paths]
    return pl.pallas_call(
        lambda *r: attn_grad_kernel(grid, per, len(pieces), *r),
        in_specs=[SMEM] + [VMEM] * len(vectors) + [ANY] * (4 + len(pieces) + len(deps)),
        out_specs=[ANY if path else VMEM] * len(paths) + [ANY, ANY],
        out_shape=paths
        + [
            jax.ShapeDtypeStruct(shape, F32),
            jax.ShapeDtypeStruct((shape[0] // 2,) + shape[1:], F32),
        ],
        scratch_shapes=[
            pltpu.VMEM((grid.devices, per + 8, width), BF),
            pltpu.VMEM((3, rows, width), BF),
            pltpu.VMEM((rows, width), BF),
            pltpu.VMEM((width, width), BF),
            pltpu.VMEM((1, 8 * width + FF), F32),
            pltpu.VMEM((rows, width), F32),
            pltpu.VMEM((3 * width, width), BF),
            pltpu.SemaphoreType.DMA((6,)),
            pltpu.SemaphoreType.DMA((grid.devices,)),
            pltpu.SemaphoreType.DMA((grid.devices,)),
            pltpu.SemaphoreType.DMA((shape[0],)),
        ],
        compiler_params=params(),
        cost_estimate=cost(6 * rows * width * width, 28 << 20),
        name="attn_grad",
    )(me, *vectors, dz, x, gout, dres, *pieces, *deps)


def gate(value, deps):
    return pl.pallas_call(
        lambda *r: None,
        in_specs=[ANY] * (1 + len(deps)),
        out_specs=ANY,
        out_shape=jax.ShapeDtypeStruct(value.shape, value.dtype),
        input_output_aliases={0: 0},
        compiler_params=params(),
        cost_estimate=cost(0, 0),
        name="gate",
    )(value, *deps)


def ordered_stack_kernel(count, *rest):
    for i in range(count):
        rest[-1][i] = rest[i][...]


def ordered_stack(parts, deps):
    return pl.pallas_call(
        lambda *r: ordered_stack_kernel(len(parts), *r),
        in_specs=[VMEM] * len(parts) + [ANY] * len(deps),
        out_specs=VMEM,
        out_shape=jax.ShapeDtypeStruct((len(parts),) + parts[0].shape, parts[0].dtype),
        compiler_params=params(),
        name="ordered_stack",
    )(*parts, *deps)


def adam_update(master, moment, second, grad, rate):
    moment_new = decay_rate * moment + (1.0 - decay_rate) * grad
    second_new = decay_rate * second + (1.0 - decay_rate) * grad * grad
    correction = 1.0 - decay_rate**STEP
    direction = moment_new / correction / (jnp.sqrt(second_new / correction) + adam_epsilon)
    master_new = master - rate * (direction + weight_decay * master)
    return (moment_new, second_new, master_new)


def join_sequences(mine, others, places):
    for s in range(others.shape[0]):
        mine = lax.dynamic_update_slice(mine, others[s : s + 1], (places[s], 0, 0))
    return mine


def share_sequences(lengths, core):
    count = lengths.shape[0]
    number = jnp.arange(count)
    longer = (lengths[None, :] > lengths[:, None]) | (
        (lengths[None, :] == lengths[:, None]) & (number[None, :] < number[:, None])
    )
    rank = jnp.sum(longer.astype(jnp.int32), axis=1)
    by_rank = jnp.sum((rank[None, :] == number[:, None]) * number[None, :], axis=1)
    sides = [[r for r in range(count) if (r + 1) // 2 % 2 == c] for c in (0, 1)]
    first, second = (jnp.stack([by_rank[r] for r in side]) for side in sides)
    mine = jnp.where(core == 0, first, second).astype(jnp.int32)
    other = jnp.where(core == 0, second, first).astype(jnp.int32)
    return mine, other


def local(
    tokens,
    cotangent,
    seq_lengths,
    slot_order,
    attn_weights,
    attn_moment,
    attn_second,
    ffn_weights,
    ffn_moment,
    ffn_second,
    vectors,
    vector_moment,
    vector_second,
):
    grid = Grid(lax.axis_size("dp"))
    core = lax.axis_index("seq")
    shard_index = lax.axis_index(AXES)
    me = shard_index.astype(jnp.int32).reshape(1)
    seq_count, half_len, width = tokens.shape
    seqs = seq_count // 2
    length = 2 * half_len
    rows = seqs * length
    per, ffn_per = attn_weights.shape[1], ffn_weights.shape[1]
    vec_per = vectors.shape[0]
    path = is_path(grid, per) and is_path(grid, ffn_per)

    slot_pick = (slot_order[0][:, None] == jnp.arange(seq_count)[None, :]).astype(jnp.int32)
    slot_len = jnp.sum(slot_pick * seq_lengths[0][None, :], axis=1)
    taken, left = share_sequences(slot_len, core)
    lens = jnp.sum((taken[:, None] == jnp.arange(seq_count)[None, :]) * slot_len[None, :], axis=1)
    me = jnp.concatenate([me, taken])

    vec_rows = jnp.zeros((8, width), BF)
    vec_rows = lax.dynamic_update_slice(vec_rows, vectors.astype(BF)[None, :], (0, 0))
    attn_block = jnp.concatenate([attn_weights.astype(BF).T, vec_rows])

    other_core = lambda value: permute(value, grid, lambda c: 1)
    tokens_other = other_core(tokens)
    if path:
        attn_parts = gather_z(grid, attn_block)
        ffn_block = ffn_weights.astype(BF).T
        ffn_parts = gather_z(grid, ffn_block)
        attn_z = ordered_stack(attn_parts, [ffn_block])
        attn_two = gather_two(grid, attn_z)
        attn_two = attn_two[:1] + [gate(t, ffn_parts[1:2]) for t in attn_two[1:]]
        attn_three = gather_three(grid, attn_two)
        ffn_z = ordered_stack(ffn_parts, attn_two[1:])
        ffn_two = gather_two(grid, ffn_z)
        weights = with_core(grid, attn_two + attn_three, [ffn_z])
        vec = natural_vectors(grid, weights, core, me[0], per, vec_per)
    else:
        whole_rows = lambda block: [lax.all_gather(block, AXES, axis=0, tiled=True)]
        weights = whole_rows(attn_block[:per])
        ffn_pieces = whole_rows(ffn_weights.astype(BF).T)
        ffn_two = []
        vec = lax.all_gather(attn_block[per:], AXES)[:, 0, :vec_per].reshape(1, -1).astype(F32)
    dy_other = other_core(cotangent)

    qkv, x = qkv_call(grid, me, vec, tokens, tokens_other, weights)
    fwd = attend_call(grid, me, lens, qkv, x, vec, weights, seqs, 0, [], [])
    ffn_two = ffn_two[:1] + [gate(t, fwd[:1]) for t in ffn_two[1:]]
    fwd = attend_call(grid, me, lens, qkv, x, vec, weights, seqs, 1, fwd, ffn_two[1:])
    ctx, lse, normed, inv, hidden = fwd
    if path:
        ffn_three = gather_three(grid, ffn_two)
        ffn_three = ffn_three[:1] + [gate(t, fwd[:1]) for t in ffn_three[1:]]
        ffn_pieces = with_core(grid, ffn_two + ffn_three, [])
    out, out_other, dres_one, datt, sums, db1, *grads_f = ffn_call(
        grid, me, vec, inv, hidden, normed, cotangent, dy_other, ffn_pieces, ffn_per
    )
    layer_out = join_sequences(out, other_core(out_other), left)

    sums_f = Sums(grid, path, grads_f)
    sends = sums_f.add_core()
    dctx, gout = out_back_call(grid, me, datt, ctx, weights, sends)
    dz, db_a, sums_f.keep[1] = attend_back_call(
        lens, qkv, dctx, lse, seqs, 0, None, sums_f.keep[1], sends
    )
    sends = sums_f.add_three()
    dz, db_b, sums_f.keep[0] = attend_back_call(
        lens, qkv, dctx, lse, seqs, 1, dz, sums_f.keep[0], sends
    )
    sends = sums_f.add_two()
    *grads_c, dx, dx_other = attn_grad_call(
        grid, me, dz, x, gout, dres_one, [sums, db1, db_a, db_b], weights, per, tokens.shape, sends
    )
    if path:
        grads_c[7] = gate(grads_c[7], sums_f.z[1:2])
    sums_c = Sums(grid, path, grads_c)
    sums_c.add_core()
    ffn_sum = sums_f.add_z()
    sums_c.add_three()
    sums_c.keep[0] = gate(sums_c.keep[0], [ffn_sum])
    input_grad = join_sequences(dx, other_core(dx_other), left)
    sums_c.add_two()
    attn_sum = sums_c.add_z()

    vector_sum = attn_sum[per, :vec_per]
    attn_sum = attn_sum[:per].T
    ffn_sum = ffn_sum[:ffn_per].T

    attn_cols = shard_index * per + jnp.arange(per)
    attn_rate = jnp.where(
        attn_cols < 2 * width, math.sqrt(2.0), jnp.where(attn_cols < 3 * width, 1.5, 1.8)
    ) * width ** (-0.5)
    ffn_cols = shard_index * ffn_per + jnp.arange(ffn_per)
    ffn_rate = jnp.where(ffn_cols < FF, width ** (-0.5), 1.5 * FF ** (-0.5))
    attn_m, attn_v, attn_new = adam_update(
        attn_weights, attn_moment, attn_second, attn_sum, attn_rate[None, :]
    )
    ffn_m, ffn_v, ffn_new = adam_update(
        ffn_weights, ffn_moment, ffn_second, ffn_sum, ffn_rate[None, :]
    )
    vec_m, vec_v, vec_new = adam_update(
        vectors, vector_moment, vector_second, vector_sum, vector_rate
    )
    return (
        layer_out,
        input_grad,
        attn_m,
        attn_v,
        attn_new,
        attn_new.astype(BF),
        ffn_m,
        ffn_v,
        ffn_new,
        ffn_new.astype(BF),
        vec_m,
        vec_v,
        vec_new,
        vec_new.astype(BF),
    )


def solution(mesh):
    columns = P(None, AXES)
    flat = P(AXES)
    rows = P("dp", "seq", None)
    placed = (rows, rows, P("dp", None), P("dp", None)) + (columns,) * 6 + (flat,) * 3
    return jax.shard_map(
        local,
        mesh=mesh,
        in_specs=placed,
        out_specs=(rows, rows) + (columns,) * 8 + (flat,) * 4,
        check_vma=False,
    )
```

```python
import math

import jax
import jax.numpy as jnp
from jax import lax
from jax.experimental import pallas as pl
from jax.experimental.pallas import tpu as pltpu
from jax.sharding import PartitionSpec as P

H = 12
FF = 3072
STEP = 5

epsilon = 1e-06
masked_score = -1e30
decay_rate = 0.5
adam_epsilon = 1e-08
weight_decay = 0.01
vector_rate = 0.5

AXES = ("dp", "seq")
BF = jnp.bfloat16
F32 = jnp.float32
VMEM_LIMIT = 56 * 1024 * 1024
TILE = 256
COST = 16
ANY = pl.BlockSpec(memory_space=pl.ANY)
SMEM = pl.BlockSpec(memory_space=pltpu.SMEM)
VMEM = pl.BlockSpec(memory_space=pltpu.VMEM)


def nn(a, b):
    return lax.dot_general(a, b, (((1,), (0,)), ((), ())), preferred_element_type=F32)


def nt(a, b):
    return lax.dot_general(a, b, (((1,), (1,)), ((), ())), preferred_element_type=F32)


def tn(a, b):
    return lax.dot_general(a, b, (((0,), (0,)), ((), ())), preferred_element_type=F32)


class Grid:
    def __init__(self, chips):
        power = chips.bit_length() - 1
        if 1 << power == chips:
            self.side = 1 << (power // 3)
            self.nz = chips // (self.side * self.side)
        else:
            self.side, self.nz = 1, chips
        self.devices = 2 * chips
        self.xor = 1 << power == chips

    def z_mask(self, m):
        return m * 2 * self.side * self.side

    def x_mask(self, m):
        return 2 * m

    def y_mask(self, m):
        return 2 * m * self.side

    def label(self, core, other, i3, i2, iz):
        x = jnp.where(core == 0, i2, i3)
        y = jnp.where(core == 0, i3, i2)
        return self.z_mask(iz) + self.y_mask(y) + self.x_mask(x) + other


def permute(value, grid, mask_of_core):
    pairs = [(i, i ^ mask_of_core(i & 1)) for i in range(grid.devices)]
    return lax.ppermute(value, AXES, pairs)


def along_two(grid, value, m):
    return permute(value, grid, lambda c: grid.x_mask(m) if c == 0 else grid.y_mask(m))


def along_three(grid, value, m):
    return permute(value, grid, lambda c: grid.y_mask(m) if c == 0 else grid.x_mask(m))


def gather_z(grid, block):
    return [block] + [permute(block, grid, lambda c: grid.z_mask(m)) for m in range(1, grid.nz)]


def gather_two(grid, zed):
    return [zed] + [along_two(grid, zed, m) for m in range(1, grid.side)]


def gather_three(grid, two):
    return [along_three(grid, t, m) for m in range(1, grid.side) for t in two]


def with_core(grid, own, deps):
    own = [gate(own[0], deps) if deps else own[0]] + own[1:]
    return own + [permute(p, grid, lambda c: 1) for p in own]


def is_path(grid, rows):
    return grid.side == 2 and grid.nz == 4 and rows % 16 == 0


def slot_of(grid, label, core):
    other = label & 1
    x = (label // 2) & (grid.side - 1)
    y = (label // (2 * grid.side)) & (grid.side - 1)
    z = label // (2 * grid.side * grid.side)
    first = (core ^ other) == 0
    i2 = jnp.where(first, x, y)
    i3 = jnp.where(first, y, x)
    return other, (i3 * grid.side + i2) * grid.nz + z


def natural_vectors(grid, pieces, core, me, row, count):
    side, nz = grid.side, grid.nz
    table = jnp.stack([p[:, row, :count] for p in pieces]).reshape(2, side, side, nz, count)
    turned = jnp.swapaxes(table, 1, 2)
    first = jnp.stack([table[0], turned[1]])
    second = jnp.stack([turned[0], table[1]])
    value = jnp.where(core == 0, first, second)
    value = jnp.transpose(value, (3, 1, 2, 0, 4)).reshape(grid.devices, count)
    bit = 1
    while bit < grid.devices:
        pairs = value.reshape(-1, 2, bit, count)
        value = jnp.where((me & bit) == 0, pairs, pairs[:, ::-1]).reshape(grid.devices, count)
        bit *= 2
    return value.reshape(1, -1).astype(F32)


def start_natural(grid, me_ref, pieces, dest, sems, first=0, last=None, order=None):
    last = grid.devices if last is None else last
    rows = dest.shape[0] // (last - first)
    if len(pieces) == 1:
        pltpu.make_async_copy(
            pieces[0].at[pl.ds(first * rows, (last - first) * rows)], dest, sems.at[0]
        ).start()
        return
    me = me_ref[0]
    core = me & 1
    side, nz = grid.side, grid.nz
    for label in sorted(range(grid.devices), key=order or (lambda j: j // (2 * side * side))):
        other, x, y = label & 1, label // 2 % side, label // (2 * side) % side
        iz = label // (2 * side * side)
        block = me ^ label

        def start(ref, block=block, iz=iz):
            row = pl.multiple_of((block - first) * rows, rows)
            pltpu.make_async_copy(
                ref.at[iz, pl.ds(0, rows)], dest.at[pl.ds(row, rows)], sems.at[block]
            ).start()

        def either(other=other, x=x, y=y, start=start):
            one = pieces[(other * side + y) * side + x]
            two = pieces[(other * side + x) * side + y]
            if x == y:
                start(one)
            else:
                pl.when((core ^ other) == 0)(lambda: start(one))
                pl.when((core ^ other) != 0)(lambda: start(two))

        if last - first == grid.devices:
            either()
        else:
            pl.when((block >= first) & (block < last))(either)


def wait_natural(grid, pieces, dest, sems, begin, count, first=0, last=None):
    last = grid.devices if last is None else last
    rows = dest.shape[0] // (last - first)
    if len(pieces) == 1:

        @pl.when(begin == first)
        def _():
            pltpu.make_async_copy(
                pieces[0].at[pl.ds(first * rows, (last - first) * rows)], dest, sems.at[0]
            ).wait()

        return
    for i in range(count):
        block = begin + i
        pltpu.make_async_copy(
            pieces[0].at[0, pl.ds(0, rows)],
            dest.at[pl.ds(pl.multiple_of((block - first) * rows, rows), rows)],
            sems.at[block],
        ).wait()


def path_shapes(grid, blocks, per, width):
    if not is_path(grid, per):
        return [
            jax.ShapeDtypeStruct((blocks * per, width), BF),
            jax.ShapeDtypeStruct((blocks, 8, width), BF),
        ]
    return [jax.ShapeDtypeStruct((grid.nz, per, width), BF)] * 8


def start_store(core, src, dests, x, y, other, iz, sem):
    one, two = (dests[4 * other + k].at[iz] for k in (2 * y + x, 2 * x + y))
    copy = pltpu.make_async_copy(src, one, sem)
    if x == y:
        copy.start()
    else:
        pl.when((core ^ other) == 0)(lambda: copy.start())
        pl.when((core ^ other) != 0)(lambda: pltpu.make_async_copy(src, two, sem).start())
    return copy


class Sums:
    def __init__(self, grid, path, blocks):
        self.grid, self.path = grid, path
        self.three, self.two, self.z = [], [], []
        if path:
            self.keep = list(blocks[:4])
            got = {k: permute(blocks[4 + k], grid, lambda c: 1) for k in (3, 2, 1, 0)}
            self.core = [got[k] for k in range(4)]
        else:
            self.keep = list(blocks)

    def terms(self, i3, i2, iz):
        grid = self.grid
        at = i3 * grid.side + i2
        total = self.keep[at][iz].astype(F32) + self.core[at][iz].astype(F32)
        if i3 == 0:
            for there, got in self.three:
                if there == i2:
                    total = total + got[iz].astype(F32)
            if i2 == 0:
                for got in self.two:
                    total = total + got[iz].astype(F32)
        return total

    def add_core(self):
        if not self.path:
            return []
        grid = self.grid
        every = slice(0, grid.nz)
        sends = [
            (i2, m, self.terms(m, i2, every).astype(BF))
            for i2 in reversed(range(grid.side))
            for m in range(1, grid.side)
        ]
        self.three = [(i2, along_three(grid, value, m)) for i2, m, value in sends]
        return [value for _, _, value in sends]

    def add_three(self):
        if not self.path:
            return []
        grid = self.grid
        every = slice(0, grid.nz)
        sends = [self.terms(0, m, every).astype(BF) for m in range(1, grid.side)]
        self.two = [along_two(grid, sends[m - 1], m) for m in range(1, grid.side)]
        return sends

    def add_two(self):
        if not self.path:
            return []
        grid = self.grid
        sends = [self.terms(0, 0, slice(m, m + 1))[0].astype(BF) for m in range(1, grid.nz)]
        self.z = [
            permute(sends[m - 1], grid, lambda c: grid.z_mask(m)) for m in range(1, grid.nz)
        ]
        return sends

    def add_z(self):
        if not self.path:
            rows = [v.reshape(-1, v.shape[-1]).astype(F32) for v in self.keep]
            return jnp.concatenate(
                [lax.psum_scatter(v, AXES, scatter_dimension=0, tiled=True) for v in rows]
            )
        total = self.terms(0, 0, slice(0, 1))[0]
        for got in self.z:
            total = total + got.astype(F32)
        return total


def params(**more):
    return pltpu.CompilerParams(vmem_limit_bytes=VMEM_LIMIT, **more)


def cost(macs, bytes_accessed, trans=0):
    return pl.CostEstimate(
        flops=2 * macs // COST, bytes_accessed=bytes_accessed // COST, transcendentals=trans // COST
    )


def rows_spec(width, tile=TILE):
    return pl.BlockSpec((tile, width), lambda i: (i, 0))


def whole(shape):
    zeros = (0,) * len(shape)
    return pl.BlockSpec(shape, lambda *i: zeros)


def fixed(*shape):
    zeros = (0,) * len(shape)
    return pl.BlockSpec(shape, lambda i: zeros)


def norm_rows(values):
    center = values - jnp.mean(values, axis=-1, keepdims=True)
    inverse = lax.rsqrt(jnp.mean(center * center, axis=-1, keepdims=True) + epsilon)
    return center * inverse, inverse


def norm_back(upstream, normed, inverse, gain):
    u = upstream * gain
    centered = u - jnp.mean(u, axis=-1, keepdims=True)
    return inverse * (centered - normed * jnp.mean(u * normed, axis=-1, keepdims=True))


def gelu_pair(u):
    phi = 0.5 + 0.5 * lax.erf(u * math.sqrt(0.5))
    density = jnp.exp(-0.5 * (u * u))
    return u * phi, phi + (u * (1.0 / math.sqrt(2.0 * math.pi))) * density


def load_sequences(me_ref, mine, others, dest, sems):
    count = mine.shape[0] // 2
    half = mine.shape[1]
    core = me_ref[0] & 1
    copies = []
    for s in range(count):
        seq = me_ref[1 + s]
        for i, src in enumerate((mine, others)):
            at = s * 2 * half + (core ^ i) * half
            copies.append(
                pltpu.make_async_copy(
                    src.at[seq], dest.at[pl.ds(pl.multiple_of(at, half), half)], sems.at[2 * s + i]
                )
            )
    for copy in copies:
        copy.start()
    return copies


def store_sequences(me_ref, src, mine, others, sems):
    count, half = others.shape[0], others.shape[1]
    core = me_ref[0] & 1
    copies = []
    for s in range(count):
        for i, dest in enumerate((mine.at[me_ref[1 + s]], others.at[s])):
            at = s * 2 * half + (core ^ i) * half
            copies.append(
                pltpu.make_async_copy(
                    src.at[pl.ds(pl.multiple_of(at, half), half)], dest, sems.at[2 * s + i]
                )
            )
    for copy in copies:
        copy.start()
    return copies


def quarter_order(grid, me_ref, pieces, i):
    if len(pieces) == 1:
        return i
    lines = grid.nz // 4
    return (i * lines ^ me_ref[0] // (2 * grid.side * grid.side)) // lines


def qkv_kernel(grid, me_ref, vec_ref, mine, others, *rest):
    pieces, (out_hbm, x_hbm, w, x, out, wsem, xsem, osem) = rest[:-8], rest[-8:]
    rows, width = x.shape
    loads = load_sequences(me_ref, mine, others, x, xsem)
    blocks = grid.devices // 4
    start_natural(grid, me_ref, pieces, w, wsem, 0, 3 * blocks)
    for copy in loads:
        copy.wait()
    copy_x = pltpu.make_async_copy(x, x_hbm, osem.at[3])
    copy_x.start()

    def store(part):
        cols = pl.ds(pl.multiple_of(part * width, width), width)
        return pltpu.make_async_copy(out.at[:, cols], out_hbm.at[:, cols], osem.at[part])

    @pl.loop(0, 4)
    def _(i):
        part = quarter_order(grid, me_ref, pieces, i)

        @pl.when(part < 3)
        def _():
            wait_natural(grid, pieces, w, wsem, part * blocks, blocks, 0, 3 * blocks)
            cols = pl.ds(pl.multiple_of(part * width, width), width)
            bias = vec_ref[:, pl.ds(pl.multiple_of(part // 2 * width, width), width)]
            bias = jnp.where(part == 1, 0.0, bias)
            scale = jnp.where(part == 0, (width // H) ** -0.5, 1.0)
            out[:, cols] = ((nt(x[...], w[cols, :]) + bias) * scale).astype(BF)
            store(part).start()

    for part in range(3):
        store(part).wait()
    copy_x.wait()


def qkv_call(grid, me, vec, mine, others, pieces):
    width = mine.shape[2]
    rows = mine.shape[0] * mine.shape[1]
    return pl.pallas_call(
        lambda *r: qkv_kernel(grid, *r),
        in_specs=[SMEM, VMEM, ANY, ANY] + [ANY] * len(pieces),
        out_specs=[ANY, ANY],
        out_shape=[
            jax.ShapeDtypeStruct((rows, 3 * width), BF),
            jax.ShapeDtypeStruct((rows, width), BF),
        ],
        scratch_shapes=[
            pltpu.VMEM((3 * width, width), BF),
            pltpu.VMEM((rows, width), BF),
            pltpu.VMEM((rows, 3 * width), BF),
            pltpu.SemaphoreType.DMA((grid.devices,)),
            pltpu.SemaphoreType.DMA((mine.shape[0],)),
            pltpu.SemaphoreType.DMA((4,)),
        ],
        compiler_params=params(),
        cost_estimate=cost(rows * width * 3 * width, 12 << 20),
        name="qkv",
    )(me, vec, mine, others, *pieces)


def vector_refs(vec_ref, width):
    tail = 3 * width + FF
    found = [vec_ref[:, 2 * width : 3 * width], vec_ref[:, 3 * width : tail]]
    return found + [vec_ref[:, tail + i * width : tail + (i + 1) * width] for i in range(5)]


def live_blocks(live_len, length, body):
    size = min(128, length)
    count = (live_len + (size - 1)) // size
    for n in range(1, length // size + 1):
        pl.when(count == n)(lambda n=n: body(n * size))


def attend_kernel(grid, npieces, seq, len_ref, me_ref, q_ref, k_ref, v_ref, x_ref, vec_ref, *rest):
    pieces = rest[:npieces]
    quarter = grid.devices // 4
    ctx_ref, lse_ref, normed_ref, inv_ref, hid_ref, w, sems = rest[-7:]
    turn = pl.program_id(0)

    @pl.when(turn == 0)
    def _():
        start_natural(grid, me_ref, pieces, w, sems, 3 * quarter)

    live_len = len_ref[seq]
    length, pair = q_ref.shape
    half = pair // 2

    def attend(keys):
        q, k, v = q_ref[...], k_ref[0:keys, :], v_ref[0:keys, :]
        lane = lax.broadcasted_iota(jnp.int32, (length, pair), 1)
        live = lax.broadcasted_iota(jnp.int32, (1, keys), 1) < live_len
        outs, stats = [], []
        for h in (0, 1):
            mine = (lane >= half) if h else (lane < half)
            s = nt(jnp.where(mine, q, jnp.zeros_like(q)), k)
            s = jnp.where(live, s, masked_score)
            top = jnp.max(s, axis=-1, keepdims=True)
            p = jnp.exp(s - top)
            total = jnp.sum(p, axis=-1, keepdims=True)
            outs.append(nn(p.astype(BF), v) / total)
            stats.append(top + jnp.log(total))
        ctx = jnp.where(lane < half, outs[0], outs[1]).astype(BF)
        ctx_ref[:, pl.ds(pl.multiple_of(turn * pair, pair), pair)] = ctx
        turned = jnp.where(lane < half, stats[0], stats[1]).T
        lse_ref[0] = jnp.concatenate([turned[0:1], turned[half : half + 1]], axis=0)

    live_blocks(live_len, length, attend)

    @pl.when(turn == pl.num_programs(0) - 1)
    def _():
        wait_natural(grid, pieces, w, sems, 3 * quarter, quarter, 3 * quarter)
        bo, _, _, g1, e1, _, _ = vector_refs(vec_ref, x_ref.shape[1])
        r = x_ref[...].astype(F32) + (nt(ctx_ref[...], w[...]) + bo)
        normed, inverse = norm_rows(r)
        normed_ref[...] = normed
        inv_ref[...] = inverse
        hid_ref[...] = (normed * g1 + e1).astype(BF)


def attend_call(grid, me, lens, qkv, x, vec, pieces, seqs, seq, before, deps):
    rows, width = x.shape
    length = rows // seqs
    pairs = H // 2
    pw = width // pairs
    at = lambda part: pl.BlockSpec((length, pw), lambda p: (seq, part * pairs + p))
    seq_rows = lambda w: pl.BlockSpec((length, w), lambda p: (seq, 0))
    first = 7 + len(pieces)
    return pl.pallas_call(
        lambda *r: attend_kernel(grid, len(pieces), seq, *r),
        grid=(pairs,),
        in_specs=[SMEM, SMEM, at(0), at(1), at(2), seq_rows(width), whole(vec.shape)]
        + [ANY] * (len(pieces) + len(before) + len(deps)),
        out_specs=[
            seq_rows(width),
            pl.BlockSpec((1, 2, length), lambda p: (seq * pairs + p, 0, 0)),
            seq_rows(width),
            seq_rows(1),
            seq_rows(width),
        ],
        out_shape=[
            jax.ShapeDtypeStruct((rows, width), BF),
            jax.ShapeDtypeStruct((seqs * pairs, 2, length), F32),
            jax.ShapeDtypeStruct((rows, width), F32),
            jax.ShapeDtypeStruct((rows, 1), F32),
            jax.ShapeDtypeStruct((rows, width), BF),
        ],
        scratch_shapes=[
            pltpu.VMEM((width, width), BF),
            pltpu.SemaphoreType.DMA((grid.devices,)),
        ],
        input_output_aliases={first + i: i for i in range(len(before))},
        compiler_params=params(),
        cost_estimate=cost(8 * H * length * length * (width // H), 9 << 20, H * length * length),
        name="attend",
    )(lens, me, qkv, qkv, qkv, x, vec, *pieces, *before, *deps)


PARTS = 4


def ffn_kernel(grid, per, me_ref, vec_ref, inv_ref, h_hbm, normed_hbm, dy_mine, dy_others, *rest):
    npieces = len(rest) - 22 - (8 if is_path(grid, per) else 2)
    pieces = rest[:npieces]
    out_mine, out_others, dres_hbm, datt_hbm, sums_ref, db1_ref = rest[npieces : npieces + 6]
    grads = rest[npieces + 6 : -16]
    (w, h, normed, dy, act, gp, acc, dres, dbr, out, dpre, stage, wsem, isem, osem, dsem) = rest[-16:]
    rows, width = h.shape
    units = w.shape[0] // 2
    size = units // PARTS
    tiles = rows // TILE
    me = me_ref[0]
    core = me & 1

    _, _, b2, g1, e1, g2, e2 = vector_refs(vec_ref, width)
    loads = [
        pltpu.make_async_copy(src, dst, isem.at[i])
        for i, (src, dst) in enumerate(((h_hbm, h), (normed_hbm, normed)))
    ]
    loads[0].start()
    half = grid.devices // 2
    start_natural(grid, me_ref, pieces, w, wsem, order=lambda j: (j % half // (half // PARTS), j))
    loads[1].start()
    loads += load_sequences(me_ref, dy_mine, dy_others, dy, dsem)
    loads[0].wait()

    def tile(r):
        return pl.ds(pl.multiple_of(r * TILE, TILE), TILE)

    def natural_part(part):
        if len(pieces) == 1:
            return part
        return part ^ (me % half // (half // PARTS))

    def span(start, count):
        return pl.ds(pl.multiple_of(start, count), count)

    for part in range(PARTS):
        there = natural_part(part)
        for base in (0, half):
            wait_natural(
                grid, pieces, w, wsem, base + there * (half // PARTS), half // PARTS
            )
        here = slice(part * size, (part + 1) * size)
        up, down = span(there * size, size), span(units + there * size, size)
        a, slope = gelu_pair(nt(h[...], w[up, :]) + vec_ref[:, span(3 * width + there * size, size)])
        a = a.astype(BF)
        act[:, here] = a
        gp[:, here] = slope.astype(BF)
        more = nn(a, w[down, :])
        if part == 0:
            acc[...] = more
        else:
            acc[...] += more

    for copy in loads[1:]:
        copy.wait()
    sums_ref[...] = jnp.zeros_like(sums_ref)

    @pl.loop(0, tiles)
    def _(r):
        at = tile(r)
        hidden = normed[at, :] * g1 + e1
        value = hidden + (acc[at, :] + b2)
        n, inverse = norm_rows(value)
        out[at, :] = (n * g2 + e2).astype(BF)
        up = dy[at, :].astype(F32)
        d = norm_back(up, n, inverse, g2)
        low = d.astype(BF)
        dres[at, :] = d
        dbr[at, :] = low
        sums_ref[0:1] += jnp.sum(up * n, axis=0, keepdims=True)
        sums_ref[1:2] += jnp.sum(up, axis=0, keepdims=True)
        sums_ref[2:3] += jnp.sum(low.astype(F32), axis=0, keepdims=True)

    out_copies = store_sequences(me_ref, out, out_mine, out_others, dsem)

    path = is_path(grid, per)
    blocks = size // per
    pending = [[], []]

    def emit(part, side, value):
        slot, there = part % 2, natural_part(part)
        stage[slot, side] = value
        if not path:
            copy = pltpu.make_async_copy(
                stage.at[slot, side],
                grads[0].at[span(side * units + there * size, size)],
                osem.at[slot, side, 0],
            )
            copy.start()
            pending[slot].append(copy)
            return
        spread = 2 * grid.side * grid.side
        iz = (side * half ^ me & half) // spread + part // 2
        for x in (0, 1):
            for other in (0, 1):
                label = 2 * x + other
                here = label ^ (me & 3)
                src = stage.at[slot, side, pl.ds(pl.multiple_of(here * per, per), per)]
                pending[slot].append(
                    start_store(core, src, grads, x, part % 2, other, iz, osem.at[slot, side, label])
                )

    for part in range(PARTS):
        there = natural_part(part)
        here = slice(part * size, (part + 1) * size)
        up, down = span(there * size, size), span(units + there * size, size)
        d = (nt(dbr[...], w[down, :]) * gp[:, here].astype(F32)).astype(BF)
        dpre[...] = d
        db1_ref[:, span(there * size, size)] = jnp.sum(d.astype(F32), axis=0, keepdims=True)
        more = nn(d, w[up, :])
        if part == 0:
            acc[...] = more
        else:
            acc[...] += more
        for copy in pending[part % 2]:
            copy.wait()
        pending[part % 2] = []
        emit(part, 0, tn(dpre[...], h[...]).astype(BF))
        emit(part, 1, tn(act[:, here], dbr[...]).astype(BF))

    def stores(r):
        return [
            pltpu.make_async_copy(dres.at[tile(r)], dres_hbm.at[tile(r)], isem.at[1]),
            pltpu.make_async_copy(out.at[tile(r)], datt_hbm.at[tile(r)], isem.at[2]),
        ]

    for copy in out_copies:
        copy.wait()

    @pl.loop(0, tiles)
    def _(r):
        at = tile(r)
        dhid = dres[at, :] + acc[at, :]
        n = normed[at, :]
        d = norm_back(dhid, n, inv_ref[at, :], g1)
        low = d.astype(BF)
        dres[at, :] = d
        out[at, :] = low
        sums_ref[3:4] += jnp.sum(dhid * n, axis=0, keepdims=True)
        sums_ref[4:5] += jnp.sum(dhid, axis=0, keepdims=True)
        sums_ref[5:6] += jnp.sum(low.astype(F32), axis=0, keepdims=True)
        for copy in stores(r):
            copy.start()

    @pl.loop(0, tiles)
    def _(r):
        for copy in stores(r):
            copy.wait()

    for copy in pending[0] + pending[1]:
        copy.wait()


def ffn_call(grid, me, vec, inv, h, normed, dy_mine, dy_others, pieces, per):
    rows, width = h.shape
    total = grid.devices * per
    units = total // 2
    size = units // PARTS
    paths = path_shapes(grid, grid.devices, per, width)
    return pl.pallas_call(
        lambda *r: ffn_kernel(grid, per, *r),
        in_specs=[SMEM, VMEM, VMEM, ANY, ANY, ANY, ANY] + [ANY] * len(pieces),
        out_specs=[ANY, ANY, ANY, ANY, VMEM, VMEM] + [ANY] * len(paths),
        out_shape=[
            jax.ShapeDtypeStruct(dy_mine.shape, BF),
            jax.ShapeDtypeStruct((dy_mine.shape[0] // 2,) + dy_mine.shape[1:], BF),
            jax.ShapeDtypeStruct((rows, width), F32),
            jax.ShapeDtypeStruct((rows, width), BF),
            jax.ShapeDtypeStruct((8, width), F32),
            jax.ShapeDtypeStruct((1, units), F32),
        ]
        + paths,
        scratch_shapes=[
            pltpu.VMEM((total, width), BF),
            pltpu.VMEM((rows, width), BF),
            pltpu.VMEM((rows, width), F32),
            pltpu.VMEM((rows, width), BF),
            pltpu.VMEM((rows, units), BF),
            pltpu.VMEM((rows, units), BF),
            pltpu.VMEM((rows, width), F32),
            pltpu.VMEM((rows, width), F32),
            pltpu.VMEM((rows, width), BF),
            pltpu.VMEM((rows, width), BF),
            pltpu.VMEM((rows, size), BF),
            pltpu.VMEM((2, 2, size, width), BF),
            pltpu.SemaphoreType.DMA((grid.devices,)),
            pltpu.SemaphoreType.DMA((3,)),
            pltpu.SemaphoreType.DMA((2, 2, max(size // per, 2))),
            pltpu.SemaphoreType.DMA((dy_mine.shape[0],)),
        ],
        compiler_params=params(),
        cost_estimate=cost(6 * rows * width * units, 40 << 20, 2 * rows * units),
        name="ffn",
    )(me, vec, inv, h, normed, dy_mine, dy_others, *pieces)


def out_back_kernel(grid, npieces, me_ref, datt_hbm, ctx_hbm, *rest):
    pieces = rest[:npieces]
    dctx_hbm, grad_hbm, w, datt, ctx, dctx, grad, sems, isem, osem = rest[-10:]
    first = 3 * grid.devices // 4
    loads = [
        pltpu.make_async_copy(datt_hbm, datt, isem.at[0]),
        pltpu.make_async_copy(ctx_hbm, ctx, isem.at[1]),
    ]
    loads[0].start()
    start_natural(grid, me_ref, pieces, w, sems, first)
    loads[1].start()
    loads[0].wait()
    wait_natural(grid, pieces, w, sems, first, grid.devices - first, first)
    dctx[...] = nn(datt[...], w[...]).astype(BF)
    stores = [
        pltpu.make_async_copy(dctx, dctx_hbm, osem.at[0]),
        pltpu.make_async_copy(grad, grad_hbm, osem.at[1]),
    ]
    stores[0].start()
    loads[1].wait()
    grad[...] = tn(datt[...], ctx[...]).astype(BF)
    stores[1].start()
    for copy in stores:
        copy.wait()


def out_back_call(grid, me, datt, ctx, pieces, deps):
    rows, width = ctx.shape
    return pl.pallas_call(
        lambda *r: out_back_kernel(grid, len(pieces), *r),
        in_specs=[SMEM, ANY, ANY] + [ANY] * (len(pieces) + len(deps)),
        out_specs=[ANY, ANY],
        out_shape=[
            jax.ShapeDtypeStruct((rows, width), BF),
            jax.ShapeDtypeStruct((width, width), BF),
        ],
        scratch_shapes=[
            pltpu.VMEM((width, width), BF),
            pltpu.VMEM((rows, width), BF),
            pltpu.VMEM((rows, width), BF),
            pltpu.VMEM((rows, width), BF),
            pltpu.VMEM((width, width), BF),
            pltpu.SemaphoreType.DMA((grid.devices,)),
            pltpu.SemaphoreType.DMA((2,)),
            pltpu.SemaphoreType.DMA((2,)),
        ],
        compiler_params=params(),
        cost_estimate=cost(2 * rows * width * width, 12 << 20),
        name="out_back",
    )(me, datt, ctx, *pieces, *deps)


def attend_back_kernel(seq, len_ref, q_ref, k_ref, v_ref, d_ref, lse_ref, *rest):
    dz_ref, db_ref, _ = rest[-3:]
    live_len = len_ref[seq]
    length, pair = q_ref.shape
    half = pair // 2

    def back(keys):
        q, k, v, d = q_ref[...], k_ref[0:keys, :], v_ref[0:keys, :], d_ref[...]
        first = lax.broadcasted_iota(jnp.int32, (length, pair), 1) < half
        live = lax.broadcasted_iota(jnp.int32, (keys, 1), 0) < live_len
        zero = jnp.zeros_like(q)
        q2, d2 = (
            jnp.concatenate([jnp.where(first, t, zero), jnp.where(first, zero, t)]) for t in (q, d)
        )
        log_total = jnp.concatenate([lse_ref[0, 0:1, :], lse_ref[0, 1:2, :]], axis=1)
        p = jnp.where(live, jnp.exp(nt(k, q2) - log_total), 0.0)
        dp = nt(v, d2)
        inner = jnp.sum(p * dp, axis=0, keepdims=True)
        ds = (p * (dp - inner)).astype(BF)
        dv = nn(p.astype(BF), d2).astype(BF)
        dk = nn(ds, q2).astype(BF)
        turned = nn(k.T, ds)
        dq = jnp.concatenate([turned[:half, :length], turned[half:, length:]]).T
        dq = (dq.astype(BF).astype(F32) * half**-0.5).astype(BF)
        dz_ref[0] = dq
        dz_ref[1, 0:keys] = dk
        dz_ref[2, 0:keys] = dv
        if keys < length:
            dead = jnp.zeros((length - keys, pair), BF)
            dz_ref[1, keys:length] = dead
            dz_ref[2, keys:length] = dead
        db_ref[0:1] = jnp.sum(dq.astype(F32), axis=0, keepdims=True)
        db_ref[1:2] = jnp.sum(dv.astype(F32), axis=0, keepdims=True)

    live_blocks(live_len, length, back)


def attend_back_call(lens, qkv, dctx, lse, seqs, seq, dz, carry, deps):
    rows, width = dctx.shape
    length = rows // seqs
    pairs = H // 2
    pw = width // pairs
    at = lambda part: pl.BlockSpec((length, pw), lambda p: (seq, part * pairs + p))
    more = [carry] + ([] if dz is None else [dz]) + list(deps)
    return pl.pallas_call(
        lambda *r: attend_back_kernel(seq, *r),
        grid=(pairs,),
        in_specs=[
            SMEM,
            at(0),
            at(1),
            at(2),
            at(0),
            pl.BlockSpec((1, 2, length), lambda p: (seq * pairs + p, 0, 0)),
        ]
        + [ANY] * len(more),
        out_specs=[
            pl.BlockSpec((3, length, pw), lambda p: (0, seq, p)),
            pl.BlockSpec((2, pw), lambda p: (0, p)),
            ANY,
        ],
        out_shape=[
            jax.ShapeDtypeStruct((3, rows, width), BF),
            jax.ShapeDtypeStruct((2, width), F32),
            jax.ShapeDtypeStruct(carry.shape, carry.dtype),
        ],
        input_output_aliases={6: 2} if dz is None else {6: 2, 7: 0},
        compiler_params=params(),
        cost_estimate=cost(
            20 * H * length * length * (width // H), 6 << 20, H * length * length
        ),
        name="attend_back",
    )(lens, qkv, qkv, qkv, dctx, lse, *more)


def attn_grad_kernel(
    grid, per, me_ref, sums, db1, db_a, db_b, dz_hbm, x_hbm, gout_hbm, *rest
):
    count = 8 if is_path(grid, per) else 2
    grads, (stage, dz, x, gout, line, isem, osem) = rest[-7 - count : -7], rest[-7:]
    rows, width = x.shape
    me = me_ref[0]
    core = me & 1
    blocks = grid.devices // 4
    path = is_path(grid, per)
    loads = [pltpu.make_async_copy(gout_hbm, gout, isem.at[4])]
    loads += [pltpu.make_async_copy(x_hbm, x, isem.at[3])]
    loads += [pltpu.make_async_copy(dz_hbm.at[p], dz.at[p], isem.at[p]) for p in range(3)]
    for copy in loads:
        copy.start()

    db = db_a[...] + db_b[...]
    tail = 3 * width + FF
    line[:, 0:width] = db[0:1]
    line[:, width : 2 * width] = db[1:2]
    line[:, 2 * width : 3 * width] = sums[5:6]
    line[:, 3 * width : tail] = db1[...]
    for i, row in enumerate((2, 3, 4, 0, 1)):
        line[:, tail + i * width : tail + (i + 1) * width] = sums[row : row + 1]
    count = line.shape[1] // grid.devices
    blank = jnp.zeros((8, width), F32)
    first_row = lax.broadcasted_iota(jnp.int32, (8, count), 0) == 0
    for d in range(grid.devices):
        values = jnp.where(first_row, line[:, d * count : (d + 1) * count], 0.0)
        values = jnp.concatenate([values, blank[:, count:]], axis=1).astype(BF)
        if path:
            stage[d, per : per + 8] = values
        else:
            grads[1][d] = values

    copies = []

    def emit(part, value):
        value = value.astype(BF)
        if not path:
            grads[0][part * width : (part + 1) * width, :] = value
            return
        stage[part * blocks : (part + 1) * blocks, 0:per] = value.reshape(blocks, per, width)
        iz = part ^ me // blocks
        for label in range(blocks):
            other, side_x, side_y = label & 1, label // 2 % 2, label // 4
            block = part * blocks + (label ^ (me & (blocks - 1)))
            copies.append(
                start_store(
                    core, stage.at[block], grads, side_x, side_y, other, iz, osem.at[part * blocks + label]
                )
            )

    loads[0].wait()
    emit(3, gout[...])
    loads[1].wait()
    for part in range(3):
        loads[2 + part].wait()
        emit(part, tn(dz[part], x[...]))
    for copy in copies:
        copy.wait()


def attn_grad_call(grid, me, dz, x, gout, vectors, per, deps):
    rows, width = x.shape
    paths = path_shapes(grid, grid.devices, per, width)
    path = is_path(grid, per)
    if path:
        paths = [jax.ShapeDtypeStruct((p.shape[0], per + 8, width), BF) for p in paths]
    return pl.pallas_call(
        lambda *r: attn_grad_kernel(grid, per, *r),
        in_specs=[SMEM] + [VMEM] * len(vectors) + [ANY] * (3 + len(deps)),
        out_specs=[ANY if path else VMEM] * len(paths),
        out_shape=paths,
        scratch_shapes=[
            pltpu.VMEM((grid.devices, per + 8, width), BF),
            pltpu.VMEM((3, rows, width), BF),
            pltpu.VMEM((rows, width), BF),
            pltpu.VMEM((width, width), BF),
            pltpu.VMEM((1, 8 * width + FF), F32),
            pltpu.SemaphoreType.DMA((5,)),
            pltpu.SemaphoreType.DMA((grid.devices,)),
        ],
        compiler_params=params(),
        cost_estimate=cost(6 * rows * width * width, 28 << 20),
        name="attn_grad",
    )(me, *vectors, dz, x, gout, *deps)


def input_grad_kernel(grid, npieces, me_ref, dz_hbm, dres_hbm, *rest):
    pieces = rest[:npieces]
    mine, others, _, dz, total, w, sems, isem, osem = rest[-9:]
    rows, width = total.shape
    blocks = grid.devices // 4

    def load(part):
        return pltpu.make_async_copy(dz_hbm.at[part], dz.at[part], isem.at[part])

    def in_order(body):
        for i in range(4):
            part = quarter_order(grid, me_ref, pieces, i)
            pl.when(part < 3)(lambda part=part: body(part))

    load_total = pltpu.make_async_copy(dres_hbm, total, isem.at[3])
    load_total.start()
    in_order(lambda part: load(part).start())
    start_natural(grid, me_ref, pieces, w, sems, 0, 3 * blocks)
    load_total.wait()

    @pl.loop(0, 4)
    def _(i):
        part = quarter_order(grid, me_ref, pieces, i)

        @pl.when(part < 3)
        def _():
            load(part).wait()
            wait_natural(grid, pieces, w, sems, part * blocks, blocks, 0, 3 * blocks)
            at = pl.ds(pl.multiple_of(part * width, width), width)
            total[...] += nn(dz[part], w[at, :])

    for copy in store_sequences(me_ref, total, mine, others, osem):
        copy.wait()


def input_grad_call(grid, me, dz, dres, pieces, shape, carry, deps):
    rows, width = dres.shape
    return pl.pallas_call(
        lambda *r: input_grad_kernel(grid, len(pieces), *r),
        in_specs=[SMEM, ANY, ANY] + [ANY] * (len(pieces) + 1 + len(deps)),
        out_specs=[ANY, ANY, ANY],
        out_shape=[
            jax.ShapeDtypeStruct(shape, F32),
            jax.ShapeDtypeStruct((shape[0] // 2,) + shape[1:], F32),
            jax.ShapeDtypeStruct(carry.shape, carry.dtype),
        ],
        input_output_aliases={3 + len(pieces): 2},
        scratch_shapes=[
            pltpu.VMEM((3, rows, width), BF),
            pltpu.VMEM((rows, width), F32),
            pltpu.VMEM((3 * width, width), BF),
            pltpu.SemaphoreType.DMA((grid.devices,)),
            pltpu.SemaphoreType.DMA((4,)),
            pltpu.SemaphoreType.DMA((shape[0],)),
        ],
        compiler_params=params(),
        cost_estimate=cost(3 * rows * width * width, 16 << 20),
        name="input_grad",
    )(me, dz, dres, *pieces, carry, *deps)


def gate(value, deps):
    return pl.pallas_call(
        lambda *r: None,
        in_specs=[ANY] * (1 + len(deps)),
        out_specs=ANY,
        out_shape=jax.ShapeDtypeStruct(value.shape, value.dtype),
        input_output_aliases={0: 0},
        compiler_params=params(),
        cost_estimate=cost(0, 0),
        name="gate",
    )(value, *deps)


def ordered_stack_kernel(count, *rest):
    for i in range(count):
        rest[-1][i] = rest[i][...]


def ordered_stack(parts, deps):
    return pl.pallas_call(
        lambda *r: ordered_stack_kernel(len(parts), *r),
        in_specs=[VMEM] * len(parts) + [ANY] * len(deps),
        out_specs=VMEM,
        out_shape=jax.ShapeDtypeStruct((len(parts),) + parts[0].shape, parts[0].dtype),
        compiler_params=params(),
        name="ordered_stack",
    )(*parts, *deps)


def adam_update(master, moment, second, grad, rate):
    moment_new = decay_rate * moment + (1.0 - decay_rate) * grad
    second_new = decay_rate * second + (1.0 - decay_rate) * grad * grad
    correction = 1.0 - decay_rate**STEP
    direction = moment_new / correction / (jnp.sqrt(second_new / correction) + adam_epsilon)
    master_new = master - rate * (direction + weight_decay * master)
    return (moment_new, second_new, master_new)


def join_sequences(mine, others, places):
    for s in range(others.shape[0]):
        mine = lax.dynamic_update_slice(mine, others[s : s + 1], (places[s], 0, 0))
    return mine


def share_sequences(lengths, core):
    count = lengths.shape[0]
    number = jnp.arange(count)
    longer = (lengths[None, :] > lengths[:, None]) | (
        (lengths[None, :] == lengths[:, None]) & (number[None, :] < number[:, None])
    )
    rank = jnp.sum(longer.astype(jnp.int32), axis=1)
    by_rank = jnp.sum((rank[None, :] == number[:, None]) * number[None, :], axis=1)
    sides = [[r for r in range(count) if (r + 1) // 2 % 2 == c] for c in (0, 1)]
    first, second = (jnp.stack([by_rank[r] for r in side]) for side in sides)
    mine = jnp.where(core == 0, first, second).astype(jnp.int32)
    other = jnp.where(core == 0, second, first).astype(jnp.int32)
    return mine, other


def local(
    tokens,
    cotangent,
    seq_lengths,
    slot_order,
    attn_weights,
    attn_moment,
    attn_second,
    ffn_weights,
    ffn_moment,
    ffn_second,
    vectors,
    vector_moment,
    vector_second,
):
    grid = Grid(lax.axis_size("dp"))
    core = lax.axis_index("seq")
    shard_index = lax.axis_index(AXES)
    me = shard_index.astype(jnp.int32).reshape(1)
    seq_count, half_len, width = tokens.shape
    seqs = seq_count // 2
    length = 2 * half_len
    rows = seqs * length
    per, ffn_per = attn_weights.shape[1], ffn_weights.shape[1]
    vec_per = vectors.shape[0]
    path = is_path(grid, per) and is_path(grid, ffn_per)

    slot_pick = (slot_order[0][:, None] == jnp.arange(seq_count)[None, :]).astype(jnp.int32)
    slot_len = jnp.sum(slot_pick * seq_lengths[0][None, :], axis=1)
    taken, left = share_sequences(slot_len, core)
    lens = jnp.sum((taken[:, None] == jnp.arange(seq_count)[None, :]) * slot_len[None, :], axis=1)
    me = jnp.concatenate([me, taken])

    vec_rows = jnp.zeros((8, width), BF)
    vec_rows = lax.dynamic_update_slice(vec_rows, vectors.astype(BF)[None, :], (0, 0))
    attn_block = jnp.concatenate([attn_weights.astype(BF).T, vec_rows])

    other_core = lambda value: permute(value, grid, lambda c: 1)
    tokens_other = other_core(tokens)
    if path:
        attn_parts = gather_z(grid, attn_block)
        ffn_block = ffn_weights.astype(BF).T
        ffn_parts = gather_z(grid, ffn_block)
        attn_z = ordered_stack(attn_parts, [ffn_block])
        attn_two = gather_two(grid, attn_z)
        attn_two = attn_two[:1] + [gate(t, ffn_parts[1:2]) for t in attn_two[1:]]
        attn_three = gather_three(grid, attn_two)
        ffn_z = ordered_stack(ffn_parts, attn_two[1:])
        ffn_two = gather_two(grid, ffn_z)
        weights = with_core(grid, attn_two + attn_three, [ffn_z])
        vec = natural_vectors(grid, weights, core, me[0], per, vec_per)
    else:
        whole_rows = lambda block: [lax.all_gather(block, AXES, axis=0, tiled=True)]
        weights = whole_rows(attn_block[:per])
        ffn_pieces = whole_rows(ffn_weights.astype(BF).T)
        ffn_two = []
        vec = lax.all_gather(attn_block[per:], AXES)[:, 0, :vec_per].reshape(1, -1).astype(F32)
    dy_other = other_core(cotangent)

    qkv, x = qkv_call(grid, me, vec, tokens, tokens_other, weights)
    fwd = attend_call(grid, me, lens, qkv, x, vec, weights, seqs, 0, [], [])
    ffn_two = ffn_two[:1] + [gate(t, fwd[:1]) for t in ffn_two[1:]]
    fwd = attend_call(grid, me, lens, qkv, x, vec, weights, seqs, 1, fwd, ffn_two[1:])
    ctx, lse, normed, inv, hidden = fwd
    if path:
        ffn_three = gather_three(grid, ffn_two)
        ffn_three = ffn_three[:1] + [gate(t, fwd[:1]) for t in ffn_three[1:]]
        ffn_pieces = with_core(grid, ffn_two + ffn_three, [])
    out, out_other, dres_one, datt, sums, db1, *grads_f = ffn_call(
        grid, me, vec, inv, hidden, normed, cotangent, dy_other, ffn_pieces, ffn_per
    )
    layer_out = join_sequences(out, other_core(out_other), left)

    sums_f = Sums(grid, path, grads_f)
    sends = sums_f.add_core()
    dctx, gout = out_back_call(grid, me, datt, ctx, weights, sends)
    dz, db_a, sums_f.keep[1] = attend_back_call(
        lens, qkv, dctx, lse, seqs, 0, None, sums_f.keep[1], sends
    )
    sends = sums_f.add_three()
    dz, db_b, sums_f.keep[0] = attend_back_call(
        lens, qkv, dctx, lse, seqs, 1, dz, sums_f.keep[0], sends
    )
    sends = sums_f.add_two()
    grads_c = list(
        attn_grad_call(grid, me, dz, x, gout, [sums, db1, db_a, db_b], per, sends)
    )
    if path:
        grads_c[7] = gate(grads_c[7], sums_f.z[1:2])
    sums_c = Sums(grid, path, grads_c)
    sends = sums_c.add_core()
    dx, dx_other, sums_c.keep[1] = input_grad_call(
        grid, me, dz, dres_one, weights, tokens.shape, sums_c.keep[1], sends
    )
    ffn_sum = sums_f.add_z()
    sums_c.add_three()
    sums_c.keep[0] = gate(sums_c.keep[0], [ffn_sum])
    input_grad = join_sequences(dx, other_core(dx_other), left)
    sums_c.add_two()
    attn_sum = sums_c.add_z()

    vector_sum = attn_sum[per, :vec_per]
    attn_sum = attn_sum[:per].T
    ffn_sum = ffn_sum[:ffn_per].T

    attn_cols = shard_index * per + jnp.arange(per)
    attn_rate = jnp.where(
        attn_cols < 2 * width, math.sqrt(2.0), jnp.where(attn_cols < 3 * width, 1.5, 1.8)
    ) * width ** (-0.5)
    ffn_cols = shard_index * ffn_per + jnp.arange(ffn_per)
    ffn_rate = jnp.where(ffn_cols < FF, width ** (-0.5), 1.5 * FF ** (-0.5))
    attn_m, attn_v, attn_new = adam_update(
        attn_weights, attn_moment, attn_second, attn_sum, attn_rate[None, :]
    )
    ffn_m, ffn_v, ffn_new = adam_update(
        ffn_weights, ffn_moment, ffn_second, ffn_sum, ffn_rate[None, :]
    )
    vec_m, vec_v, vec_new = adam_update(
        vectors, vector_moment, vector_second, vector_sum, vector_rate
    )
    return (
        layer_out,
        input_grad,
        attn_m,
        attn_v,
        attn_new,
        attn_new.astype(BF),
        ffn_m,
        ffn_v,
        ffn_new,
        ffn_new.astype(BF),
        vec_m,
        vec_v,
        vec_new,
        vec_new.astype(BF),
    )


def solution(mesh):
    columns = P(None, AXES)
    flat = P(AXES)
    rows = P("dp", "seq", None)
    placed = (rows, rows, P("dp", None), P("dp", None)) + (columns,) * 6 + (flat,) * 3
    return jax.shard_map(
        local,
        mesh=mesh,
        in_specs=placed,
        out_specs=(rows, rows) + (columns,) * 8 + (flat,) * 4,
        check_vma=False,
    )
```
